32 devices in a mesh: gx: 4 (over x, core), gy: 2 (over y), gz: 4 (over z).
Axes of the slice: x: 2, y: 2, z: 4, core: 2. Of those that a mesh axis runs over, the one named last changes fastest.
Arguments:
- solution: float32 [3, 32, 32, 512], P(None, 'gx', 'gy', 'gz'), may hold values from -6 to 6
- residual: float32 [3, 32, 32, 512], P(None, 'gx', 'gy', 'gz'), may hold values from -18 to 18
- direction: float32 [3, 32, 32, 512], P(None, 'gx', 'gy', 'gz'), may hold values from -18 to 18
- density: float32 [32, 32, 512], P('gx', 'gy', 'gz'), may hold values from 0.2 to 1
- labels: int32 [32, 32, 512], P('gx', 'gy', 'gz'), may hold values from 0 to 2
Outputs:
- new_solution: float32 [3, 32, 32, 512], P(None, 'gx', 'gy', 'gz')
- new_residual: float32 [3, 32, 32, 512], P(None, 'gx', 'gy', 'gz')
- new_direction: float32 [3, 32, 32, 512], P(None, 'gx', 'gy', 'gz')
- sensitivity: float32 [32, 32, 512], P('gx', 'gy', 'gz')
The draws below stay inside these ranges and needn't reach their ends.
All inputs are finite; a program needn't handle non-finite values.
Results may differ from the reference program's by a relative error of at most 0.0003.
Values sent between devices are 32-bit elements; how exact they have to be, the bound alone decides.
No kernel may reach another device: no remote copies, remote signals or barrier semaphores. Data moves between devices by JAX's collectives and lax.ppermute only.
A program may use at most 64 MiB of HBM per device.

```python
import math
import jax
import jax.numpy as jnp
from jax import lax

RAD = 3
NX = 32
NY = 32
NZ = 512


def rising_scale():
    along_x = jnp.arange(NX, dtype=jnp.float32) / NX
    along_z = jnp.arange(NZ, dtype=jnp.float32) / NZ
    return ((1.0 + 2.0 * along_x)[:, None, None] * (1.0 + 0.5 * along_z)[None, None, :])[None]


def draw_residual(key, part):
    key = jax.random.fold_in(key, 11)
    values = jax.random.truncated_normal(key, -4.0, 4.0, (3, NX, NY, NZ), jnp.float32)
    return (values * rising_scale()).astype(jnp.float32)


def draw_direction(key, part):
    key = jax.random.fold_in(key, 12)
    values = jax.random.truncated_normal(key, -4.0, 4.0, (3, NX, NY, NZ), jnp.float32)
    return (values * rising_scale()).astype(jnp.float32)


def set_ends(values, own_key, low, top_value):
    longest = values.shape.index(max(values.shape))
    spots = []
    for shift in (0, 1):
        where = [jax.random.randint(jax.random.fold_in(own_key, axis), (), 0, length) for axis, length in enumerate(values.shape)]
        where[longest] = (where[longest] + shift) % values.shape[longest]
        spots.append(tuple(where))
    return values.at[spots[0]].set(low).at[spots[1]].set(top_value)


def block_scale(own_key, dims, pieces, smallest, top_value):
    level, own = 1.0, jax.random.fold_in(own_key, 6)
    for dim, parts in pieces:
        steps = jnp.exp(jax.random.uniform(jax.random.fold_in(own, dim), (parts,), jnp.float32, smallest / len(pieces), top_value / len(pieces)))
        level = level * jnp.repeat(steps, dims[dim] // parts).reshape([-1 if axis == dim else 1 for axis in range(len(dims))])
    return level


def normal_values(rng, shape, deviation, bound, cuts=(), kind=jnp.bfloat16):
    values = jax.random.normal(rng, shape, jnp.float32) * deviation
    if len(cuts) > 0:
        values = block_scale(rng, shape, cuts, -0.22, 0.18) * values
    return jnp.clip(values, min=-bound, max=bound).astype(kind)


def setup_inputs(seed: int = 0) -> dict:
    seeds = jax.random.split(jax.random.key(seed), 6)
    return {
        "solution": normal_values(seeds[0], (3, NX, NY, NZ), 1.0, 6.0, ((1, 4), (2, 2), (3, 4)), jnp.float32),
        "residual": draw_residual(jax.random.fold_in(seeds[5], 71), 0),
        "direction": draw_direction(jax.random.fold_in(seeds[5], 71), 0),
        "density": jnp.clip(jnp.exp(math.log(1.0) - 1.609438 * jax.random.uniform(seeds[3], (NX, NY, NZ), jnp.float32) ** block_scale(seeds[3], (NX, NY, NZ), ((0, 4), (1, 2), (2, 4)), -0.2, 0.2)), 0.2, 1.0),
        "labels": set_ends(jax.random.randint(seeds[4], (NX, NY, NZ), 0, 3), jax.random.fold_in(seeds[4], 1), 0, 2).astype(jnp.int32),
    }


stiff_floor = 0.001
penalty = 3.0
neighbour_offsets = [(off_x, off_y, off_z) for off_x in (-1, 0, 1) for off_y in (-1, 0, 1) for off_z in (-1, 0, 1) if (off_x, off_y, off_z) != (0, 0, 0)]

def filter_table(reach):
    table = []
    for off_x in range(-reach, reach + 1):
        for off_y in range(-reach, reach + 1):
            for off_z in range(-reach, reach + 1):
                distance = math.sqrt(off_x * off_x + off_y * off_y + off_z * off_z)
                weight = reach + 0.5 - distance
                if weight > 0:
                    table.append((off_x, off_y, off_z, weight))
    return table

def shifted(padded, shift_x, shift_y, shift_z, depth):
    size_x = padded.shape[-3] - 2 * depth
    size_y = padded.shape[-2] - 2 * depth
    size_z = padded.shape[-1] - 2 * depth
    return padded[..., depth + shift_x:depth + shift_x + size_x, depth + shift_y:depth + shift_y + size_y, depth + shift_z:depth + shift_z + size_z]

def pull(differ, off_x, off_y, off_z):
    norm_sq = float(off_x * off_x + off_y * off_y + off_z * off_z)
    along = (off_x * differ[0] + off_y * differ[1] + off_z * differ[2]) / (norm_sq * norm_sq)
    return jnp.stack([differ[0] / norm_sq + off_x * along, differ[1] / norm_sq + off_y * along, differ[2] / norm_sq + off_z * along])

def corner_entries(off_x, off_y, off_z):
    norm_sq = float(off_x * off_x + off_y * off_y + off_z * off_z)
    values = [1.0 / norm_sq + off_x * off_x / (norm_sq * norm_sq), 1.0 / norm_sq + off_y * off_y / (norm_sq * norm_sq), 1.0 / norm_sq + off_z * off_z / (norm_sq * norm_sq)]
    return jnp.array(values, dtype=jnp.float32).reshape(3, 1, 1, 1)

def couple(padded, stiff_pad):
    center = shifted(padded, 0, 0, 0, 1)
    stiff_mid = shifted(stiff_pad, 0, 0, 0, 1)
    total = jnp.zeros_like(center)
    diagonal = jnp.zeros_like(center)
    for off_x, off_y, off_z in neighbour_offsets:
        weight = 0.5 * (stiff_mid + shifted(stiff_pad, off_x, off_y, off_z, 1))
        differ = center - shifted(padded, off_x, off_y, off_z, 1)
        total = total + weight[None] * pull(differ, off_x, off_y, off_z)
        diagonal = diagonal + weight[None] * corner_entries(off_x, off_y, off_z).astype(center.dtype)
    return (total, diagonal)

def energy(padded):
    center = shifted(padded, 0, 0, 0, 1)
    total = jnp.zeros_like(center[0])
    for off_x, off_y, off_z in neighbour_offsets:
        differ = center - shifted(padded, off_x, off_y, off_z, 1)
        total = total + 0.5 * lax.optimization_barrier(jnp.sum(differ * pull(differ, off_x, off_y, off_z), axis=0))
    return total

def masks(labels):
    clamped = labels == 1
    roller = labels == 2
    first = jnp.where(clamped, 0.0, 1.0).astype(jnp.float32)
    last = jnp.where(clamped | roller, 0.0, 1.0).astype(jnp.float32)
    return jnp.stack([first, first, last])

def spread(table, padded, depth):
    total = jnp.zeros_like(shifted(padded, 0, 0, 0, depth))
    for off_x, off_y, off_z, weight in table:
        total = total + weight * shifted(padded, off_x, off_y, off_z, depth)
    return total

def reference(solution, residual, direction, density, labels):
    stiffness = stiff_floor + (1.0 - stiff_floor) * density * density * density
    free_mask = masks(labels).astype(solution.dtype)
    masked = free_mask * direction
    pad_four = ((0, 0), (1, 1), (1, 1), (1, 1))
    image_raw, diag_raw = couple(jnp.pad(masked, pad_four), jnp.pad(stiffness, 1))
    image = free_mask * image_raw
    precond = free_mask * diag_raw + (1.0 - free_mask)
    zeta = residual / precond
    norm_now = jnp.sum(residual * zeta)
    curvature = jnp.sum(masked * image)
    alpha = norm_now / curvature
    new_solution = solution + alpha * masked
    new_residual = residual - alpha * image
    new_zeta = new_residual / precond
    norm_next = jnp.sum(new_residual * new_zeta)
    new_direction = new_zeta + norm_next / norm_now * direction
    compliance = -penalty * (1.0 - stiff_floor) * density * density * energy(jnp.pad(new_solution, pad_four))
    table = filter_table(RAD)
    inside = jnp.pad(jnp.ones_like(density), RAD)
    hsum = spread(table, inside, RAD)
    scaled = compliance / hsum
    sensitivity = spread(table, jnp.pad(scaled, RAD), RAD)
    return (new_solution, new_residual, new_direction, sensitivity)
```

```python
import functools
import math

import jax
import jax.numpy as jnp
from jax import lax
from jax.experimental import pallas as pl
from jax.experimental.pallas import tpu as pltpu
from jax.sharding import PartitionSpec as P

RAD = 3
HALO = RAD + 1
stiff_floor = 0.001
penalty = 3.0
f32 = jnp.float32
neighbour_offsets = [
    (off_x, off_y, off_z)
    for off_x in (-1, 0, 1)
    for off_y in (-1, 0, 1)
    for off_z in (-1, 0, 1)
    if (off_x, off_y, off_z) != (0, 0, 0)
]
AXES = ("gx", "gy", "gz")


def cone(a, b, k):
    return max(0.0, RAD + 0.5 - math.sqrt(a * a + b * b + k * k))


def lanes_of(shape):
    return lax.broadcasted_iota(jnp.int32, shape, len(shape) - 1)


def rows_of(shape):
    return lax.broadcasted_iota(jnp.int32, shape, len(shape) - 2)


def roll(value, amount, axis):
    size = value.shape[axis]
    amount = amount % size
    return value if amount == 0 else pltpu.roll(value, amount, axis)


def call(body, outs, *args, scratch=(), cost=20000):
    return pl.pallas_call(
        body,
        out_shape=[jax.ShapeDtypeStruct(shape, f32) for shape in outs],
        in_specs=[pl.BlockSpec(memory_space=pltpu.VMEM)] * len(args),
        out_specs=[pl.BlockSpec(memory_space=pltpu.VMEM)] * len(outs),
        scratch_shapes=list(scratch),
        compiler_params=pltpu.CompilerParams(vmem_limit_bytes=24 * 1024 * 1024),
        cost_estimate=pl.CostEstimate(flops=cost * 1000, bytes_accessed=cost, transcendentals=0),
    )(*args)


def pack_faces(two, sol, dire, den, lab, lo, hi, *sides):
    sub = rows_of((8, 128))
    first = (lax.axis_index("gy") == 0) if two else None
    for t in range(4):
        planes = []
        for x in (2 * t, 2 * t + 1):
            label = lab[x]
            keep = jnp.where(label == 1, 0.0, 1.0).astype(f32)
            keep_last = jnp.where(label >= 1, 0.0, 1.0).astype(f32)
            fields = [dire[0, x] * keep, dire[1, x] * keep, dire[2, x] * keep_last]
            fields += [sol[0, x], sol[1, x], sol[2, x], den[x]]
            target, at = (lo, x) if x < 4 else (hi, x - 4)
            for f in range(7):
                target[f, at] = fields[f]
            planes.append(fields)
        for f in range(7):
            p, q = planes[0][f], planes[1][f]
            low = jnp.where(sub < 4, p[0:8], roll(q[0:8], 4, 0))
            high = jnp.where(sub < 4, roll(p[8:16], 4, 0), q[8:16])
            tiles = [jnp.where(first, high, low)] if two else [low, high]
            for s, tile in enumerate(tiles):
                sides[3 * s][f, t] = tile
                sides[3 * s + 1 + t // 2][f, t % 2] = tile


def extend(two, lo, hi, xl, xh, y0, c0l, c0h, y1, c1l, c1h, ext, ends):
    sub = rows_of((8, 128))
    lane = lanes_of((24, 128))
    if two:
        gy = lax.axis_index("gy")
        has_low = (gy == 1).astype(f32)
        has_high = (gy == 0).astype(f32)
    for f in range(7):
        packed = None
        for X in range(16):
            src = (xl, lo, hi, xh)[X // 4]
            own = src[f, X % 4]
            a, b = roll(own[0:8], 4, 0), roll(own[8:16], 4, 0)
            if X < 4:
                low, high = c0l[f, X // 2], c1l[f, X // 2]
            elif X < 12:
                low, high = y0[f, (X - 4) // 2], y1[f, (X - 4) // 2]
            else:
                low, high = c0h[f, (X - 12) // 2], c1h[f, (X - 12) // 2]
            if two:
                low, high = low * has_low, high * has_high
            if X % 2 == 0:
                high = roll(high, 4, 0)
            else:
                low = roll(low, 4, 0)
            plane = jnp.concatenate(
                [jnp.where(sub < 4, low, a), jnp.where(sub < 4, a, b), jnp.where(sub < 4, b, high)],
                axis=0,
            )
            ext[f, X] = plane
            turned = roll(plane, 8 * X + 4, 1)
            packed = turned if X == 0 else jnp.where(lane >= 8 * X, turned, packed)
        ends[f] = packed


def inverse_sums(counts, main, side):
    shape = (24, 128)
    row, lane = rows_of(shape), lanes_of(shape)
    nx, ny, nz = counts
    base_x = lax.axis_index("gx") * 8 - HALO
    base_y = lax.axis_index("gy") * 16 - HALO
    base_z = lax.axis_index("gz") * 128

    def folded(place, limit):
        def inside(p):
            return jnp.where((p >= 0) & (p < limit), 1.0, 0.0).astype(f32)

        return [inside(place)] + [inside(place - k) + inside(place + k) for k in range(1, RAD + 1)]

    along_y = folded(row + base_y, ny * 16)

    def partial(along_z):
        table = []
        for a in range(RAD + 1):
            total = jnp.zeros(shape, f32)
            for b in range(RAD + 1):
                line = None
                for k in range(RAD + 1):
                    w = cone(a, b, k)
                    if w > 0:
                        line = w * along_z[k] if line is None else line + w * along_z[k]
                if line is not None:
                    total = total + along_y[b] * line
            table.append(total)
        return table

    def finish(total, along_x, along_z):
        inner = along_x[0] * along_y[0] * along_z[0] > 0
        return jnp.where(inner, 1.0 / jnp.where(inner, total, 1.0), 0.0)

    along_z = folded(lane + base_z, nz * 128)
    table = partial(along_z)
    for X in range(16):
        along_x = folded(jnp.full(shape, X, jnp.int32) + base_x, nx * 8)
        total = sum(along_x[a] * table[a] for a in range(RAD + 1))
        main[X] = finish(total, along_x, along_z)
    place = lane % 8
    along_x = folded(lane // 8 + base_x, nx * 8)
    for s, shift in enumerate((-4, 124)):
        along_z = folded(place + (base_z + shift), nz * 128)
        table = partial(along_z)
        total = sum(along_x[a] * table[a] for a in range(RAD + 1))
        side[s] = finish(total, along_x, along_z)


def apply_operator(ext, ends, from_low, from_high, res, lab, image, inverse, sums, shifts):
    lane = lanes_of((24, 128))
    lane2 = lanes_of((16, 128))
    fields = (0, 1, 2, 6)
    del lane2
    for g, f in enumerate(fields):
        halo = jnp.where(lane % 8 < 4, from_low[f], from_high[f])
        for n in range(10):
            X = n + 3
            value = ext[f, X]
            near = roll(halo, 124 - 8 * X, 1)
            if g == 3:
                value = stiff_floor + (1.0 - stiff_floor) * value * value * value
                value = jnp.where(ext[f, X] > 0, value, 0.0)
                near_stiff = stiff_floor + (1.0 - stiff_floor) * near * near * near
                near = jnp.where(near > 0, near_stiff, 0.0)
            up = roll(jnp.where(lane == 0, near, value), -1, 1)
            down = roll(jnp.where(lane == 127, near, value), 1, 1)
            for z, plane in enumerate((down, value, up)):
                for y in range(3):
                    shifts[g, y, z, n] = roll(plane, -(HALO - 1 + y), 0)[0:16]
    parts = [jnp.zeros((16, 128), f32) for _ in range(4)]
    for x in range(8):
        n = x + 1
        mid = [shifts[g, 1, 1, n] for g in range(4)]
        classes = {1: [None] * 3, 2: [None] * 3, 3: [None] * 3}
        faces = [None] * 3
        edges = [None] * 3
        corners = None

        def add(old, new):
            return new if old is None else old + new

        for o in neighbour_offsets:
            near = [shifts[g, 1 + o[1], 1 + o[2], n + o[0]] for g in range(4)]
            norm = sum(abs(c) for c in o)
            weight = mid[3] + near[3]
            d = [mid[c] - near[c] for c in range(3)]
            acc = classes[norm]
            if norm == 1:
                c0 = [c for c in range(3) if o[c] != 0][0]
                faces[c0] = add(faces[c0], near[3])
                for c in range(3):
                    acc[c] = add(acc[c], weight * (d[c] + d[c] if c == c0 else d[c]))
            else:
                along = None
                for c in range(3):
                    if o[c] != 0:
                        term = d[c]
                        if along is None:
                            along, sign = term, o[c]
                        else:
                            along = along + term if o[c] == sign else along - term
                along = along * (1.0 / norm)
                for c in range(3):
                    if o[c] == 0:
                        pulled = d[c]
                    elif o[c] == sign:
                        pulled = d[c] + along
                    else:
                        pulled = d[c] - along
                    acc[c] = add(acc[c], weight * pulled)
                if norm == 2:
                    c0 = [c for c in range(3) if o[c] == 0][0]
                    edges[c0] = add(edges[c0], near[3])
                else:
                    corners = add(corners, near[3])
        s0 = mid[3]
        all_faces = faces[0] + faces[1] + faces[2]
        all_edges = edges[0] + edges[1] + edges[2]
        common = (all_faces + 6.0 * s0) + 0.75 * (all_edges + 12.0 * s0) + (4.0 / 9.0) * (corners + 8.0 * s0)
        label = lab[x]
        for c in range(3):
            diag = 0.5 * (common + (faces[c] + 2.0 * s0) - 0.25 * (edges[c] + 4.0 * s0))
            fixed = (label == 1) if c < 2 else (label >= 1)
            total = 0.5 * classes[1][c] + 0.25 * classes[2][c] + (1.0 / 6.0) * classes[3][c]
            total = jnp.where(fixed, 0.0, total)
            inv = 1.0 / jnp.where(fixed, 1.0, diag)
            r = res[c, x]
            zeta = r * inv
            scaled = total * inv
            image[c, x] = total
            inverse[c, x] = inv
            parts[0] = parts[0] + r * zeta
            parts[1] = parts[1] + mid[c] * total
            parts[2] = parts[2] + r * scaled
            parts[3] = parts[3] + total * scaled
    sub = rows_of((8, 128))
    out = jnp.zeros((8, 128), f32)
    for k in range(4):
        part = parts[k][0:8] + parts[k][8:16]
        out = jnp.where(sub == k, jnp.sum(part, axis=0, keepdims=True), out)
    sums[...] = out


def quadratic(d, o):
    norm = sum(abs(c) for c in o)
    square = d[0] * d[0] + d[1] * d[1] + d[2] * d[2]
    along, sign = None, 1
    for c in range(3):
        if o[c] != 0:
            if along is None:
                along, sign = d[c], o[c]
            else:
                along = along + d[c] if o[c] == sign else along - d[c]
    return (0.5 / norm) * square + (0.5 / (norm * norm)) * (along * along)


flat_half = [(1, -1, 0), (1, 0, 0), (1, 1, 0), (0, 1, 0)]
up_half = [(a, b, 1) for a in (-1, 0, 1) for b in (-1, 0, 1)]


def finish_step(
    ext, ends, from_low, from_high, total, image, inverse, res, dire, hinv, hside,
    new_sol, new_res, new_dir, sens, us, scaled,
):
    lane = lanes_of((24, 128))
    lows = lane % 8 < 4
    tot = jnp.sum(total[...], axis=1, keepdims=True)
    rz, pq, s2, s3 = tot[0:1], tot[1:2], tot[2:3], tot[3:4]
    alpha = rz / pq
    beta = (rz + alpha * (alpha * s3 - 2.0 * s2)) / rz

    for x in range(8):
        for c in range(3):
            r = res[c, x] - alpha * image[c, x]
            new_res[c, x] = r
            new_dir[c, x] = r * inverse[c, x] + beta * dire[c, x]

    halos = []
    lefts, rights = [], []
    for c in range(3):
        low_u = from_low[3 + c] + alpha * from_low[c]
        high_u = from_high[3 + c] + alpha * from_high[c]
        own_u = ends[3 + c] + alpha * ends[c]
        halos.append(jnp.where(lows, low_u, high_u))
        lefts.append(jnp.where(lows, low_u, own_u))
        rights.append(jnp.where(lows, own_u, high_u))
    for X in range(16):
        for c in range(3):
            u = ext[3 + c, X] + alpha * ext[c, X]
            if 4 <= X < 12:
                new_sol[c, X - 4] = roll(u, -HALO, 0)[0:16]
            near = roll(halos[c], 124 - 8 * X, 1)
            up = roll(jnp.where(lane == 0, near, u), -1, 1)
            for z, plane in enumerate((u, up)):
                us[3 * z, c, X] = roll(plane, 1, 0)
                us[3 * z + 1, c, X] = plane
                us[3 * z + 2, c, X] = roll(plane, -1, 0)

    sides, side_low = [], None
    den_left = jnp.where(lows, from_low[6], ends[6])
    den_right = jnp.where(lows, ends[6], from_high[6])
    for s, (u, den) in enumerate(((lefts, den_left), (rights, den_right))):
        turned = {oy: [roll(v, -oy, 0) for v in u] for oy in (-1, 0, 1)}
        forward = jnp.zeros((24, 128), f32)
        back = {(oy, oz): jnp.zeros((24, 128), f32) for oy in (-1, 0, 1) for oz in (0, 1)}
        for o in flat_half + up_half:
            move = 8 * o[0] + o[2]
            g = quadratic([u[c] - roll(turned[o[1]][c], -move, 1) for c in range(3)], o)
            forward = forward + g
            back[o[1], o[2]] = back[o[1], o[2]] + roll(g, 8 * o[0], 1)
        flat = back[0, 0] + roll(back[1, 0], 1, 0) + roll(back[-1, 0], -1, 0)
        up = back[0, 1] + roll(back[1, 1], 1, 0) + roll(back[-1, 1], -1, 0)
        if s == 0:
            side_low = up
        energy = forward + flat + roll(up, 1, 1)
        sides.append((-penalty * (1.0 - stiff_floor)) * (den * den) * energy * hside[s])
    ends_scaled = jnp.where(lows, sides[0], sides[1])

    zero = jnp.zeros((24, 128), f32)
    forward = [zero] * 16
    back = [{(oy, oz): None for oy in (-1, 0, 1) for oz in (0, 1)} for _ in range(16)]
    for X in range(0, 16):
        mine = [us[1, c, X] for c in range(3)]
        for o in flat_half + up_half:
            to = X + o[0]
            if not 0 <= to < 16:
                continue
            k = 3 * o[2] + o[1] + 1
            g = quadratic([mine[c] - us[k, c, to] for c in range(3)], o)
            forward[X] = forward[X] + g
            old = back[to][o[1], o[2]]
            back[to][o[1], o[2]] = g if old is None else old + g
        done = X - 1
        if done >= 1:
            bk = back[done]
            flat = bk[0, 0] + roll(bk[1, 0], 1, 0) + roll(bk[-1, 0], -1, 0)
            up = bk[0, 1] + roll(bk[1, 1], 1, 0) + roll(bk[-1, 1], -1, 0)
            below = roll(side_low, 127 - (8 * done + 3), 1)
            up = roll(jnp.where(lane == 127, below, up), 1, 1)
            den = ext[6, done]
            energy = forward[done] + flat + up
            scaled[done] = (-penalty * (1.0 - stiff_floor)) * (den * den) * energy * hinv[done]

    rows = [[None] * (RAD + 1) for _ in range(8)]
    for X in range(1, 15):
        s = scaled[X]
        near = roll(ends_scaled, 124 - 8 * X, 1)
        fold = [s]
        for k in range(1, RAD + 1):
            above = roll(jnp.where(lane < k, near, s), -k, 1)
            under = roll(jnp.where(lane >= 128 - k, near, s), k, 1)
            fold.append(above + under)
        made = {}
        for b in range(RAD + 1):
            for a in range(-RAD, RAD + 1):
                x = X - a - HALO
                if not 0 <= x < 8 or cone(a, b, 0) <= 0:
                    continue
                key = a * a + b * b
                if key not in made:
                    line = None
                    for k in range(RAD + 1):
                        w = cone(a, b, k)
                        if w > 0:
                            line = w * fold[k] if line is None else line + w * fold[k]
                    made[key] = line
                old = rows[x][b]
                rows[x][b] = made[key] if old is None else old + made[key]
        x = X - 2 * RAD - 1
        if x >= 0:
            value = rows[x][0]
            for b in range(1, RAD + 1):
                value = value + roll(rows[x][b], b, 0) + roll(rows[x][b], -b, 0)
            sens[x] = roll(value, -HALO, 0)[0:16]


def line_pairs(count, step):
    return [(i, i + step) for i in range(count) if 0 <= i + step < count]


def plane_pairs(nx, ny, step_x, step_y):
    pairs = []
    for ix in range(nx):
        for iy in range(ny):
            to_x, to_y = ix + step_x, (1 - iy if step_y is None else iy + step_y)
            if 0 <= to_x < nx and 0 <= to_y < ny:
                pairs.append((ix * ny + iy, to_x * ny + to_y))
    return pairs


def prime_factors(count):
    factors, p = [], 2
    while count > 1:
        while count % p == 0:
            factors.append(p)
            count //= p
        p += 1
    return factors


def total_over(value, mesh_shape):
    for axis in AXES:
        count = mesh_shape[axis]
        stride = 1
        for factor in prime_factors(count):
            block = stride * factor
            got = []
            for step in range(1, factor):
                pairs = []
                for i in range(count):
                    digit = (i // stride) % factor
                    to = i + (((digit + step) % factor) - digit) * stride
                    pairs.append((i, to))
                got.append(lax.ppermute(value, axis, pairs))
            for other in got:
                value = value + other
            stride = block
    return value


def per_device(mesh_shape, solution, residual, direction, density, labels):
    nx, ny, nz = (mesh_shape[a] for a in AXES)
    two = ny == 2
    half, full, corner = (7, 4, 16, 128), (7, 4, 8, 128), (7, 2, 8, 128)
    n_sides = 1 if two else 2
    packed = call(
        functools.partial(pack_faces, two),
        [half, half] + [full, corner, corner] * n_sides,
        solution, direction, density, labels,
    )
    lo, hi = packed[:2]
    plane = ("gx", "gy")
    xl = lax.ppermute(hi, "gx", line_pairs(nx, 1))
    xh = lax.ppermute(lo, "gx", line_pairs(nx, -1))
    received = []
    for s in range(n_sides):
        rows, first, second = packed[2 + 3 * s : 5 + 3 * s]
        step = None if two else (-1, 1)[s]
        received.append(
            [
                lax.ppermute(rows, plane, plane_pairs(nx, ny, 0, step)),
                lax.ppermute(second, plane, plane_pairs(nx, ny, 1, step)),
                lax.ppermute(first, plane, plane_pairs(nx, ny, -1, step)),
            ]
        )
    low_side, high_side = (received[0], received[0]) if two else (received[1], received[0])
    hinv, hside = call(functools.partial(inverse_sums, (nx, ny, nz)), [(16, 24, 128), (2, 24, 128)])
    ext, ends = call(
        functools.partial(extend, two),
        [(7, 16, 24, 128), (7, 24, 128)],
        lo, hi, xl, xh, *low_side, *high_side,
    )
    from_low = lax.ppermute(ends, "gz", line_pairs(nz, 1))
    from_high = lax.ppermute(ends, "gz", line_pairs(nz, -1))
    field = (3, 8, 16, 128)
    image, inverse, sums = call(
        apply_operator,
        [field, field, (8, 128)],
        ext, ends, from_low, from_high, residual, labels,
        scratch=[pltpu.VMEM((4, 3, 3, 10, 16, 128), f32)],
    )
    total = total_over(sums, mesh_shape)
    return tuple(
        call(
            finish_step,
            [field, field, field, (8, 16, 128)],
            ext, ends, from_low, from_high, total, image, inverse, residual, direction, hinv, hside,
            scratch=[pltpu.VMEM((6, 3, 16, 24, 128), f32), pltpu.VMEM((16, 24, 128), f32)],
        )
    )


def solution(mesh):
    wide, flat = P(None, "gx", "gy", "gz"), P("gx", "gy", "gz")
    return jax.shard_map(
        functools.partial(per_device, dict(mesh.shape)),
        mesh=mesh,
        in_specs=(wide, wide, wide, flat, flat),
        out_specs=(wide, wide, wide, flat),
        check_vma=False,
    )
```

```python
import functools
import math

import jax
import jax.numpy as jnp
from jax import lax
from jax.experimental import pallas as pl
from jax.experimental.pallas import tpu as pltpu
from jax.sharding import PartitionSpec as P

RAD = 3
HALO = RAD + 1
stiff_floor = 0.001
penalty = 3.0
f32 = jnp.float32
neighbour_offsets = [
    (off_x, off_y, off_z)
    for off_x in (-1, 0, 1)
    for off_y in (-1, 0, 1)
    for off_z in (-1, 0, 1)
    if (off_x, off_y, off_z) != (0, 0, 0)
]
AXES = ("gx", "gy", "gz")


def cone(a, b, k):
    return max(0.0, RAD + 0.5 - math.sqrt(a * a + b * b + k * k))


def lanes_of(shape):
    return lax.broadcasted_iota(jnp.int32, shape, len(shape) - 1)


def rows_of(shape):
    return lax.broadcasted_iota(jnp.int32, shape, len(shape) - 2)


def roll(value, amount, axis):
    size = value.shape[axis]
    amount = amount % size
    return value if amount == 0 else pltpu.roll(value, amount, axis)


def call(body, outs, *args, scratch=(), cost=20000, far=()):
    args = [
        pltpu.with_memory_space_constraint(a, pltpu.HBM) if i in far else a for i, a in enumerate(args)
    ]
    return pl.pallas_call(
        body,
        out_shape=[jax.ShapeDtypeStruct(shape, f32) for shape in outs],
        in_specs=[
            pl.BlockSpec(memory_space=pl.ANY if i in far else pltpu.VMEM) for i in range(len(args))
        ],
        out_specs=[pl.BlockSpec(memory_space=pltpu.VMEM)] * len(outs),
        scratch_shapes=list(scratch),
        compiler_params=pltpu.CompilerParams(vmem_limit_bytes=24 * 1024 * 1024),
        cost_estimate=pl.CostEstimate(flops=cost * 1000, bytes_accessed=cost, transcendentals=0),
    )(*args)


def is_even(axis):
    return lax.axis_index(axis) % 2 == 0


def pack_faces(rounds_y, sol_any, dire_any, den_any, lab_any, *refs):
    halves, packs = refs[:2], refs[2 : 2 + 3 * rounds_y]
    sol, dire, den, lab, sems = refs[2 + 3 * rounds_y :]
    copies = [
        pltpu.make_async_copy(source, target, sems.at[i])
        for i, (source, target) in enumerate(
            ((dire_any, dire), (sol_any, sol), (den_any, den), (lab_any, lab))
        )
    ]
    for copy in copies:
        copy.start()
    sub = rows_of((8, 128))
    even_x, even_y = is_even("gx"), is_even("gy")
    for copy in copies:
        copy.wait()

    def masked(x):
        label = lab[x]
        keep = jnp.where(label == 1, 0.0, 1.0).astype(f32)
        keep_last = jnp.where(label >= 1, 0.0, 1.0).astype(f32)
        fields = [dire[0, x] * keep, dire[1, x] * keep, dire[2, x] * keep_last]
        return fields + [sol[0, x], sol[1, x], sol[2, x], den[x]]

    for t in range(2):
        planes = {x: masked(x) for x in (2 * t, 2 * t + 1, 2 * t + 4, 2 * t + 5)}
        for f in range(7):
            for i in (2 * t, 2 * t + 1):
                low, high = planes[i][f], planes[i + 4][f]
                halves[0][f, i] = jnp.where(even_x, high, low)
                halves[1][f, i] = jnp.where(even_x, low, high)
            tiles = []
            for i in (2 * t, 2 * t + 4):
                p, q = planes[i][f], planes[i + 1][f]
                low = jnp.where(sub < 4, p[0:8], roll(q[0:8], 4, 0))
                high = jnp.where(sub < 4, roll(p[8:16], 4, 0), q[8:16])
                tiles.append((jnp.where(even_y, high, low), jnp.where(even_y, low, high)))
            for s in range(rounds_y):
                rows, corner0, corner1 = packs[3 * s : 3 * s + 3]
                low, high = tiles[0][s], tiles[1][s]
                rows[f, t] = low
                rows[f, t + 2] = high
                corner0[f, t] = jnp.where(even_x, high, low)
                corner1[f, t] = jnp.where(even_x, low, high)


def extend(counts, half0, half1, got0, got1, *refs):
    nx, ny, nz = counts
    sides, (ext, ends) = refs[:-2], refs[-2:]
    sub = rows_of((8, 128))
    lane = lanes_of((24, 128))
    ix, iy = lax.axis_index("gx"), lax.axis_index("gy")
    even_y = is_even("gy")
    x_ok = ((ix > 0).astype(f32), (ix < nx - 1).astype(f32))
    y_ok = ((iy > 0).astype(f32), (iy < ny - 1).astype(f32))

    def body(blocks, order):
        def strip(which, f, t):
            tiles = []
            for s in range(len(sides) // 3):
                rows, corner0, corner1 = sides[3 * s : 3 * s + 3]
                ref = rows if which is None else (corner0, corner1)[order[which]]
                tiles.append(ref[f, t])
            keep = 1.0 if which is None else x_ok[which]
            other = tiles[-1]
            low = jnp.where(even_y, other, tiles[0]) * (y_ok[0] * keep)
            high = jnp.where(even_y, tiles[0], other) * (y_ok[1] * keep)
            return low, high

        for f in range(7):
            packed = None
            for X in range(16):
                own = blocks[X // 4][f, X % 4]
                which = None
                if X < 4:
                    which, t = 0, X // 2
                elif X >= 12:
                    which, t = 1, (X - 12) // 2
                else:
                    t = (X - 4) // 2
                if which is not None:
                    own = own * x_ok[which]
                low, high = strip(which, f, t)
                a, b = roll(own[0:8], 4, 0), roll(own[8:16], 4, 0)
                if X % 2 == 0:
                    high = roll(high, 4, 0)
                else:
                    low = roll(low, 4, 0)
                plane = jnp.concatenate(
                    [jnp.where(sub < 4, low, a), jnp.where(sub < 4, a, b), jnp.where(sub < 4, b, high)],
                    axis=0,
                )
                ext[f, X] = plane
                turned = roll(plane, 8 * X + 4, 1)
                packed = turned if X == 0 else jnp.where(lane >= 8 * X, turned, packed)
            ends[f] = packed

    @pl.when(ix % 2 == 0)
    def _():
        body((got1, half1, half0, got0), (1, 0))

    @pl.when(ix % 2 == 1)
    def _():
        body((got0, half0, half1, got1), (0, 1))


def inverse_sums(counts, main, side):
    shape = (24, 128)
    row, lane = rows_of(shape), lanes_of(shape)
    nx, ny, nz = counts
    base_x = lax.axis_index("gx") * 8 - HALO
    base_y = lax.axis_index("gy") * 16 - HALO
    base_z = lax.axis_index("gz") * 128

    def folded(place, limit):
        def inside(p):
            return jnp.where((p >= 0) & (p < limit), 1.0, 0.0).astype(f32)

        return [inside(place)] + [inside(place - k) + inside(place + k) for k in range(1, RAD + 1)]

    along_y = folded(row + base_y, ny * 16)

    def partial(along_z):
        table = []
        for a in range(RAD + 1):
            total = jnp.zeros(shape, f32)
            for b in range(RAD + 1):
                line = None
                for k in range(RAD + 1):
                    w = cone(a, b, k)
                    if w > 0:
                        line = w * along_z[k] if line is None else line + w * along_z[k]
                if line is not None:
                    total = total + along_y[b] * line
            table.append(total)
        return table

    def finish(total, along_x, along_z):
        inner = along_x[0] * along_y[0] * along_z[0] > 0
        return jnp.where(inner, 1.0 / jnp.where(inner, total, 1.0), 0.0)

    along_z = folded(lane + base_z, nz * 128)
    table = partial(along_z)
    for X in range(16):
        along_x = folded(jnp.full(shape, X, jnp.int32) + base_x, nx * 8)
        total = sum(along_x[a] * table[a] for a in range(RAD + 1))
        main[X] = finish(total, along_x, along_z)
    place = lane % 8
    along_x = folded(lane // 8 + base_x, nx * 8)
    for s, shift in enumerate((-4, 124)):
        along_z = folded(place + (base_z + shift), nz * 128)
        table = partial(along_z)
        total = sum(along_x[a] * table[a] for a in range(RAD + 1))
        side[s] = finish(total, along_x, along_z)


def apply_operator(nz, ext, got0, got1, res, lab, image, inverse, sums, around, shifts):
    lane = lanes_of((24, 128))
    fields = (0, 1, 2, 6)
    iz = lax.axis_index("gz")
    lows = lane % 8 < 4
    from_zero = (lane // 4) % 2 == (iz + 1) % 2
    keep = jnp.where(lows, (iz > 0).astype(f32), (iz < nz - 1).astype(f32))
    for f in range(7):
        around[f] = jnp.where(from_zero, got0[f], got1[f]) * keep
    for g, f in enumerate(fields):
        halo = around[f]
        for n in range(10):
            X = n + 3
            value = ext[f, X]
            near = roll(halo, 124 - 8 * X, 1)
            if g == 3:
                value = stiff_floor + (1.0 - stiff_floor) * value * value * value
                value = jnp.where(ext[f, X] > 0, value, 0.0)
                near_stiff = stiff_floor + (1.0 - stiff_floor) * near * near * near
                near = jnp.where(near > 0, near_stiff, 0.0)
            up = roll(jnp.where(lane == 0, near, value), -1, 1)
            down = roll(jnp.where(lane == 127, near, value), 1, 1)
            for z, plane in enumerate((down, value, up)):
                for y in range(3):
                    shifts[g, y, z, n] = roll(plane, -(HALO - 1 + y), 0)[0:16]
    parts = [jnp.zeros((16, 128), f32) for _ in range(4)]
    for x in range(8):
        n = x + 1
        mid = [shifts[g, 1, 1, n] for g in range(4)]
        classes = {1: [None] * 3, 2: [None] * 3, 3: [None] * 3}
        faces = [None] * 3
        edges = [None] * 3
        corners = None

        def add(old, new):
            return new if old is None else old + new

        for o in neighbour_offsets:
            near = [shifts[g, 1 + o[1], 1 + o[2], n + o[0]] for g in range(4)]
            norm = sum(abs(c) for c in o)
            weight = mid[3] + near[3]
            d = [mid[c] - near[c] for c in range(3)]
            acc = classes[norm]
            if norm == 1:
                c0 = [c for c in range(3) if o[c] != 0][0]
                faces[c0] = add(faces[c0], near[3])
                for c in range(3):
                    acc[c] = add(acc[c], weight * (d[c] + d[c] if c == c0 else d[c]))
            else:
                along = None
                for c in range(3):
                    if o[c] != 0:
                        term = d[c]
                        if along is None:
                            along, sign = term, o[c]
                        else:
                            along = along + term if o[c] == sign else along - term
                along = along * (1.0 / norm)
                for c in range(3):
                    if o[c] == 0:
                        pulled = d[c]
                    elif o[c] == sign:
                        pulled = d[c] + along
                    else:
                        pulled = d[c] - along
                    acc[c] = add(acc[c], weight * pulled)
                if norm == 2:
                    c0 = [c for c in range(3) if o[c] == 0][0]
                    edges[c0] = add(edges[c0], near[3])
                else:
                    corners = add(corners, near[3])
        s0 = mid[3]
        all_faces = faces[0] + faces[1] + faces[2]
        all_edges = edges[0] + edges[1] + edges[2]
        common = (all_faces + 6.0 * s0) + 0.75 * (all_edges + 12.0 * s0) + (4.0 / 9.0) * (corners + 8.0 * s0)
        label = lab[x]
        for c in range(3):
            diag = 0.5 * (common + (faces[c] + 2.0 * s0) - 0.25 * (edges[c] + 4.0 * s0))
            fixed = (label == 1) if c < 2 else (label >= 1)
            total = 0.5 * classes[1][c] + 0.25 * classes[2][c] + (1.0 / 6.0) * classes[3][c]
            total = jnp.where(fixed, 0.0, total)
            inv = 1.0 / jnp.where(fixed, 1.0, diag)
            r = res[c, x]
            zeta = r * inv
            scaled = total * inv
            image[c, x] = total
            inverse[c, x] = inv
            parts[0] = parts[0] + r * zeta
            parts[1] = parts[1] + mid[c] * total
            parts[2] = parts[2] + r * scaled
            parts[3] = parts[3] + total * scaled
    sub = rows_of((8, 128))
    out = jnp.zeros((8, 128), f32)
    for k in range(4):
        part = parts[k][0:8] + parts[k][8:16]
        out = jnp.where(sub == k, jnp.sum(part, axis=0, keepdims=True), out)
    sums[...] = out


def quadratic(d, o):
    norm = sum(abs(c) for c in o)
    square = d[0] * d[0] + d[1] * d[1] + d[2] * d[2]
    along, sign = None, 1
    for c in range(3):
        if o[c] != 0:
            if along is None:
                along, sign = d[c], o[c]
            else:
                along = along + d[c] if o[c] == sign else along - d[c]
    return (0.5 / norm) * square + (0.5 / (norm * norm)) * (along * along)


flat_half = [(1, -1, 0), (1, 0, 0), (1, 1, 0), (0, 1, 0)]
up_half = [(a, b, 1) for a in (-1, 0, 1) for b in (-1, 0, 1)]


def finish_step(
    ext, ends, around, total, image, inverse, res, dire, hinv, hside,
    new_sol, new_res, new_dir, sens, us, scaled,
):
    lane = lanes_of((24, 128))
    lows = lane % 8 < 4
    tot = jnp.sum(total[...], axis=1, keepdims=True)
    rz, pq, s2, s3 = tot[0:1], tot[1:2], tot[2:3], tot[3:4]
    alpha = rz / pq
    beta = (rz + alpha * (alpha * s3 - 2.0 * s2)) / rz

    for x in range(8):
        for c in range(3):
            r = res[c, x] - alpha * image[c, x]
            new_res[c, x] = r
            new_dir[c, x] = r * inverse[c, x] + beta * dire[c, x]

    halos = []
    lefts, rights = [], []
    for c in range(3):
        halo_u = around[3 + c] + alpha * around[c]
        own_u = ends[3 + c] + alpha * ends[c]
        halos.append(halo_u)
        lefts.append(jnp.where(lows, halo_u, own_u))
        rights.append(jnp.where(lows, own_u, halo_u))
    for X in range(16):
        for c in range(3):
            u = ext[3 + c, X] + alpha * ext[c, X]
            if 4 <= X < 12:
                new_sol[c, X - 4] = roll(u, -HALO, 0)[0:16]
            near = roll(halos[c], 124 - 8 * X, 1)
            up = roll(jnp.where(lane == 0, near, u), -1, 1)
            for z, plane in enumerate((u, up)):
                us[3 * z, c, X] = roll(plane, 1, 0)
                us[3 * z + 1, c, X] = plane
                us[3 * z + 2, c, X] = roll(plane, -1, 0)

    sides, side_low = [], None
    den_left = jnp.where(lows, around[6], ends[6])
    den_right = jnp.where(lows, ends[6], around[6])
    for s, (u, den) in enumerate(((lefts, den_left), (rights, den_right))):
        turned = {oy: [roll(v, -oy, 0) for v in u] for oy in (-1, 0, 1)}
        forward = jnp.zeros((24, 128), f32)
        back = {(oy, oz): jnp.zeros((24, 128), f32) for oy in (-1, 0, 1) for oz in (0, 1)}
        for o in flat_half + up_half:
            move = 8 * o[0] + o[2]
            g = quadratic([u[c] - roll(turned[o[1]][c], -move, 1) for c in range(3)], o)
            forward = forward + g
            back[o[1], o[2]] = back[o[1], o[2]] + roll(g, 8 * o[0], 1)
        flat = back[0, 0] + roll(back[1, 0], 1, 0) + roll(back[-1, 0], -1, 0)
        up = back[0, 1] + roll(back[1, 1], 1, 0) + roll(back[-1, 1], -1, 0)
        if s == 0:
            side_low = up
        energy = forward + flat + roll(up, 1, 1)
        sides.append((-penalty * (1.0 - stiff_floor)) * (den * den) * energy * hside[s])
    ends_scaled = jnp.where(lows, sides[0], sides[1])

    zero = jnp.zeros((24, 128), f32)
    forward = [zero] * 16
    back = [{(oy, oz): None for oy in (-1, 0, 1) for oz in (0, 1)} for _ in range(16)]
    for X in range(0, 16):
        mine = [us[1, c, X] for c in range(3)]
        for o in flat_half + up_half:
            to = X + o[0]
            if not 0 <= to < 16:
                continue
            k = 3 * o[2] + o[1] + 1
            g = quadratic([mine[c] - us[k, c, to] for c in range(3)], o)
            forward[X] = forward[X] + g
            old = back[to][o[1], o[2]]
            back[to][o[1], o[2]] = g if old is None else old + g
        done = X - 1
        if done >= 1:
            bk = back[done]
            flat = bk[0, 0] + roll(bk[1, 0], 1, 0) + roll(bk[-1, 0], -1, 0)
            up = bk[0, 1] + roll(bk[1, 1], 1, 0) + roll(bk[-1, 1], -1, 0)
            below = roll(side_low, 127 - (8 * done + 3), 1)
            up = roll(jnp.where(lane == 127, below, up), 1, 1)
            den = ext[6, done]
            energy = forward[done] + flat + up
            scaled[done] = (-penalty * (1.0 - stiff_floor)) * (den * den) * energy * hinv[done]

    rows = [[None] * (RAD + 1) for _ in range(8)]
    for X in range(1, 15):
        s = scaled[X]
        near = roll(ends_scaled, 124 - 8 * X, 1)
        fold = [s]
        for k in range(1, RAD + 1):
            above = roll(jnp.where(lane < k, near, s), -k, 1)
            under = roll(jnp.where(lane >= 128 - k, near, s), k, 1)
            fold.append(above + under)
        made = {}
        for b in range(RAD + 1):
            for a in range(-RAD, RAD + 1):
                x = X - a - HALO
                if not 0 <= x < 8 or cone(a, b, 0) <= 0:
                    continue
                key = a * a + b * b
                if key not in made:
                    line = None
                    for k in range(RAD + 1):
                        w = cone(a, b, k)
                        if w > 0:
                            line = w * fold[k] if line is None else line + w * fold[k]
                    made[key] = line
                old = rows[x][b]
                rows[x][b] = made[key] if old is None else old + made[key]
        x = X - 2 * RAD - 1
        if x >= 0:
            value = rows[x][0]
            for b in range(1, RAD + 1):
                value = value + roll(rows[x][b], b, 0) + roll(rows[x][b], -b, 0)
            sens[x] = roll(value, -HALO, 0)[0:16]


def partner(place, turn, count):
    other = (place ^ 1) if turn == 0 else ((place + 1) ^ 1) - 1
    return other if 0 <= other < count else None


def swap_pairs(counts, turns):
    pairs = []
    for flat in range(math.prod(counts)):
        rest, place = flat, []
        for count in reversed(counts):
            place.insert(0, rest % count)
            rest //= count
        to = [p if t is None else partner(p, t, c) for p, t, c in zip(place, turns, counts)]
        if None in to:
            to = place
        index = 0
        for p, count in zip(to, counts):
            index = index * count + p
        pairs.append((flat, index))
    return pairs


def prime_factors(count):
    factors, p = [], 2
    while count > 1:
        while count % p == 0:
            factors.append(p)
            count //= p
        p += 1
    return factors


def total_over(value, mesh_shape):
    for axis in AXES:
        count = mesh_shape[axis]
        stride = 1
        for factor in prime_factors(count):
            block = stride * factor
            got = []
            for step in range(1, factor):
                pairs = []
                for i in range(count):
                    digit = (i // stride) % factor
                    to = i + (((digit + step) % factor) - digit) * stride
                    pairs.append((i, to))
                got.append(lax.ppermute(value, axis, pairs))
            for other in got:
                value = value + other
            stride = block
    return value


def per_device(mesh_shape, solution, residual, direction, density, labels):
    nx, ny, nz = (mesh_shape[a] for a in AXES)
    half, full, corner = (7, 4, 16, 128), (7, 4, 8, 128), (7, 2, 8, 128)
    rounds_y = 1 if ny == 2 else 2
    field, flat = (3, 8, 16, 128), (8, 16, 128)
    packed = call(
        functools.partial(pack_faces, rounds_y),
        [half, half] + [full, corner, corner] * rounds_y,
        solution, direction, density, labels,
        far=range(4),
        scratch=[
            pltpu.VMEM(field, f32), pltpu.VMEM(field, f32), pltpu.VMEM(flat, f32),
            pltpu.VMEM(flat, jnp.int32), pltpu.SemaphoreType.DMA((4,)),
        ],
    )
    halves = packed[:2]
    plane = ("gx", "gy")
    got = [lax.ppermute(halves[r], plane, swap_pairs((nx, ny), (r, None))) for r in (0, 1)]
    strips = []
    for s in range(rounds_y):
        for array, turn in zip(packed[2 + 3 * s : 5 + 3 * s], (None, 0, 1)):
            strips.append(lax.ppermute(array, plane, swap_pairs((nx, ny), (turn, s))))
    hinv, hside = call(functools.partial(inverse_sums, (nx, ny, nz)), [(16, 24, 128), (2, 24, 128)])
    ext, ends = call(
        functools.partial(extend, (nx, ny, nz)),
        [(7, 16, 24, 128), (7, 24, 128)],
        *halves, *got, *strips,
    )
    ends_got = [lax.ppermute(ends, "gz", swap_pairs((nz,), (r,))) for r in (0, 1)]
    image, inverse, sums, around = call(
        functools.partial(apply_operator, nz),
        [field, field, (8, 128), (7, 24, 128)],
        ext, *ends_got, residual, labels,
        scratch=[pltpu.VMEM((4, 3, 3, 10, 16, 128), f32)],
    )
    total = total_over(sums, mesh_shape)
    return tuple(
        call(
            finish_step,
            [field, field, field, flat],
            ext, ends, around, total, image, inverse, residual, direction, hinv, hside,
            scratch=[pltpu.VMEM((6, 3, 16, 24, 128), f32), pltpu.VMEM((16, 24, 128), f32)],
        )
    )


def solution(mesh):
    wide, flat = P(None, "gx", "gy", "gz"), P("gx", "gy", "gz")
    return jax.shard_map(
        functools.partial(per_device, dict(mesh.shape)),
        mesh=mesh,
        in_specs=(wide, wide, wide, flat, flat),
        out_specs=(wide, wide, wide, flat),
        check_vma=False,
    )
```

```python
import functools
import math

import jax
import jax.numpy as jnp
from jax import lax
from jax.experimental import pallas as pl
from jax.experimental.pallas import tpu as pltpu
from jax.sharding import PartitionSpec as P

RAD = 3
HALO = RAD + 1
stiff_floor = 0.001
penalty = 3.0
f32 = jnp.float32
neighbour_offsets = [
    (off_x, off_y, off_z)
    for off_x in (-1, 0, 1)
    for off_y in (-1, 0, 1)
    for off_z in (-1, 0, 1)
    if (off_x, off_y, off_z) != (0, 0, 0)
]
AXES = ("gx", "gy", "gz")


def cone(a, b, k):
    return max(0.0, RAD + 0.5 - math.sqrt(a * a + b * b + k * k))


def lanes_of(shape):
    return lax.broadcasted_iota(jnp.int32, shape, len(shape) - 1)


def rows_of(shape):
    return lax.broadcasted_iota(jnp.int32, shape, len(shape) - 2)


def roll(value, amount, axis):
    size = value.shape[axis]
    amount = amount % size
    return value if amount == 0 else pltpu.roll(value, amount, axis)


def call(body, outs, *args, scratch=(), cost=20000, far=(), far_out=False):
    args = [
        pltpu.with_memory_space_constraint(a, pltpu.HBM) if i in far else a for i, a in enumerate(args)
    ]
    return pl.pallas_call(
        body,
        out_shape=[jax.ShapeDtypeStruct(shape, f32) for shape in outs],
        in_specs=[
            pl.BlockSpec(memory_space=pl.ANY if i in far else pltpu.VMEM) for i in range(len(args))
        ],
        out_specs=[pl.BlockSpec(memory_space=pl.ANY if far_out else pltpu.VMEM)] * len(outs),
        scratch_shapes=list(scratch),
        compiler_params=pltpu.CompilerParams(vmem_limit_bytes=24 * 1024 * 1024),
        cost_estimate=pl.CostEstimate(flops=cost * 1000, bytes_accessed=cost, transcendentals=0),
    )(*args)


def is_even(axis):
    return lax.axis_index(axis) % 2 == 0


def pack_faces(rounds_y, sol_any, dire_any, den_any, lab_any, *refs):
    halves, packs = refs[:2], refs[2 : 2 + 3 * rounds_y]
    sol, dire, den, lab, sems = refs[2 + 3 * rounds_y :]
    copies = [
        pltpu.make_async_copy(source, target, sems.at[i])
        for i, (source, target) in enumerate(
            ((dire_any, dire), (sol_any, sol), (den_any, den), (lab_any, lab))
        )
    ]
    for copy in copies:
        copy.start()
    sub = rows_of((8, 128))
    even_x, even_y = is_even("gx"), is_even("gy")
    for copy in copies:
        copy.wait()

    def masked(x):
        label = lab[x]
        keep = jnp.where(label == 1, 0.0, 1.0).astype(f32)
        keep_last = jnp.where(label >= 1, 0.0, 1.0).astype(f32)
        fields = [dire[0, x] * keep, dire[1, x] * keep, dire[2, x] * keep_last]
        return fields + [sol[0, x], sol[1, x], sol[2, x], den[x]]

    for t in range(2):
        planes = {x: masked(x) for x in (2 * t, 2 * t + 1, 2 * t + 4, 2 * t + 5)}
        for f in range(7):
            for i in (2 * t, 2 * t + 1):
                low, high = planes[i][f], planes[i + 4][f]
                halves[0][f, i] = jnp.where(even_x, high, low)
                halves[1][f, i] = jnp.where(even_x, low, high)
            tiles = []
            for i in (2 * t, 2 * t + 4):
                p, q = planes[i][f], planes[i + 1][f]
                low = jnp.where(sub < 4, p[0:8], roll(q[0:8], 4, 0))
                high = jnp.where(sub < 4, roll(p[8:16], 4, 0), q[8:16])
                tiles.append((jnp.where(even_y, high, low), jnp.where(even_y, low, high)))
            for s in range(rounds_y):
                rows, corner0, corner1 = packs[3 * s : 3 * s + 3]
                low, high = tiles[0][s], tiles[1][s]
                rows[f, t] = low
                rows[f, t + 2] = high
                corner0[f, t] = jnp.where(even_x, high, low)
                corner1[f, t] = jnp.where(even_x, low, high)


def extend(counts, half0, half1, got0, got1, *refs):
    nx, ny, nz = counts
    sides, (ext, ends) = refs[:-2], refs[-2:]
    sub = rows_of((8, 128))
    lane = lanes_of((24, 128))
    ix, iy = lax.axis_index("gx"), lax.axis_index("gy")
    even_y = is_even("gy")
    x_ok = ((ix > 0).astype(f32), (ix < nx - 1).astype(f32))
    y_ok = ((iy > 0).astype(f32), (iy < ny - 1).astype(f32))

    def body(blocks, order):
        def strip(which, f, t):
            tiles = []
            for s in range(len(sides) // 3):
                rows, corner0, corner1 = sides[3 * s : 3 * s + 3]
                ref = rows if which is None else (corner0, corner1)[order[which]]
                tiles.append(ref[f, t])
            keep = 1.0 if which is None else x_ok[which]
            other = tiles[-1]
            low = jnp.where(even_y, other, tiles[0]) * (y_ok[0] * keep)
            high = jnp.where(even_y, tiles[0], other) * (y_ok[1] * keep)
            return low, high

        for f in range(7):
            packed = None
            for X in range(16):
                own = blocks[X // 4][f, X % 4]
                which = None
                if X < 4:
                    which, t = 0, X // 2
                elif X >= 12:
                    which, t = 1, (X - 12) // 2
                else:
                    t = (X - 4) // 2
                if which is not None:
                    own = own * x_ok[which]
                low, high = strip(which, f, t)
                a, b = roll(own[0:8], 4, 0), roll(own[8:16], 4, 0)
                if X % 2 == 0:
                    high = roll(high, 4, 0)
                else:
                    low = roll(low, 4, 0)
                plane = jnp.concatenate(
                    [jnp.where(sub < 4, low, a), jnp.where(sub < 4, a, b), jnp.where(sub < 4, b, high)],
                    axis=0,
                )
                ext[f, X] = plane
                turned = roll(plane, 8 * X + 4, 1)
                packed = turned if X == 0 else jnp.where(lane >= 8 * X, turned, packed)
            ends[f] = packed

    @pl.when(ix % 2 == 0)
    def _():
        body((got1, half1, half0, got0), (1, 0))

    @pl.when(ix % 2 == 1)
    def _():
        body((got0, half0, half1, got1), (0, 1))


def inverse_sums(counts, main, side):
    shape = (24, 128)
    row, lane = rows_of(shape), lanes_of(shape)
    nx, ny, nz = counts
    base_x = lax.axis_index("gx") * 8 - HALO
    base_y = lax.axis_index("gy") * 16 - HALO
    base_z = lax.axis_index("gz") * 128

    def folded(place, limit):
        def inside(p):
            return jnp.where((p >= 0) & (p < limit), 1.0, 0.0).astype(f32)

        return [inside(place)] + [inside(place - k) + inside(place + k) for k in range(1, RAD + 1)]

    along_y = folded(row + base_y, ny * 16)

    def partial(along_z):
        table = []
        for a in range(RAD + 1):
            total = jnp.zeros(shape, f32)
            for b in range(RAD + 1):
                line = None
                for k in range(RAD + 1):
                    w = cone(a, b, k)
                    if w > 0:
                        line = w * along_z[k] if line is None else line + w * along_z[k]
                if line is not None:
                    total = total + along_y[b] * line
            table.append(total)
        return table

    def finish(total, along_x, along_z):
        inner = along_x[0] * along_y[0] * along_z[0] > 0
        return jnp.where(inner, 1.0 / jnp.where(inner, total, 1.0), 0.0)

    along_z = folded(lane + base_z, nz * 128)
    table = partial(along_z)
    for X in range(16):
        along_x = folded(jnp.full(shape, X, jnp.int32) + base_x, nx * 8)
        total = sum(along_x[a] * table[a] for a in range(RAD + 1))
        main[X] = finish(total, along_x, along_z)
    place = lane % 8
    along_x = folded(lane // 8 + base_x, nx * 8)
    for s, shift in enumerate((-4, 124)):
        along_z = folded(place + (base_z + shift), nz * 128)
        table = partial(along_z)
        total = sum(along_x[a] * table[a] for a in range(RAD + 1))
        side[s] = finish(total, along_x, along_z)


def apply_operator(nz, ext, got0, got1, res, lab, image, inverse, sums, around, shifts):
    lane = lanes_of((24, 128))
    fields = (0, 1, 2, 6)
    iz = lax.axis_index("gz")
    lows = lane % 8 < 4
    from_zero = (lane // 4) % 2 == (iz + 1) % 2
    keep = jnp.where(lows, (iz > 0).astype(f32), (iz < nz - 1).astype(f32))
    for f in range(7):
        around[f] = jnp.where(from_zero, got0[f], got1[f]) * keep
    for g, f in enumerate(fields):
        halo = around[f]
        for n in range(10):
            X = n + 3
            value = ext[f, X]
            near = roll(halo, 124 - 8 * X, 1)
            if g == 3:
                value = stiff_floor + (1.0 - stiff_floor) * value * value * value
                value = jnp.where(ext[f, X] > 0, value, 0.0)
                near_stiff = stiff_floor + (1.0 - stiff_floor) * near * near * near
                near = jnp.where(near > 0, near_stiff, 0.0)
            up = roll(jnp.where(lane == 0, near, value), -1, 1)
            down = roll(jnp.where(lane == 127, near, value), 1, 1)
            for z, plane in enumerate((down, value, up)):
                for y in range(3):
                    shifts[g, y, z, n] = roll(plane, -(HALO - 1 + y), 0)[0:16]
    parts = [jnp.zeros((16, 128), f32) for _ in range(4)]
    for x in range(8):
        n = x + 1
        mid = [shifts[g, 1, 1, n] for g in range(4)]
        classes = {1: [None] * 3, 2: [None] * 3, 3: [None] * 3}
        faces = [None] * 3
        edges = [None] * 3
        corners = None

        def add(old, new):
            return new if old is None else old + new

        for o in neighbour_offsets:
            near = [shifts[g, 1 + o[1], 1 + o[2], n + o[0]] for g in range(4)]
            norm = sum(abs(c) for c in o)
            weight = mid[3] + near[3]
            d = [mid[c] - near[c] for c in range(3)]
            acc = classes[norm]
            if norm == 1:
                c0 = [c for c in range(3) if o[c] != 0][0]
                faces[c0] = add(faces[c0], near[3])
                for c in range(3):
                    acc[c] = add(acc[c], weight * (d[c] + d[c] if c == c0 else d[c]))
            else:
                along = None
                for c in range(3):
                    if o[c] != 0:
                        term = d[c]
                        if along is None:
                            along, sign = term, o[c]
                        else:
                            along = along + term if o[c] == sign else along - term
                along = along * (1.0 / norm)
                for c in range(3):
                    if o[c] == 0:
                        pulled = d[c]
                    elif o[c] == sign:
                        pulled = d[c] + along
                    else:
                        pulled = d[c] - along
                    acc[c] = add(acc[c], weight * pulled)
                if norm == 2:
                    c0 = [c for c in range(3) if o[c] == 0][0]
                    edges[c0] = add(edges[c0], near[3])
                else:
                    corners = add(corners, near[3])
        s0 = mid[3]
        all_faces = faces[0] + faces[1] + faces[2]
        all_edges = edges[0] + edges[1] + edges[2]
        common = (all_faces + 6.0 * s0) + 0.75 * (all_edges + 12.0 * s0) + (4.0 / 9.0) * (corners + 8.0 * s0)
        label = lab[x]
        for c in range(3):
            diag = 0.5 * (common + (faces[c] + 2.0 * s0) - 0.25 * (edges[c] + 4.0 * s0))
            fixed = (label == 1) if c < 2 else (label >= 1)
            total = 0.5 * classes[1][c] + 0.25 * classes[2][c] + (1.0 / 6.0) * classes[3][c]
            total = jnp.where(fixed, 0.0, total)
            inv = 1.0 / jnp.where(fixed, 1.0, diag)
            r = res[c, x]
            zeta = r * inv
            scaled = total * inv
            image[c, x] = total
            inverse[c, x] = inv
            parts[0] = parts[0] + r * zeta
            parts[1] = parts[1] + mid[c] * total
            parts[2] = parts[2] + r * scaled
            parts[3] = parts[3] + total * scaled
    sub = rows_of((8, 128))
    out = jnp.zeros((8, 128), f32)
    for k in range(4):
        part = parts[k][0:8] + parts[k][8:16]
        out = jnp.where(sub == k, jnp.sum(part, axis=0, keepdims=True), out)
    sums[...] = out


def quadratic(d, o):
    norm = sum(abs(c) for c in o)
    square = d[0] * d[0] + d[1] * d[1] + d[2] * d[2]
    along, sign = None, 1
    for c in range(3):
        if o[c] != 0:
            if along is None:
                along, sign = d[c], o[c]
            else:
                along = along + d[c] if o[c] == sign else along - d[c]
    if norm == 1:
        return square + along * along
    return (1.0 / norm) * square + (1.0 / (norm * norm)) * (along * along)


pairs = [((1, 0, 0), 0, 0, 0, 0)]
pairs += [((a, 1, 0), 0, 0, 2, 2) for a in (-1, 0, 1)]
pairs += [((a, 0, 1), 0, 0, 1, 1) for a in (-1, 0, 1)]
pairs += [((a, 1, 1), 0, 0, 3, 3) for a in (-1, 0, 1)]
pairs += [((a, -1, 1), 2, 2, 1, 1) for a in (-1, 0, 1)]
energy_scale = -penalty * (1.0 - stiff_floor) * 0.5


def plus(old, new):
    return new if old is None else old + new


def finish_step(
    ext, ends, around, total, image, inverse, res, dire, hinv, hside,
    new_sol_any, new_res_any, new_dir_any, sens_any, us, scaled, new_sol, new_res, new_dir, sens, sems,
):
    lane = lanes_of((24, 128))
    lows = lane % 8 < 4
    copies = [
        pltpu.make_async_copy(source, target, sems.at[i])
        for i, (source, target) in enumerate(
            ((new_res, new_res_any), (new_dir, new_dir_any), (new_sol, new_sol_any), (sens, sens_any))
        )
    ]
    tot = jnp.sum(total[...], axis=1, keepdims=True)
    rz, pq, s2, s3 = tot[0:1], tot[1:2], tot[2:3], tot[3:4]
    alpha = rz / pq
    beta = (rz + alpha * (alpha * s3 - 2.0 * s2)) / rz

    for x in range(8):
        for c in range(3):
            r = res[c, x] - alpha * image[c, x]
            new_res[c, x] = r
            new_dir[c, x] = r * inverse[c, x] + beta * dire[c, x]
    copies[0].start()
    copies[1].start()

    halos, lefts, rights = [], [], []
    for c in range(3):
        halo_u = around[3 + c] + alpha * around[c]
        own_u = ends[3 + c] + alpha * ends[c]
        halos.append(halo_u)
        lefts.append(jnp.where(lows, halo_u, own_u))
        rights.append(jnp.where(lows, own_u, halo_u))
    for X in range(16):
        for c in range(3):
            u = ext[3 + c, X] + alpha * ext[c, X]
            if 4 <= X < 12:
                new_sol[c, X - 4] = roll(u, -HALO, 0)[0:16]
            near = roll(halos[c], 124 - 8 * X, 1)
            up = roll(jnp.where(lane == 0, near, u), -1, 1)
            us[0, c, X] = u
            us[1, c, X] = up
            us[2, c, X] = roll(u, -1, 0)
            us[3, c, X] = roll(up, -1, 0)
    copies[2].start()

    sides, side_low = [], None
    den_left = jnp.where(lows, around[6], ends[6])
    den_right = jnp.where(lows, ends[6], around[6])
    for s, (u, den) in enumerate(((lefts, den_left), (rights, den_right))):
        up = [roll(v, -1, 1) for v in u]
        moved = [u, up, [roll(v, -1, 0) for v in u], [roll(v, -1, 0) for v in up]]
        far = {}
        acc = {}
        for o, field0, frame0, field1, frame1 in pairs:
            key = (field1, o[0])
            if key not in far:
                far[key] = [roll(v, -8 * o[0], 1) for v in moved[field1]]
            g = quadratic([moved[field0][c] - far[key][c] for c in range(3)], o)
            acc[frame0, 0] = plus(acc.get((frame0, 0)), g)
            acc[frame1, o[0]] = plus(acc.get((frame1, o[0])), g)
        frames = []
        for frame in range(4):
            value = None
            for a in (-1, 0, 1):
                if (frame, a) in acc:
                    value = plus(value, roll(acc[frame, a], 8 * a, 1))
            frames.append(value)
        up = frames[1] + roll(frames[3], 1, 0)
        if s == 0:
            side_low = up
        energy = frames[0] + roll(frames[2], 1, 0) + roll(up, 1, 1)
        sides.append(energy_scale * (den * den) * energy * hside[s])
    ends_scaled = jnp.where(lows, sides[0], sides[1])

    acc = [[None] * 4 for _ in range(16)]
    for X in range(16):
        for o, field0, frame0, field1, frame1 in pairs:
            to = X + o[0]
            if not 0 <= to < 16 or not (1 <= X < 15 or 1 <= to < 15):
                continue
            g = quadratic([us[field0, c, X] - us[field1, c, to] for c in range(3)], o)
            if 1 <= X < 15:
                acc[X][frame0] = plus(acc[X][frame0], g)
            if 1 <= to < 15:
                acc[to][frame1] = plus(acc[to][frame1], g)
        done = X - 1
        if done >= 1:
            frames = acc[done]
            up = frames[1] + roll(frames[3], 1, 0)
            below = roll(side_low, 127 - (8 * done + 3), 1)
            up = roll(jnp.where(lane == 127, below, up), 1, 1)
            den = ext[6, done]
            energy = frames[0] + roll(frames[2], 1, 0) + up
            scaled[done] = energy_scale * (den * den) * energy * hinv[done]

    rows = [[None] * (RAD + 1) for _ in range(8)]
    for X in range(1, 15):
        s = scaled[X]
        near = roll(ends_scaled, 124 - 8 * X, 1)
        fold = [s]
        for k in range(1, RAD + 1):
            above = roll(jnp.where(lane < k, near, s), -k, 1)
            under = roll(jnp.where(lane >= 128 - k, near, s), k, 1)
            fold.append(above + under)
        made = {}
        for b in range(RAD + 1):
            for a in range(-RAD, RAD + 1):
                x = X - a - HALO
                if not 0 <= x < 8 or cone(a, b, 0) <= 0:
                    continue
                key = a * a + b * b
                if key not in made:
                    line = None
                    for k in range(RAD + 1):
                        w = cone(a, b, k)
                        if w > 0:
                            line = w * fold[k] if line is None else line + w * fold[k]
                    made[key] = line
                old = rows[x][b]
                rows[x][b] = made[key] if old is None else old + made[key]
        x = X - 2 * RAD - 1
        if x >= 0:
            value = rows[x][0]
            for b in range(1, RAD + 1):
                value = value + roll(rows[x][b], b, 0) + roll(rows[x][b], -b, 0)
            sens[x] = roll(value, -HALO, 0)[0:16]
    copies[3].start()
    for copy in copies:
        copy.wait()


def partner(place, turn, count):
    other = (place ^ 1) if turn == 0 else ((place + 1) ^ 1) - 1
    return other if 0 <= other < count else None


def swap_pairs(counts, turns):
    pairs = []
    for flat in range(math.prod(counts)):
        rest, place = flat, []
        for count in reversed(counts):
            place.insert(0, rest % count)
            rest //= count
        to = [p if t is None else partner(p, t, c) for p, t, c in zip(place, turns, counts)]
        if None in to:
            to = place
        index = 0
        for p, count in zip(to, counts):
            index = index * count + p
        pairs.append((flat, index))
    return pairs


def prime_factors(count):
    factors, p = [], 2
    while count > 1:
        while count % p == 0:
            factors.append(p)
            count //= p
        p += 1
    return factors


def total_over(value, mesh_shape):
    return jnp.sum(lax.all_gather(value, AXES), axis=0)


def per_device(mesh_shape, solution, residual, direction, density, labels):
    nx, ny, nz = (mesh_shape[a] for a in AXES)
    half, full, corner = (7, 4, 16, 128), (7, 4, 8, 128), (7, 2, 8, 128)
    rounds_y = 1 if ny == 2 else 2
    field, flat = (3, 8, 16, 128), (8, 16, 128)
    packed = call(
        functools.partial(pack_faces, rounds_y),
        [half, half] + [full, corner, corner] * rounds_y,
        solution, direction, density, labels,
        far=range(4),
        scratch=[
            pltpu.VMEM(field, f32), pltpu.VMEM(field, f32), pltpu.VMEM(flat, f32),
            pltpu.VMEM(flat, jnp.int32), pltpu.SemaphoreType.DMA((4,)),
        ],
    )
    halves = packed[:2]
    plane = ("gx", "gy")
    got = [lax.ppermute(halves[r], plane, swap_pairs((nx, ny), (r, None))) for r in (0, 1)]
    strips = []
    for s in range(rounds_y):
        for array, turn in zip(packed[2 + 3 * s : 5 + 3 * s], (None, 0, 1)):
            strips.append(lax.ppermute(array, plane, swap_pairs((nx, ny), (turn, s))))
    hinv, hside = call(functools.partial(inverse_sums, (nx, ny, nz)), [(16, 24, 128), (2, 24, 128)])
    ext, ends = call(
        functools.partial(extend, (nx, ny, nz)),
        [(7, 16, 24, 128), (7, 24, 128)],
        *halves, *got, *strips,
    )
    ends_got = [lax.ppermute(ends, "gz", swap_pairs((nz,), (r,))) for r in (0, 1)]
    image, inverse, sums, around = call(
        functools.partial(apply_operator, nz),
        [field, field, (8, 128), (7, 24, 128)],
        ext, *ends_got, residual, labels,
        scratch=[pltpu.VMEM((4, 3, 3, 10, 16, 128), f32)],
    )
    total = total_over(sums, mesh_shape)
    return tuple(
        call(
            finish_step,
            [field, field, field, flat],
            ext, ends, around, total, image, inverse, residual, direction, hinv, hside,
            scratch=[
                pltpu.VMEM((4, 3, 16, 24, 128), f32), pltpu.VMEM((16, 24, 128), f32),
                pltpu.VMEM(field, f32), pltpu.VMEM(field, f32), pltpu.VMEM(field, f32),
                pltpu.VMEM(flat, f32), pltpu.SemaphoreType.DMA((4,)),
            ],
            far_out=True,
        )
    )


def solution(mesh):
    wide, flat = P(None, "gx", "gy", "gz"), P("gx", "gy", "gz")
    return jax.shard_map(
        functools.partial(per_device, dict(mesh.shape)),
        mesh=mesh,
        in_specs=(wide, wide, wide, flat, flat),
        out_specs=(wide, wide, wide, flat),
        check_vma=False,
    )
```

```python
import functools
import math

import jax
import jax.numpy as jnp
from jax import lax
from jax.experimental import pallas as pl
from jax.experimental.pallas import tpu as pltpu
from jax.sharding import PartitionSpec as P

RAD = 3
HALO = RAD + 1
stiff_floor = 0.001
penalty = 3.0
f32 = jnp.float32
neighbour_offsets = [
    (off_x, off_y, off_z)
    for off_x in (-1, 0, 1)
    for off_y in (-1, 0, 1)
    for off_z in (-1, 0, 1)
    if (off_x, off_y, off_z) != (0, 0, 0)
]
AXES = ("gx", "gy", "gz")


def cone(a, b, k):
    return max(0.0, RAD + 0.5 - math.sqrt(a * a + b * b + k * k))


def lanes_of(shape):
    return lax.broadcasted_iota(jnp.int32, shape, len(shape) - 1)


def rows_of(shape):
    return lax.broadcasted_iota(jnp.int32, shape, len(shape) - 2)


def roll(value, amount, axis):
    size = value.shape[axis]
    amount = amount % size
    return value if amount == 0 else pltpu.roll(value, amount, axis)


def call(body, outs, *args, scratch=(), cost=20000, far=(), far_out=False):
    args = [
        pltpu.with_memory_space_constraint(a, pltpu.HBM) if i in far else a for i, a in enumerate(args)
    ]
    return pl.pallas_call(
        body,
        out_shape=[jax.ShapeDtypeStruct(shape, f32) for shape in outs],
        in_specs=[
            pl.BlockSpec(memory_space=pl.ANY if i in far else pltpu.VMEM) for i in range(len(args))
        ],
        out_specs=[pl.BlockSpec(memory_space=pl.ANY if far_out else pltpu.VMEM)] * len(outs),
        scratch_shapes=list(scratch),
        compiler_params=pltpu.CompilerParams(vmem_limit_bytes=24 * 1024 * 1024),
        cost_estimate=pl.CostEstimate(flops=cost * 1000, bytes_accessed=cost, transcendentals=0),
    )(*args)


def is_even(axis):
    return lax.axis_index(axis) % 2 == 0


def pack_faces(rounds_y, sol_any, dire_any, den_any, lab_any, *refs):
    halves, packs = refs[:2], refs[2 : 2 + 3 * rounds_y]
    sol, dire, den, lab, sems = refs[2 + 3 * rounds_y :]
    copies = [
        pltpu.make_async_copy(source, target, sems.at[i])
        for i, (source, target) in enumerate(
            ((dire_any, dire), (sol_any, sol), (den_any, den), (lab_any, lab))
        )
    ]
    for copy in copies:
        copy.start()
    sub = rows_of((8, 128))
    even_x, even_y = is_even("gx"), is_even("gy")
    for copy in copies:
        copy.wait()

    def masked(x):
        label = lab[x]
        keep = jnp.where(label == 1, 0.0, 1.0).astype(f32)
        keep_last = jnp.where(label >= 1, 0.0, 1.0).astype(f32)
        fields = [dire[0, x] * keep, dire[1, x] * keep, dire[2, x] * keep_last]
        return fields + [sol[0, x], sol[1, x], sol[2, x], den[x]]

    for t in range(2):
        planes = {x: masked(x) for x in (2 * t, 2 * t + 1, 2 * t + 4, 2 * t + 5)}
        for f in range(7):
            for i in (2 * t, 2 * t + 1):
                low, high = planes[i][f], planes[i + 4][f]
                halves[0][f, i] = jnp.where(even_x, high, low)
                halves[1][f, i] = jnp.where(even_x, low, high)
            tiles = []
            for i in (2 * t, 2 * t + 4):
                p, q = planes[i][f], planes[i + 1][f]
                low = jnp.where(sub < 4, p[0:8], roll(q[0:8], 4, 0))
                high = jnp.where(sub < 4, roll(p[8:16], 4, 0), q[8:16])
                tiles.append((jnp.where(even_y, high, low), jnp.where(even_y, low, high)))
            for s in range(rounds_y):
                rows, corner0, corner1 = packs[3 * s : 3 * s + 3]
                low, high = tiles[0][s], tiles[1][s]
                rows[f, t] = low
                rows[f, t + 2] = high
                corner0[f, t] = jnp.where(even_x, high, low)
                corner1[f, t] = jnp.where(even_x, low, high)


def extend(counts, half0, half1, got0, got1, *refs):
    nx, ny, nz = counts
    sides, (ext, ends) = refs[:-2], refs[-2:]
    sub = rows_of((8, 128))
    lane = lanes_of((24, 128))
    ix, iy = lax.axis_index("gx"), lax.axis_index("gy")
    even_y = is_even("gy")
    x_ok = ((ix > 0).astype(f32), (ix < nx - 1).astype(f32))
    y_ok = ((iy > 0).astype(f32), (iy < ny - 1).astype(f32))

    def body(blocks, order):
        def strip(which, f, t):
            tiles = []
            for s in range(len(sides) // 3):
                rows, corner0, corner1 = sides[3 * s : 3 * s + 3]
                ref = rows if which is None else (corner0, corner1)[order[which]]
                tiles.append(ref[f, t])
            keep = 1.0 if which is None else x_ok[which]
            other = tiles[-1]
            low = jnp.where(even_y, other, tiles[0]) * (y_ok[0] * keep)
            high = jnp.where(even_y, tiles[0], other) * (y_ok[1] * keep)
            return low, high

        for f in range(7):
            packed = None
            for X in range(16):
                own = blocks[X // 4][f, X % 4]
                which = None
                if X < 4:
                    which, t = 0, X // 2
                elif X >= 12:
                    which, t = 1, (X - 12) // 2
                else:
                    t = (X - 4) // 2
                if which is not None:
                    own = own * x_ok[which]
                low, high = strip(which, f, t)
                if X % 2 == 0:
                    low = roll(low, 4, 0)
                else:
                    high = roll(high, 4, 0)
                plane = jnp.concatenate([own, jnp.where(sub < 4, high, low)], axis=0)
                ext[f, X] = plane
                turned = roll(plane, 8 * X + 4, 1)
                packed = turned if X == 0 else jnp.where(lane >= 8 * X, turned, packed)
            ends[f] = packed

    @pl.when(ix % 2 == 0)
    def _():
        body((got1, half1, half0, got0), (1, 0))

    @pl.when(ix % 2 == 1)
    def _():
        body((got0, half0, half1, got1), (0, 1))


def inverse_sums(counts, main, side):
    shape = (24, 128)
    row, lane = rows_of(shape), lanes_of(shape)
    nx, ny, nz = counts
    base_x = lax.axis_index("gx") * 8 - HALO
    base_y = lax.axis_index("gy") * 16
    base_z = lax.axis_index("gz") * 128

    def folded(place, limit):
        def inside(p):
            return jnp.where((p >= 0) & (p < limit), 1.0, 0.0).astype(f32)

        return [inside(place)] + [inside(place - k) + inside(place + k) for k in range(1, RAD + 1)]

    along_y = folded(jnp.where(row < 16 + HALO, row, row - 24) + base_y, ny * 16)

    def partial(along_z):
        table = []
        for a in range(RAD + 1):
            total = jnp.zeros(shape, f32)
            for b in range(RAD + 1):
                line = None
                for k in range(RAD + 1):
                    w = cone(a, b, k)
                    if w > 0:
                        line = w * along_z[k] if line is None else line + w * along_z[k]
                if line is not None:
                    total = total + along_y[b] * line
            table.append(total)
        return table

    def finish(total, along_x, along_z):
        inner = along_x[0] * along_y[0] * along_z[0] > 0
        return jnp.where(inner, 1.0 / jnp.where(inner, total, 1.0), 0.0)

    along_z = folded(lane + base_z, nz * 128)
    table = partial(along_z)
    for X in range(16):
        along_x = folded(jnp.full(shape, X, jnp.int32) + base_x, nx * 8)
        total = sum(along_x[a] * table[a] for a in range(RAD + 1))
        main[X] = finish(total, along_x, along_z)
    place = lane % 8
    along_x = folded(lane // 8 + base_x, nx * 8)
    for s, shift in enumerate((-4, 124)):
        along_z = folded(place + (base_z + shift), nz * 128)
        table = partial(along_z)
        total = sum(along_x[a] * table[a] for a in range(RAD + 1))
        side[s] = finish(total, along_x, along_z)


def apply_operator(nz, ext, got0, got1, res, lab, image, inverse, sums, around, shifts):
    lane = lanes_of((24, 128))
    fields = (0, 1, 2, 6)
    iz = lax.axis_index("gz")
    lows = lane % 8 < 4
    from_zero = (lane // 4) % 2 == (iz + 1) % 2
    keep = jnp.where(lows, (iz > 0).astype(f32), (iz < nz - 1).astype(f32))
    for f in range(7):
        around[f] = jnp.where(from_zero, got0[f], got1[f]) * keep
    parts = [jnp.zeros((16, 128), f32) for _ in range(4)]
    for plane_at in range(10):
        X = plane_at + 3
        for g, f in enumerate(fields):
            value = ext[f, X]
            near = roll(around[f], 124 - 8 * X, 1)
            if g == 3:
                stiff = stiff_floor + (1.0 - stiff_floor) * value * value * value
                value = jnp.where(value > 0, stiff, 0.0)
                stiff = stiff_floor + (1.0 - stiff_floor) * near * near * near
                near = jnp.where(near > 0, stiff, 0.0)
            up = roll(jnp.where(lane == 0, near, value), -1, 1)
            down = roll(jnp.where(lane == 127, near, value), 1, 1)
            for z, plane in enumerate((down, value, up)):
                for y in range(3):
                    shifts[g, y, z, plane_at] = roll(plane, 1 - y, 0)[0:16]
        x = plane_at - 2
        if x < 0:
            continue
        n = x + 1
        mid = [shifts[g, 1, 1, n] for g in range(4)]
        classes = {1: [None] * 3, 2: [None] * 3, 3: [None] * 3}
        faces = [None] * 3
        edges = [None] * 3
        corners = None

        def add(old, new):
            return new if old is None else old + new

        for o in neighbour_offsets:
            near = [shifts[g, 1 + o[1], 1 + o[2], n + o[0]] for g in range(4)]
            norm = sum(abs(c) for c in o)
            weight = mid[3] + near[3]
            d = [mid[c] - near[c] for c in range(3)]
            acc = classes[norm]
            if norm == 1:
                c0 = [c for c in range(3) if o[c] != 0][0]
                faces[c0] = add(faces[c0], near[3])
                for c in range(3):
                    acc[c] = add(acc[c], weight * (d[c] + d[c] if c == c0 else d[c]))
            else:
                along = None
                for c in range(3):
                    if o[c] != 0:
                        term = d[c]
                        if along is None:
                            along, sign = term, o[c]
                        else:
                            along = along + term if o[c] == sign else along - term
                along = along * (1.0 / norm)
                for c in range(3):
                    if o[c] == 0:
                        pulled = d[c]
                    elif o[c] == sign:
                        pulled = d[c] + along
                    else:
                        pulled = d[c] - along
                    acc[c] = add(acc[c], weight * pulled)
                if norm == 2:
                    c0 = [c for c in range(3) if o[c] == 0][0]
                    edges[c0] = add(edges[c0], near[3])
                else:
                    corners = add(corners, near[3])
        s0 = mid[3]
        all_faces = faces[0] + faces[1] + faces[2]
        all_edges = edges[0] + edges[1] + edges[2]
        common = (all_faces + 6.0 * s0) + 0.75 * (all_edges + 12.0 * s0) + (4.0 / 9.0) * (corners + 8.0 * s0)
        label = lab[x]
        for c in range(3):
            diag = 0.5 * (common + (faces[c] + 2.0 * s0) - 0.25 * (edges[c] + 4.0 * s0))
            fixed = (label == 1) if c < 2 else (label >= 1)
            total = 0.5 * classes[1][c] + 0.25 * classes[2][c] + (1.0 / 6.0) * classes[3][c]
            total = jnp.where(fixed, 0.0, total)
            inv = 1.0 / jnp.where(fixed, 1.0, diag)
            r = res[c, x]
            zeta = r * inv
            scaled = total * inv
            image[c, x] = total
            inverse[c, x] = inv
            parts[0] = parts[0] + r * zeta
            parts[1] = parts[1] + mid[c] * total
            parts[2] = parts[2] + r * scaled
            parts[3] = parts[3] + total * scaled
    sub = rows_of((8, 128))
    out = jnp.zeros((8, 128), f32)
    for k in range(4):
        part = parts[k][0:8] + parts[k][8:16]
        out = jnp.where(sub == k, jnp.sum(part, axis=0, keepdims=True), out)
    sums[...] = out


def quadratic(d, o):
    norm = sum(abs(c) for c in o)
    square = d[0] * d[0] + d[1] * d[1] + d[2] * d[2]
    along, sign = None, 1
    for c in range(3):
        if o[c] != 0:
            if along is None:
                along, sign = d[c], o[c]
            else:
                along = along + d[c] if o[c] == sign else along - d[c]
    if norm == 1:
        return square + along * along
    return (1.0 / norm) * square + (1.0 / (norm * norm)) * (along * along)


pairs = [((1, 0, 0), 0, 0, 0, 0)]
pairs += [((a, 1, 0), 0, 0, 2, 2) for a in (-1, 0, 1)]
pairs += [((a, 0, 1), 0, 0, 1, 1) for a in (-1, 0, 1)]
pairs += [((a, 1, 1), 0, 0, 3, 3) for a in (-1, 0, 1)]
pairs += [((a, -1, 1), 2, 2, 1, 1) for a in (-1, 0, 1)]
distances = sorted({a * a + b * b for a in range(RAD + 1) for b in range(RAD + 1) if cone(a, b, 0) > 0})
energy_scale = -penalty * (1.0 - stiff_floor) * 0.5


def plus(old, new):
    return new if old is None else old + new


def finish_step(
    ext, ends, around, total, image, inverse, res, dire, hinv, hside,
    new_sol_any, new_res_any, new_dir_any, sens_any, us, lines, new_sol, new_res, new_dir, sens, sems,
):
    lane = lanes_of((24, 128))
    lows = lane % 8 < 4
    copies = [
        pltpu.make_async_copy(source, target, sems.at[i])
        for i, (source, target) in enumerate(
            ((new_res, new_res_any), (new_dir, new_dir_any), (new_sol, new_sol_any), (sens, sens_any))
        )
    ]
    tot = jnp.sum(total[...], axis=1, keepdims=True)
    rz, pq, s2, s3 = tot[0:1], tot[1:2], tot[2:3], tot[3:4]
    alpha = rz / pq
    beta = (rz + alpha * (alpha * s3 - 2.0 * s2)) / rz

    for x in range(8):
        for c in range(3):
            r = res[c, x] - alpha * image[c, x]
            new_res[c, x] = r
            new_dir[c, x] = r * inverse[c, x] + beta * dire[c, x]
    copies[0].start()
    copies[1].start()

    halos, lefts, rights = [], [], []
    for c in range(3):
        halo_u = around[3 + c] + alpha * around[c]
        own_u = ends[3 + c] + alpha * ends[c]
        halos.append(halo_u)
        lefts.append(jnp.where(lows, halo_u, own_u))
        rights.append(jnp.where(lows, own_u, halo_u))
    sides, side_low = [], None
    den_left = jnp.where(lows, around[6], ends[6])
    den_right = jnp.where(lows, ends[6], around[6])
    for s, (u, den) in enumerate(((lefts, den_left), (rights, den_right))):
        up = [roll(v, -1, 1) for v in u]
        moved = [u, up, [roll(v, -1, 0) for v in u], [roll(v, -1, 0) for v in up]]
        far = {}
        acc = {}
        for o, field0, frame0, field1, frame1 in pairs:
            key = (field1, o[0])
            if key not in far:
                far[key] = [roll(v, -8 * o[0], 1) for v in moved[field1]]
            g = quadratic([moved[field0][c] - far[key][c] for c in range(3)], o)
            acc[frame0, 0] = plus(acc.get((frame0, 0)), g)
            acc[frame1, o[0]] = plus(acc.get((frame1, o[0])), g)
        frames = []
        for frame in range(4):
            value = None
            for a in (-1, 0, 1):
                if (frame, a) in acc:
                    value = plus(value, roll(acc[frame, a], 8 * a, 1))
            frames.append(value)
        up = frames[1] + roll(frames[3], 1, 0)
        if s == 0:
            side_low = up
        energy = frames[0] + roll(frames[2], 1, 0) + roll(up, 1, 1)
        sides.append(energy_scale * (den * den) * energy * hside[s])
    ends_scaled = jnp.where(lows, sides[0], sides[1])

    def iterate(X):
        for c in range(3):
            u = ext[3 + c, X] + alpha * ext[c, X]
            if 4 <= X < 12:
                new_sol[c, X - 4] = u[0:16]
            near = roll(halos[c], 124 - 8 * X, 1)
            up = roll(jnp.where(lane == 0, near, u), -1, 1)
            us[0, c, X] = u
            us[1, c, X] = up
            us[2, c, X] = roll(u, -1, 0)
            us[3, c, X] = roll(up, -1, 0)
        if X == 11:
            copies[2].start()

    acc = [[None] * 4 for _ in range(16)]

    def pair_up(X):
        for o, field0, frame0, field1, frame1 in pairs:
            to = X + o[0]
            if not 0 <= to < 16 or not (1 <= X < 15 or 1 <= to < 15):
                continue
            g = quadratic([us[field0, c, X] - us[field1, c, to] for c in range(3)], o)
            if 1 <= X < 15:
                acc[X][frame0] = plus(acc[X][frame0], g)
            if 1 <= to < 15:
                acc[to][frame1] = plus(acc[to][frame1], g)

    def filter_lines(X):
        frames = acc[X]
        up = frames[1] + roll(frames[3], 1, 0)
        below = roll(side_low, 127 - (8 * X + 3), 1)
        up = roll(jnp.where(lane == 127, below, up), 1, 1)
        den = ext[6, X]
        energy = frames[0] + roll(frames[2], 1, 0) + up
        s = energy_scale * (den * den) * energy * hinv[X]
        near = roll(ends_scaled, 124 - 8 * X, 1)
        fold = [s]
        for k in range(1, RAD + 1):
            above = roll(jnp.where(lane < k, near, s), -k, 1)
            under = roll(jnp.where(lane >= 128 - k, near, s), k, 1)
            fold.append(above + under)
        for i, d in enumerate(distances):
            line = None
            for k in range(RAD + 1):
                w = max(0.0, RAD + 0.5 - math.sqrt(d + k * k))
                if w > 0:
                    line = plus(line, w * fold[k])
            lines[X, i] = line

    def filter_rows(x):
        value = None
        for b in range(RAD + 1):
            row = None
            for a in range(-RAD, RAD + 1):
                if cone(a, b, 0) > 0:
                    row = plus(row, lines[x + HALO + a, distances.index(a * a + b * b)])
            value = row if b == 0 else value + roll(row, b, 0) + roll(row, -b, 0)
        sens[x] = value[0:16]

    for X in range(16 + 1):
        if X < 16:
            iterate(X)
        if X >= 1:
            pair_up(X - 1)
        if X >= 3:
            filter_lines(X - 2)
        if X - 2 - 2 * RAD - 1 >= 0:
            filter_rows(X - 2 - 2 * RAD - 1)
    copies[3].start()
    for copy in copies:
        copy.wait()


def partner(place, turn, count):
    other = (place ^ 1) if turn == 0 else ((place + 1) ^ 1) - 1
    return other if 0 <= other < count else None


def swap_pairs(counts, turns):
    pairs = []
    for flat in range(math.prod(counts)):
        rest, place = flat, []
        for count in reversed(counts):
            place.insert(0, rest % count)
            rest //= count
        to = [p if t is None else partner(p, t, c) for p, t, c in zip(place, turns, counts)]
        if None in to:
            to = place
        index = 0
        for p, count in zip(to, counts):
            index = index * count + p
        pairs.append((flat, index))
    return pairs


def prime_factors(count):
    factors, p = [], 2
    while count > 1:
        while count % p == 0:
            factors.append(p)
            count //= p
        p += 1
    return factors


def total_over(value, mesh_shape):
    count = math.prod(mesh_shape[a] for a in AXES)
    copies = jnp.broadcast_to(value, (count,) + value.shape)
    return jnp.sum(lax.all_to_all(copies, AXES, 0, 0), axis=0)


def per_device(mesh_shape, solution, residual, direction, density, labels):
    nx, ny, nz = (mesh_shape[a] for a in AXES)
    half, full, corner = (7, 4, 16, 128), (7, 4, 8, 128), (7, 2, 8, 128)
    rounds_y = 1 if ny == 2 else 2
    field, flat = (3, 8, 16, 128), (8, 16, 128)
    packed = call(
        functools.partial(pack_faces, rounds_y),
        [half, half] + [full, corner, corner] * rounds_y,
        solution, direction, density, labels,
        far=range(4),
        scratch=[
            pltpu.VMEM(field, f32), pltpu.VMEM(field, f32), pltpu.VMEM(flat, f32),
            pltpu.VMEM(flat, jnp.int32), pltpu.SemaphoreType.DMA((4,)),
        ],
    )
    halves = packed[:2]
    plane = ("gx", "gy")
    got = [lax.ppermute(halves[r], plane, swap_pairs((nx, ny), (r, None))) for r in (0, 1)]
    strips = []
    for s in range(rounds_y):
        for array, turn in zip(packed[2 + 3 * s : 5 + 3 * s], (None, 0, 1)):
            strips.append(lax.ppermute(array, plane, swap_pairs((nx, ny), (turn, s))))
    hinv, hside = call(functools.partial(inverse_sums, (nx, ny, nz)), [(16, 24, 128), (2, 24, 128)])
    ext, ends = call(
        functools.partial(extend, (nx, ny, nz)),
        [(7, 16, 24, 128), (7, 24, 128)],
        *halves, *got, *strips,
    )
    ends_got = [lax.ppermute(ends, "gz", swap_pairs((nz,), (r,))) for r in (0, 1)]
    image, inverse, sums, around = call(
        functools.partial(apply_operator, nz),
        [field, field, (8, 128), (7, 24, 128)],
        ext, *ends_got, residual, labels,
        scratch=[pltpu.VMEM((4, 3, 3, 10, 16, 128), f32)],
    )
    total = total_over(sums, mesh_shape)
    return tuple(
        call(
            finish_step,
            [field, field, field, flat],
            ext, ends, around, total, image, inverse, residual, direction, hinv, hside,
            scratch=[
                pltpu.VMEM((4, 3, 16, 24, 128), f32), pltpu.VMEM((16, len(distances), 24, 128), f32),
                pltpu.VMEM(field, f32), pltpu.VMEM(field, f32), pltpu.VMEM(field, f32),
                pltpu.VMEM(flat, f32), pltpu.SemaphoreType.DMA((4,)),
            ],
            far_out=True,
        )
    )


def solution(mesh):
    wide, flat = P(None, "gx", "gy", "gz"), P("gx", "gy", "gz")
    return jax.shard_map(
        functools.partial(per_device, dict(mesh.shape)),
        mesh=mesh,
        in_specs=(wide, wide, wide, flat, flat),
        out_specs=(wide, wide, wide, flat),
        check_vma=False,
    )
```

```python
import functools
import math

import jax
import jax.numpy as jnp
from jax import lax
from jax.experimental import pallas as pl
from jax.experimental.pallas import tpu as pltpu
from jax.sharding import PartitionSpec as P

RAD = 3
HALO = RAD + 1
stiff_floor = 0.001
penalty = 3.0
f32 = jnp.float32
neighbour_offsets = [
    (off_x, off_y, off_z)
    for off_x in (-1, 0, 1)
    for off_y in (-1, 0, 1)
    for off_z in (-1, 0, 1)
    if (off_x, off_y, off_z) != (0, 0, 0)
]
AXES = ("gx", "gy", "gz")


def cone(a, b, k):
    return max(0.0, RAD + 0.5 - math.sqrt(a * a + b * b + k * k))


def lanes_of(shape):
    return lax.broadcasted_iota(jnp.int32, shape, len(shape) - 1)


def rows_of(shape):
    return lax.broadcasted_iota(jnp.int32, shape, len(shape) - 2)


def roll(value, amount, axis):
    size = value.shape[axis]
    amount = amount % size
    return value if amount == 0 else pltpu.roll(value, amount, axis)


def call(body, outs, *args, scratch=(), cost=20000, far=(), far_out=False):
    args = [
        pltpu.with_memory_space_constraint(a, pltpu.HBM) if i in far else a for i, a in enumerate(args)
    ]
    return pl.pallas_call(
        body,
        out_shape=[jax.ShapeDtypeStruct(shape, f32) for shape in outs],
        in_specs=[
            pl.BlockSpec(memory_space=pl.ANY if i in far else pltpu.VMEM) for i in range(len(args))
        ],
        out_specs=[pl.BlockSpec(memory_space=pl.ANY if far_out else pltpu.VMEM)] * len(outs),
        scratch_shapes=list(scratch),
        compiler_params=pltpu.CompilerParams(vmem_limit_bytes=24 * 1024 * 1024),
        cost_estimate=pl.CostEstimate(flops=cost * 1000, bytes_accessed=cost, transcendentals=0),
    )(*args)


def is_even(axis):
    return lax.axis_index(axis) % 2 == 0


def pack_faces(rounds_y, sol_any, dire_any, den_any, lab_any, *refs):
    halves, packs = refs[:2], refs[2 : 2 + 3 * rounds_y]
    sol, dire, den, lab, sems = refs[2 + 3 * rounds_y :]
    copies = [
        pltpu.make_async_copy(source, target, sems.at[i])
        for i, (source, target) in enumerate(
            ((dire_any, dire), (sol_any, sol), (den_any, den), (lab_any, lab))
        )
    ]
    for copy in copies:
        copy.start()
    sub = rows_of((8, 128))
    even_x, even_y = is_even("gx"), is_even("gy")
    for copy in copies:
        copy.wait()

    def masked(x):
        label = lab[x]
        keep = jnp.where(label == 1, 0.0, 1.0).astype(f32)
        keep_last = jnp.where(label >= 1, 0.0, 1.0).astype(f32)
        fields = [dire[0, x] * keep, dire[1, x] * keep, dire[2, x] * keep_last]
        return fields + [sol[0, x], sol[1, x], sol[2, x], den[x]]

    for t in range(2):
        planes = {x: masked(x) for x in (2 * t, 2 * t + 1, 2 * t + 4, 2 * t + 5)}
        for f in range(7):
            for i in (2 * t, 2 * t + 1):
                low, high = planes[i][f], planes[i + 4][f]
                halves[0][f, i] = jnp.where(even_x, high, low)
                halves[1][f, i] = jnp.where(even_x, low, high)
            tiles = []
            for i in (2 * t, 2 * t + 4):
                p, q = planes[i][f], planes[i + 1][f]
                low = jnp.where(sub < 4, p[0:8], roll(q[0:8], 4, 0))
                high = jnp.where(sub < 4, roll(p[8:16], 4, 0), q[8:16])
                tiles.append((jnp.where(even_y, high, low), jnp.where(even_y, low, high)))
            for s in range(rounds_y):
                rows, corner0, corner1 = packs[3 * s : 3 * s + 3]
                low, high = tiles[0][s], tiles[1][s]
                rows[f, t] = low
                rows[f, t + 2] = high
                corner0[f, t] = jnp.where(even_x, high, low)
                corner1[f, t] = jnp.where(even_x, low, high)


def extend(counts, half0, half1, got0, got1, *refs):
    nx, ny, nz = counts
    sides, (ext, ends) = refs[:-2], refs[-2:]
    sub = rows_of((8, 128))
    lane = lanes_of((24, 128))
    ix, iy = lax.axis_index("gx"), lax.axis_index("gy")
    even_y = is_even("gy")
    x_ok = ((ix > 0).astype(f32), (ix < nx - 1).astype(f32))
    y_ok = ((iy > 0).astype(f32), (iy < ny - 1).astype(f32))

    def body(blocks, order):
        def strip(which, f, t):
            tiles = []
            for s in range(len(sides) // 3):
                rows, corner0, corner1 = sides[3 * s : 3 * s + 3]
                ref = rows if which is None else (corner0, corner1)[order[which]]
                tiles.append(ref[f, t])
            keep = 1.0 if which is None else x_ok[which]
            other = tiles[-1]
            low = jnp.where(even_y, other, tiles[0]) * (y_ok[0] * keep)
            high = jnp.where(even_y, tiles[0], other) * (y_ok[1] * keep)
            return low, high

        for f in range(7):
            packed = None
            for X in range(16):
                own = blocks[X // 4][f, X % 4]
                which = None
                if X < 4:
                    which, t = 0, X // 2
                elif X >= 12:
                    which, t = 1, (X - 12) // 2
                else:
                    t = (X - 4) // 2
                if which is not None:
                    own = own * x_ok[which]
                low, high = strip(which, f, t)
                if X % 2 == 0:
                    low = roll(low, 4, 0)
                else:
                    high = roll(high, 4, 0)
                plane = jnp.concatenate([own, jnp.where(sub < 4, high, low)], axis=0)
                ext[f, X] = plane
                turned = roll(plane, 8 * X + 4, 1)
                packed = turned if X == 0 else jnp.where(lane >= 8 * X, turned, packed)
            ends[f] = packed

    @pl.when(ix % 2 == 0)
    def _():
        body((got1, half1, half0, got0), (1, 0))

    @pl.when(ix % 2 == 1)
    def _():
        body((got0, half0, half1, got1), (0, 1))


def inverse_sums(counts, main, side):
    shape = (24, 128)
    row, lane = rows_of(shape), lanes_of(shape)
    nx, ny, nz = counts
    base_x = lax.axis_index("gx") * 8 - HALO
    base_y = lax.axis_index("gy") * 16
    base_z = lax.axis_index("gz") * 128

    def folded(place, limit):
        def inside(p):
            return jnp.where((p >= 0) & (p < limit), 1.0, 0.0).astype(f32)

        return [inside(place)] + [inside(place - k) + inside(place + k) for k in range(1, RAD + 1)]

    along_y = folded(jnp.where(row < 16 + HALO, row, row - 24) + base_y, ny * 16)

    def partial(along_z):
        table = []
        for a in range(RAD + 1):
            total = jnp.zeros(shape, f32)
            for b in range(RAD + 1):
                line = None
                for k in range(RAD + 1):
                    w = cone(a, b, k)
                    if w > 0:
                        line = w * along_z[k] if line is None else line + w * along_z[k]
                if line is not None:
                    total = total + along_y[b] * line
            table.append(total)
        return table

    def finish(total, along_x, along_z):
        inner = along_x[0] * along_y[0] * along_z[0] > 0
        return jnp.where(inner, 1.0 / jnp.where(inner, total, 1.0), 0.0)

    along_z = folded(lane + base_z, nz * 128)
    table = partial(along_z)
    for X in range(16):
        along_x = folded(jnp.full(shape, X, jnp.int32) + base_x, nx * 8)
        total = sum(along_x[a] * table[a] for a in range(RAD + 1))
        main[X] = finish(total, along_x, along_z)
    place = lane % 8
    along_x = folded(lane // 8 + base_x, nx * 8)
    for s, shift in enumerate((-4, 124)):
        along_z = folded(place + (base_z + shift), nz * 128)
        table = partial(along_z)
        total = sum(along_x[a] * table[a] for a in range(RAD + 1))
        side[s] = finish(total, along_x, along_z)


def apply_operator(nz, ext, got0, got1, res, lab, image, inverse, sums, around, shifts):
    lane = lanes_of((24, 128))
    fields = (0, 1, 2, 6)
    iz = lax.axis_index("gz")
    lows = lane % 8 < 4
    from_zero = (lane // 4) % 2 == (iz + 1) % 2
    keep = jnp.where(lows, (iz > 0).astype(f32), (iz < nz - 1).astype(f32))
    for f in range(7):
        around[f] = jnp.where(from_zero, got0[f], got1[f]) * keep
    parts = [jnp.zeros((16, 128), f32) for _ in range(4)]
    for plane_at in range(10):
        X = plane_at + 3
        for g, f in enumerate(fields):
            value = ext[f, X]
            near = roll(around[f], 124 - 8 * X, 1)
            if g == 3:
                stiff = stiff_floor + (1.0 - stiff_floor) * value * value * value
                value = jnp.where(value > 0, stiff, 0.0)
                stiff = stiff_floor + (1.0 - stiff_floor) * near * near * near
                near = jnp.where(near > 0, stiff, 0.0)
            up = roll(jnp.where(lane == 0, near, value), -1, 1)
            down = roll(jnp.where(lane == 127, near, value), 1, 1)
            for z, plane in enumerate((down, value, up)):
                for y in range(3):
                    shifts[g, y, z, plane_at] = roll(plane, 1 - y, 0)[0:16]
        x = plane_at - 2
        if x < 0:
            continue
        n = x + 1
        mid = [shifts[g, 1, 1, n] for g in range(4)]
        classes = {1: [None] * 3, 2: [None] * 3, 3: [None] * 3}
        faces = [None] * 3
        edges = [None] * 3
        corners = None

        def add(old, new):
            return new if old is None else old + new

        for o in neighbour_offsets:
            near = [shifts[g, 1 + o[1], 1 + o[2], n + o[0]] for g in range(4)]
            norm = sum(abs(c) for c in o)
            weight = mid[3] + near[3]
            d = [mid[c] - near[c] for c in range(3)]
            acc = classes[norm]
            if norm == 1:
                c0 = [c for c in range(3) if o[c] != 0][0]
                faces[c0] = add(faces[c0], near[3])
                for c in range(3):
                    acc[c] = add(acc[c], weight * (d[c] + d[c] if c == c0 else d[c]))
            else:
                along = None
                for c in range(3):
                    if o[c] != 0:
                        term = d[c]
                        if along is None:
                            along, sign = term, o[c]
                        else:
                            along = along + term if o[c] == sign else along - term
                along = along * (1.0 / norm)
                for c in range(3):
                    if o[c] == 0:
                        pulled = d[c]
                    elif o[c] == sign:
                        pulled = d[c] + along
                    else:
                        pulled = d[c] - along
                    acc[c] = add(acc[c], weight * pulled)
                if norm == 2:
                    c0 = [c for c in range(3) if o[c] == 0][0]
                    edges[c0] = add(edges[c0], near[3])
                else:
                    corners = add(corners, near[3])
        s0 = mid[3]
        all_faces = faces[0] + faces[1] + faces[2]
        all_edges = edges[0] + edges[1] + edges[2]
        common = (all_faces + 6.0 * s0) + 0.75 * (all_edges + 12.0 * s0) + (4.0 / 9.0) * (corners + 8.0 * s0)
        label = lab[x]
        for c in range(3):
            diag = 0.5 * (common + (faces[c] + 2.0 * s0) - 0.25 * (edges[c] + 4.0 * s0))
            fixed = (label == 1) if c < 2 else (label >= 1)
            total = 0.5 * classes[1][c] + 0.25 * classes[2][c] + (1.0 / 6.0) * classes[3][c]
            total = jnp.where(fixed, 0.0, total)
            inv = 1.0 / jnp.where(fixed, 1.0, diag)
            r = res[c, x]
            zeta = r * inv
            scaled = total * inv
            image[c, x] = total
            inverse[c, x] = inv
            parts[0] = parts[0] + r * zeta
            parts[1] = parts[1] + mid[c] * total
            parts[2] = parts[2] + r * scaled
            parts[3] = parts[3] + total * scaled
    row = jnp.zeros((1, 128), f32)
    for k in range(4):
        part = jnp.sum(parts[k], axis=0, keepdims=True)
        part = jnp.sum(part, axis=1, keepdims=True)
        row = jnp.where(lanes_of((1, 128)) == k, part, row)
    sums[...] = jnp.broadcast_to(row[None], sums.shape)


def quadratic(d, o):
    norm = sum(abs(c) for c in o)
    square = d[0] * d[0] + d[1] * d[1] + d[2] * d[2]
    along, sign = None, 1
    for c in range(3):
        if o[c] != 0:
            if along is None:
                along, sign = d[c], o[c]
            else:
                along = along + d[c] if o[c] == sign else along - d[c]
    if norm == 1:
        return square + along * along
    return (1.0 / norm) * square + (1.0 / (norm * norm)) * (along * along)


pairs = [((1, 0, 0), 0, 0, 0, 0)]
pairs += [((a, 1, 0), 0, 0, 2, 2) for a in (-1, 0, 1)]
pairs += [((a, 0, 1), 0, 0, 1, 1) for a in (-1, 0, 1)]
pairs += [((a, 1, 1), 0, 0, 3, 3) for a in (-1, 0, 1)]
pairs += [((a, -1, 1), 2, 2, 1, 1) for a in (-1, 0, 1)]
energy_scale = -penalty * (1.0 - stiff_floor) * 0.5


def plus(old, new):
    return new if old is None else old + new


def finish_step(
    ext, ends, around, total, image, inverse, res, dire, hinv, hside,
    new_sol_any, new_res_any, new_dir_any, sens_any, us, lines, new_sol, new_res, new_dir, sens, sems,
):
    lane = lanes_of((24, 128))
    lows = lane % 8 < 4
    copies = [
        pltpu.make_async_copy(source, target, sems.at[i])
        for i, (source, target) in enumerate(
            ((new_res, new_res_any), (new_dir, new_dir_any), (new_sol, new_sol_any), (sens, sens_any))
        )
    ]
    tot = jnp.sum(total[...], axis=0)
    rz, pq, s2, s3 = (tot[:, k : k + 1] for k in range(4))
    alpha = rz / pq
    beta = (rz + alpha * (alpha * s3 - 2.0 * s2)) / rz

    for x in range(8):
        for c in range(3):
            r = res[c, x] - alpha * image[c, x]
            new_res[c, x] = r
            new_dir[c, x] = r * inverse[c, x] + beta * dire[c, x]
    copies[0].start()
    copies[1].start()

    halos, lefts, rights = [], [], []
    for c in range(3):
        halo_u = around[3 + c] + alpha * around[c]
        own_u = ends[3 + c] + alpha * ends[c]
        halos.append(halo_u)
        lefts.append(jnp.where(lows, halo_u, own_u))
        rights.append(jnp.where(lows, own_u, halo_u))
    sides, side_low = [], None
    den_left = jnp.where(lows, around[6], ends[6])
    den_right = jnp.where(lows, ends[6], around[6])
    for s, (u, den) in enumerate(((lefts, den_left), (rights, den_right))):
        up = [roll(v, -1, 1) for v in u]
        moved = [u, up, [roll(v, -1, 0) for v in u], [roll(v, -1, 0) for v in up]]
        far = {}
        acc = {}
        for o, field0, frame0, field1, frame1 in pairs:
            key = (field1, o[0])
            if key not in far:
                far[key] = [roll(v, -8 * o[0], 1) for v in moved[field1]]
            g = quadratic([moved[field0][c] - far[key][c] for c in range(3)], o)
            acc[frame0, 0] = plus(acc.get((frame0, 0)), g)
            acc[frame1, o[0]] = plus(acc.get((frame1, o[0])), g)
        frames = []
        for frame in range(4):
            value = None
            for a in (-1, 0, 1):
                if (frame, a) in acc:
                    value = plus(value, roll(acc[frame, a], 8 * a, 1))
            frames.append(value)
        up = frames[1] + roll(frames[3], 1, 0)
        if s == 0:
            side_low = up
        energy = frames[0] + roll(frames[2], 1, 0) + roll(up, 1, 1)
        sides.append(energy_scale * (den * den) * energy * hside[s])
    ends_scaled = jnp.where(lows, sides[0], sides[1])

    def iterate(X):
        for c in range(3):
            u = ext[3 + c, X] + alpha * ext[c, X]
            if 4 <= X < 12:
                new_sol[c, X - 4] = u[0:16]
            near = roll(halos[c], 124 - 8 * X, 1)
            up = roll(jnp.where(lane == 0, near, u), -1, 1)
            us[0, c, X] = u
            us[1, c, X] = up
            us[2, c, X] = roll(u, -1, 0)
            us[3, c, X] = roll(up, -1, 0)
        if X == 11:
            copies[2].start()

    acc = [[None] * 4 for _ in range(16)]

    def pair_up(X):
        for o, field0, frame0, field1, frame1 in pairs:
            to = X + o[0]
            if not 0 <= to < 16 or not (1 <= X < 15 or 1 <= to < 15):
                continue
            g = quadratic([us[field0, c, X] - us[field1, c, to] for c in range(3)], o)
            if 1 <= X < 15:
                acc[X][frame0] = plus(acc[X][frame0], g)
            if 1 <= to < 15:
                acc[to][frame1] = plus(acc[to][frame1], g)

    def filter_lines(X):
        frames = acc[X]
        up = frames[1] + roll(frames[3], 1, 0)
        below = roll(side_low, 127 - (8 * X + 3), 1)
        up = roll(jnp.where(lane == 127, below, up), 1, 1)
        den = ext[6, X]
        energy = frames[0] + roll(frames[2], 1, 0) + up
        s = energy_scale * (den * den) * energy * hinv[X]
        near = roll(ends_scaled, 124 - 8 * X, 1)
        fold = [s]
        for k in range(1, RAD + 1):
            above = roll(jnp.where(lane < k, near, s), -k, 1)
            under = roll(jnp.where(lane >= 128 - k, near, s), k, 1)
            fold.append(above + under)
        for k in range(RAD + 1):
            lines[X, k] = fold[k]

    def filter_rows(x):
        groups = {}
        for a in range(RAD + 1):
            for k in range(RAD + 1):
                if cone(a, 0, k) > 0:
                    both = lines[x + HALO + a, k]
                    if a > 0:
                        both = both + lines[x + HALO - a, k]
                    groups[a * a + k * k] = plus(groups.get(a * a + k * k), both)
        value = None
        for b in range(RAD + 1):
            row = None
            for d, group in groups.items():
                w = RAD + 0.5 - math.sqrt(d + b * b)
                if w > 0:
                    row = plus(row, w * group)
            value = row if b == 0 else value + roll(row, b, 0) + roll(row, -b, 0)
        sens[x] = value[0:16]

    for X in range(16 + 1):
        if X < 16:
            iterate(X)
        if X >= 1:
            pair_up(X - 1)
        if X >= 3:
            filter_lines(X - 2)
        if X - 2 - 2 * RAD - 1 >= 0:
            filter_rows(X - 2 - 2 * RAD - 1)
    copies[3].start()
    for copy in copies:
        copy.wait()


def partner(place, turn, count):
    other = (place ^ 1) if turn == 0 else ((place + 1) ^ 1) - 1
    return other if 0 <= other < count else None


def swap_pairs(counts, turns):
    pairs = []
    for flat in range(math.prod(counts)):
        rest, place = flat, []
        for count in reversed(counts):
            place.insert(0, rest % count)
            rest //= count
        to = [p if t is None else partner(p, t, c) for p, t, c in zip(place, turns, counts)]
        if None in to:
            continue
        index = 0
        for p, count in zip(to, counts):
            index = index * count + p
        pairs.append((flat, index))
    return pairs


def per_device(mesh_shape, solution, residual, direction, density, labels):
    nx, ny, nz = (mesh_shape[a] for a in AXES)
    half, full, corner = (7, 4, 16, 128), (7, 4, 8, 128), (7, 2, 8, 128)
    rounds_y = 1 if ny == 2 else 2
    field, flat = (3, 8, 16, 128), (8, 16, 128)
    packed = call(
        functools.partial(pack_faces, rounds_y),
        [half, half] + [full, corner, corner] * rounds_y,
        solution, direction, density, labels,
        far=range(4),
        scratch=[
            pltpu.VMEM(field, f32), pltpu.VMEM(field, f32), pltpu.VMEM(flat, f32),
            pltpu.VMEM(flat, jnp.int32), pltpu.SemaphoreType.DMA((4,)),
        ],
    )
    halves = packed[:2]
    plane = ("gx", "gy")
    got = [lax.ppermute(halves[r], plane, swap_pairs((nx, ny), (r, None))) for r in (0, 1)]
    strips = []
    for s in range(rounds_y):
        for array, turn in zip(packed[2 + 3 * s : 5 + 3 * s], (None, 0, 1)):
            strips.append(lax.ppermute(array, plane, swap_pairs((nx, ny), (turn, s))))
    hinv, hside = call(functools.partial(inverse_sums, (nx, ny, nz)), [(16, 24, 128), (2, 24, 128)])
    ext, ends = call(
        functools.partial(extend, (nx, ny, nz)),
        [(7, 16, 24, 128), (7, 24, 128)],
        *halves, *got, *strips,
    )
    ends_got = [lax.ppermute(ends, "gz", swap_pairs((nz,), (r,))) for r in (0, 1)]
    image, inverse, sums, around = call(
        functools.partial(apply_operator, nz),
        [field, field, (nx * ny * nz, 1, 128), (7, 24, 128)],
        ext, *ends_got, residual, labels,
        scratch=[pltpu.VMEM((4, 3, 3, 10, 16, 128), f32)],
    )
    total = lax.all_to_all(sums, AXES, 0, 0)
    return tuple(
        call(
            finish_step,
            [field, field, field, flat],
            ext, ends, around, total, image, inverse, residual, direction, hinv, hside,
            scratch=[
                pltpu.VMEM((4, 3, 16, 24, 128), f32), pltpu.VMEM((16, RAD + 1, 24, 128), f32),
                pltpu.VMEM(field, f32), pltpu.VMEM(field, f32), pltpu.VMEM(field, f32),
                pltpu.VMEM(flat, f32), pltpu.SemaphoreType.DMA((4,)),
            ],
            far_out=True,
        )
    )


def solution(mesh):
    wide, flat = P(None, "gx", "gy", "gz"), P("gx", "gy", "gz")
    return jax.shard_map(
        functools.partial(per_device, dict(mesh.shape)),
        mesh=mesh,
        in_specs=(wide, wide, wide, flat, flat),
        out_specs=(wide, wide, wide, flat),
        check_vma=False,
    )
```

```python
import functools
import math

import jax
import jax.numpy as jnp
from jax import lax
from jax.experimental import pallas as pl
from jax.experimental.pallas import tpu as pltpu
from jax.sharding import PartitionSpec as P

RAD = 3
HALO = RAD + 1
ZTILES = 11
stiff_floor = 0.001
penalty = 3.0
f32 = jnp.float32
neighbour_offsets = [
    (off_x, off_y, off_z)
    for off_x in (-1, 0, 1)
    for off_y in (-1, 0, 1)
    for off_z in (-1, 0, 1)
    if (off_x, off_y, off_z) != (0, 0, 0)
]
AXES = ("gx", "gy", "gz")


def cone(a, b, k):
    return max(0.0, RAD + 0.5 - math.sqrt(a * a + b * b + k * k))


def lanes_of(shape):
    return lax.broadcasted_iota(jnp.int32, shape, len(shape) - 1)


def rows_of(shape):
    return lax.broadcasted_iota(jnp.int32, shape, len(shape) - 2)


def roll(value, amount, axis):
    size = value.shape[axis]
    amount = amount % size
    return value if amount == 0 else pltpu.roll(value, amount, axis)


def call(body, outs, *args, scratch=(), cost=20000, far=(), far_out=False):
    args = [
        pltpu.with_memory_space_constraint(a, pltpu.HBM) if i in far else a for i, a in enumerate(args)
    ]
    return pl.pallas_call(
        body,
        out_shape=[jax.ShapeDtypeStruct(shape, f32) for shape in outs],
        in_specs=[
            pl.BlockSpec(memory_space=pl.ANY if i in far else pltpu.VMEM) for i in range(len(args))
        ],
        out_specs=[pl.BlockSpec(memory_space=pl.ANY if far_out else pltpu.VMEM)] * len(outs),
        scratch_shapes=list(scratch),
        compiler_params=pltpu.CompilerParams(vmem_limit_bytes=24 * 1024 * 1024),
        cost_estimate=pl.CostEstimate(flops=cost * 1000, bytes_accessed=cost, transcendentals=0),
    )(*args)


def is_even(axis):
    return lax.axis_index(axis) % 2 == 0


def pack_faces(rounds_y, sol_any, dire_any, den_any, lab_any, *refs):
    halves, packs = refs[:2], refs[2 : 2 + 3 * rounds_y]
    sol, dire, den, lab, sems = refs[2 + 3 * rounds_y :]
    copies = [
        pltpu.make_async_copy(source, target, sems.at[i])
        for i, (source, target) in enumerate(
            ((dire_any, dire), (sol_any, sol), (den_any, den), (lab_any, lab))
        )
    ]
    for copy in copies:
        copy.start()
    sub = rows_of((8, 128))
    even_x, even_y = is_even("gx"), is_even("gy")
    for copy in copies:
        copy.wait()

    def masked(x):
        label = lab[x]
        keep = jnp.where(label == 1, 0.0, 1.0).astype(f32)
        keep_last = jnp.where(label >= 1, 0.0, 1.0).astype(f32)
        fields = [dire[0, x] * keep, dire[1, x] * keep, dire[2, x] * keep_last]
        return fields + [sol[0, x], sol[1, x], sol[2, x], den[x]]

    for t in range(2):
        planes = {x: masked(x) for x in (2 * t, 2 * t + 1, 2 * t + 4, 2 * t + 5)}
        for f in range(7):
            for i in (2 * t, 2 * t + 1):
                low, high = planes[i][f], planes[i + 4][f]
                halves[0][f, i] = jnp.where(even_x, high, low)
                halves[1][f, i] = jnp.where(even_x, low, high)
            tiles = []
            for i in (2 * t, 2 * t + 4):
                p, q = planes[i][f], planes[i + 1][f]
                low = jnp.where(sub < 4, p[0:8], roll(q[0:8], 4, 0))
                high = jnp.where(sub < 4, roll(p[8:16], 4, 0), q[8:16])
                tiles.append((jnp.where(even_y, high, low), jnp.where(even_y, low, high)))
            for s in range(rounds_y):
                rows, corner0, corner1 = packs[3 * s : 3 * s + 3]
                low, high = tiles[0][s], tiles[1][s]
                rows[f, t] = low
                rows[f, t + 2] = high
                corner0[f, t] = jnp.where(even_x, high, low)
                corner1[f, t] = jnp.where(even_x, low, high)


def extend(counts, half0, half1, got0, got1, *refs):
    nx, ny, nz = counts
    sides, (ext, ends, send0, send1) = refs[:-4], refs[-4:]
    sub = rows_of((8, 128))
    lane = lanes_of((24, 128))
    lows = lanes_of((8, 128)) % 8 < 4
    ix, iy = lax.axis_index("gx"), lax.axis_index("gy")
    even_y, even_z = is_even("gy"), is_even("gz")
    x_ok = ((ix > 0).astype(f32), (ix < nx - 1).astype(f32))
    y_ok = ((iy > 0).astype(f32), (iy < ny - 1).astype(f32))

    def body(blocks, order):
        def strip(which, f, t):
            tiles = []
            for s in range(len(sides) // 3):
                rows, corner0, corner1 = sides[3 * s : 3 * s + 3]
                ref = rows if which is None else (corner0, corner1)[order[which]]
                tiles.append(ref[f, t])
            keep = 1.0 if which is None else x_ok[which]
            other = tiles[-1]
            low = jnp.where(even_y, other, tiles[0]) * (y_ok[0] * keep)
            high = jnp.where(even_y, tiles[0], other) * (y_ok[1] * keep)
            return low, high

        for f in range(7):
            packed = None
            for X in range(16):
                own = blocks[X // 4][f, X % 4]
                which = None
                if X < 4:
                    which, t = 0, X // 2
                elif X >= 12:
                    which, t = 1, (X - 12) // 2
                else:
                    t = (X - 4) // 2
                if which is not None:
                    own = own * x_ok[which]
                low, high = strip(which, f, t)
                if X % 2 == 0:
                    low = roll(low, 4, 0)
                else:
                    high = roll(high, 4, 0)
                plane = jnp.concatenate([own, jnp.where(sub < 4, high, low)], axis=0)
                ext[f, X] = plane
                turned = roll(plane, 8 * X + 4, 1)
                packed = turned if X == 0 else jnp.where(lane >= 8 * X, turned, packed)
            ends[f] = packed
        for j in range(ZTILES):
            tiles = []
            for t in (j, j + ZTILES):
                tiles.append(ends[t // 3, 8 * (t % 3) : 8 * (t % 3) + 8] if t < 21 else None)
            up, down = tiles[0], tiles[0]
            if tiles[1] is not None:
                up = jnp.where(lows, tiles[0], roll(tiles[1], 4, 1))
                down = jnp.where(lows, roll(tiles[1], -4, 1), tiles[0])
            send0[j] = jnp.where(even_z, up, down)
            send1[j] = jnp.where(even_z, down, up)

    @pl.when(ix % 2 == 0)
    def _():
        body((got1, half1, half0, got0), (1, 0))

    @pl.when(ix % 2 == 1)
    def _():
        body((got0, half0, half1, got1), (0, 1))


def inverse_sums(counts, main, side):
    shape = (24, 128)
    row, lane = rows_of(shape), lanes_of(shape)
    nx, ny, nz = counts
    base_x = lax.axis_index("gx") * 8 - HALO
    base_y = lax.axis_index("gy") * 16
    base_z = lax.axis_index("gz") * 128

    def folded(place, limit):
        def inside(p):
            return jnp.where((p >= 0) & (p < limit), 1.0, 0.0).astype(f32)

        return [inside(place)] + [inside(place - k) + inside(place + k) for k in range(1, RAD + 1)]

    along_y = folded(jnp.where(row < 16 + HALO, row, row - 24) + base_y, ny * 16)

    def partial(along_z):
        table = []
        for a in range(RAD + 1):
            total = jnp.zeros(shape, f32)
            for b in range(RAD + 1):
                line = None
                for k in range(RAD + 1):
                    w = cone(a, b, k)
                    if w > 0:
                        line = w * along_z[k] if line is None else line + w * along_z[k]
                if line is not None:
                    total = total + along_y[b] * line
            table.append(total)
        return table

    def finish(total, along_x, along_z):
        inner = along_x[0] * along_y[0] * along_z[0] > 0
        return jnp.where(inner, 1.0 / jnp.where(inner, total, 1.0), 0.0)

    along_z = folded(lane + base_z, nz * 128)
    table = partial(along_z)
    for X in range(16):
        along_x = folded(jnp.full(shape, X, jnp.int32) + base_x, nx * 8)
        total = sum(along_x[a] * table[a] for a in range(RAD + 1))
        main[X] = finish(total, along_x, along_z)
    place = lane % 8
    along_x = folded(lane // 8 + base_x, nx * 8)
    for s, shift in enumerate((-4, 124)):
        along_z = folded(place + (base_z + shift), nz * 128)
        table = partial(along_z)
        total = sum(along_x[a] * table[a] for a in range(RAD + 1))
        side[s] = finish(total, along_x, along_z)


def apply_operator(nz, ext, got0, got1, res, lab, image, inverse, sums, around, shifts):
    lane = lanes_of((24, 128))
    fields = (0, 1, 2, 6)
    iz = lax.axis_index("gz")
    even = is_even("gz")
    lows = lanes_of((8, 128)) % 8 < 4
    keep = jnp.where(lows, (iz > 0).astype(f32), (iz < nz - 1).astype(f32))
    for j in range(ZTILES):
        zero, one = got0[j], got1[j]
        below, above = jnp.where(even, one, zero), jnp.where(even, zero, one)
        for t in (j, j + ZTILES):
            if t < 21:
                if t != j:
                    below, above = roll(below, -4, 1), roll(above, 4, 1)
                around[t // 3, 8 * (t % 3) : 8 * (t % 3) + 8] = jnp.where(lows, below, above) * keep
    parts = [jnp.zeros((16, 128), f32) for _ in range(4)]
    for plane_at in range(10):
        X = plane_at + 3
        for g, f in enumerate(fields):
            value = ext[f, X]
            near = roll(around[f], 124 - 8 * X, 1)
            if g == 3:
                stiff = stiff_floor + (1.0 - stiff_floor) * value * value * value
                value = jnp.where(value > 0, stiff, 0.0)
                stiff = stiff_floor + (1.0 - stiff_floor) * near * near * near
                near = jnp.where(near > 0, stiff, 0.0)
            up = roll(jnp.where(lane == 0, near, value), -1, 1)
            down = roll(jnp.where(lane == 127, near, value), 1, 1)
            for z, plane in enumerate((down, value, up)):
                for y in range(3):
                    shifts[g, y, z, plane_at] = roll(plane, 1 - y, 0)[0:16]
        x = plane_at - 2
        if x < 0:
            continue
        n = x + 1
        mid = [shifts[g, 1, 1, n] for g in range(4)]
        classes = {1: [None] * 3, 2: [None] * 3, 3: [None] * 3}
        faces = [None] * 3
        edges = [None] * 3
        corners = None

        def add(old, new):
            return new if old is None else old + new

        for o in neighbour_offsets:
            near = [shifts[g, 1 + o[1], 1 + o[2], n + o[0]] for g in range(4)]
            norm = sum(abs(c) for c in o)
            weight = mid[3] + near[3]
            d = [mid[c] - near[c] for c in range(3)]
            acc = classes[norm]
            if norm == 1:
                c0 = [c for c in range(3) if o[c] != 0][0]
                faces[c0] = add(faces[c0], near[3])
                for c in range(3):
                    acc[c] = add(acc[c], weight * (d[c] + d[c] if c == c0 else d[c]))
            else:
                along = None
                for c in range(3):
                    if o[c] != 0:
                        term = d[c]
                        if along is None:
                            along, sign = term, o[c]
                        else:
                            along = along + term if o[c] == sign else along - term
                along = along * (1.0 / norm)
                for c in range(3):
                    if o[c] == 0:
                        pulled = d[c]
                    elif o[c] == sign:
                        pulled = d[c] + along
                    else:
                        pulled = d[c] - along
                    acc[c] = add(acc[c], weight * pulled)
                if norm == 2:
                    c0 = [c for c in range(3) if o[c] == 0][0]
                    edges[c0] = add(edges[c0], near[3])
                else:
                    corners = add(corners, near[3])
        s0 = mid[3]
        all_faces = faces[0] + faces[1] + faces[2]
        all_edges = edges[0] + edges[1] + edges[2]
        common = (all_faces + 6.0 * s0) + 0.75 * (all_edges + 12.0 * s0) + (4.0 / 9.0) * (corners + 8.0 * s0)
        label = lab[x]
        for c in range(3):
            diag = 0.5 * (common + (faces[c] + 2.0 * s0) - 0.25 * (edges[c] + 4.0 * s0))
            fixed = (label == 1) if c < 2 else (label >= 1)
            total = 0.5 * classes[1][c] + 0.25 * classes[2][c] + (1.0 / 6.0) * classes[3][c]
            total = jnp.where(fixed, 0.0, total)
            inv = 1.0 / jnp.where(fixed, 1.0, diag)
            r = res[c, x]
            zeta = r * inv
            scaled = total * inv
            image[c, x] = total
            inverse[c, x] = inv
            parts[0] = parts[0] + r * zeta
            parts[1] = parts[1] + mid[c] * total
            parts[2] = parts[2] + r * scaled
            parts[3] = parts[3] + total * scaled
    place = lanes_of((1, 128)) // 32
    row = None
    for k in range(4):
        part = parts[k][0:8] + parts[k][8:16]
        part = part + roll(part, 64, 1)
        part = jnp.sum(part + roll(part, 32, 1), axis=0, keepdims=True)
        row = part if k == 0 else jnp.where(place == k, part, row)
    sums[...] = jnp.broadcast_to(row[None], sums.shape)


def quadratic(d, o):
    norm = sum(abs(c) for c in o)
    square = d[0] * d[0] + d[1] * d[1] + d[2] * d[2]
    along, sign = None, 1
    for c in range(3):
        if o[c] != 0:
            if along is None:
                along, sign = d[c], o[c]
            else:
                along = along + d[c] if o[c] == sign else along - d[c]
    if norm == 1:
        return square + along * along
    return (1.0 / norm) * square + (1.0 / (norm * norm)) * (along * along)


pairs = [((1, 0, 0), 0, 0, 0, 0)]
pairs += [((a, 1, 0), 0, 0, 2, 2) for a in (-1, 0, 1)]
pairs += [((a, 0, 1), 0, 0, 1, 1) for a in (-1, 0, 1)]
pairs += [((a, 1, 1), 0, 0, 3, 3) for a in (-1, 0, 1)]
pairs += [((a, -1, 1), 2, 2, 1, 1) for a in (-1, 0, 1)]
energy_scale = -penalty * (1.0 - stiff_floor) * 0.5


def plus(old, new):
    return new if old is None else old + new


def finish_step(
    ext, ends, around, total, image, inverse, res, dire, hinv, hside,
    new_sol_any, new_res_any, new_dir_any, sens_any, us, lines, new_sol, new_res, new_dir, sens, sems,
):
    lane = lanes_of((24, 128))
    lows = lane % 8 < 4
    copies = [
        pltpu.make_async_copy(source, target, sems.at[i])
        for i, (source, target) in enumerate(
            ((new_res, new_res_any), (new_dir, new_dir_any), (new_sol, new_sol_any), (sens, sens_any))
        )
    ]
    spread = jnp.broadcast_to(jnp.sum(total[...], axis=0), (8, 128))
    tot = jnp.sum(jnp.where(lanes_of((8, 128)) // 32 == rows_of((8, 128)), spread, 0.0), axis=1, keepdims=True)
    rz, pq, s2, s3 = (tot[k : k + 1] for k in range(4))
    alpha = rz / pq
    beta = (rz + alpha * (alpha * s3 - 2.0 * s2)) / rz

    for x in range(8):
        for c in range(3):
            r = res[c, x] - alpha * image[c, x]
            new_res[c, x] = r
            new_dir[c, x] = r * inverse[c, x] + beta * dire[c, x]
    copies[0].start()
    copies[1].start()

    halos, lefts, rights = [], [], []
    for c in range(3):
        halo_u = around[3 + c] + alpha * around[c]
        own_u = ends[3 + c] + alpha * ends[c]
        halos.append(halo_u)
        lefts.append(jnp.where(lows, halo_u, own_u))
        rights.append(jnp.where(lows, own_u, halo_u))
    sides, side_low = [], None
    den_left = jnp.where(lows, around[6], ends[6])
    den_right = jnp.where(lows, ends[6], around[6])
    for s, (u, den) in enumerate(((lefts, den_left), (rights, den_right))):
        up = [roll(v, -1, 1) for v in u]
        moved = [u, up, [roll(v, -1, 0) for v in u], [roll(v, -1, 0) for v in up]]
        far = {}
        acc = {}
        for o, field0, frame0, field1, frame1 in pairs:
            key = (field1, o[0])
            if key not in far:
                far[key] = [roll(v, -8 * o[0], 1) for v in moved[field1]]
            g = quadratic([moved[field0][c] - far[key][c] for c in range(3)], o)
            acc[frame0, 0] = plus(acc.get((frame0, 0)), g)
            acc[frame1, o[0]] = plus(acc.get((frame1, o[0])), g)
        frames = []
        for frame in range(4):
            value = None
            for a in (-1, 0, 1):
                if (frame, a) in acc:
                    value = plus(value, roll(acc[frame, a], 8 * a, 1))
            frames.append(value)
        up = frames[1] + roll(frames[3], 1, 0)
        if s == 0:
            side_low = up
        energy = frames[0] + roll(frames[2], 1, 0) + roll(up, 1, 1)
        sides.append(energy_scale * (den * den) * energy * hside[s])
    ends_scaled = jnp.where(lows, sides[0], sides[1])

    def iterate(X):
        for c in range(3):
            u = ext[3 + c, X] + alpha * ext[c, X]
            if 4 <= X < 12:
                new_sol[c, X - 4] = u[0:16]
            near = roll(halos[c], 124 - 8 * X, 1)
            up = roll(jnp.where(lane == 0, near, u), -1, 1)
            us[0, c, X] = u
            us[1, c, X] = up
            us[2, c, X] = roll(u, -1, 0)
            us[3, c, X] = roll(up, -1, 0)
        if X == 11:
            copies[2].start()

    acc = [[None] * 4 for _ in range(16)]

    def pair_up(X):
        for o, field0, frame0, field1, frame1 in pairs:
            to = X + o[0]
            if not 0 <= to < 16 or not (1 <= X < 15 or 1 <= to < 15):
                continue
            g = quadratic([us[field0, c, X] - us[field1, c, to] for c in range(3)], o)
            if 1 <= X < 15:
                acc[X][frame0] = plus(acc[X][frame0], g)
            if 1 <= to < 15:
                acc[to][frame1] = plus(acc[to][frame1], g)

    def filter_lines(X):
        frames = acc[X]
        up = frames[1] + roll(frames[3], 1, 0)
        below = roll(side_low, 127 - (8 * X + 3), 1)
        up = roll(jnp.where(lane == 127, below, up), 1, 1)
        den = ext[6, X]
        energy = frames[0] + roll(frames[2], 1, 0) + up
        s = energy_scale * (den * den) * energy * hinv[X]
        near = roll(ends_scaled, 124 - 8 * X, 1)
        fold = [s]
        for k in range(1, RAD + 1):
            above = roll(jnp.where(lane < k, near, s), -k, 1)
            under = roll(jnp.where(lane >= 128 - k, near, s), k, 1)
            fold.append(above + under)
        for k in range(RAD + 1):
            lines[X, k] = fold[k]

    def filter_rows(x):
        groups = {}
        for a in range(RAD + 1):
            for k in range(RAD + 1):
                if cone(a, 0, k) > 0:
                    both = lines[x + HALO + a, k]
                    if a > 0:
                        both = both + lines[x + HALO - a, k]
                    groups[a * a + k * k] = plus(groups.get(a * a + k * k), both)
        value = None
        for b in range(RAD + 1):
            row = None
            for d, group in groups.items():
                w = RAD + 0.5 - math.sqrt(d + b * b)
                if w > 0:
                    row = plus(row, w * group)
            value = row if b == 0 else value + roll(row, b, 0) + roll(row, -b, 0)
        sens[x] = value[0:16]

    for X in range(16 + 1):
        if X < 16:
            iterate(X)
        if X >= 1:
            pair_up(X - 1)
        if X >= 3:
            filter_lines(X - 2)
        if X - 2 - 2 * RAD - 1 >= 0:
            filter_rows(X - 2 - 2 * RAD - 1)
    copies[3].start()
    for copy in copies:
        copy.wait()


def partner(place, turn, count):
    other = (place ^ 1) if turn == 0 else ((place + 1) ^ 1) - 1
    return other if 0 <= other < count else None


def swap_pairs(counts, turns):
    pairs = []
    for flat in range(math.prod(counts)):
        rest, place = flat, []
        for count in reversed(counts):
            place.insert(0, rest % count)
            rest //= count
        to = [p if t is None else partner(p, t, c) for p, t, c in zip(place, turns, counts)]
        if None in to:
            continue
        index = 0
        for p, count in zip(to, counts):
            index = index * count + p
        pairs.append((flat, index))
    return pairs


def per_device(mesh_shape, solution, residual, direction, density, labels):
    nx, ny, nz = (mesh_shape[a] for a in AXES)
    half, full, corner = (7, 4, 16, 128), (7, 4, 8, 128), (7, 2, 8, 128)
    rounds_y = 1 if ny == 2 else 2
    field, flat = (3, 8, 16, 128), (8, 16, 128)
    packed = call(
        functools.partial(pack_faces, rounds_y),
        [half, half] + [full, corner, corner] * rounds_y,
        solution, direction, density, labels,
        far=range(4),
        scratch=[
            pltpu.VMEM(field, f32), pltpu.VMEM(field, f32), pltpu.VMEM(flat, f32),
            pltpu.VMEM(flat, jnp.int32), pltpu.SemaphoreType.DMA((4,)),
        ],
    )
    halves = packed[:2]
    plane = ("gx", "gy")
    got = [lax.ppermute(halves[r], plane, swap_pairs((nx, ny), (r, None))) for r in (0, 1)]
    strips = []
    for s in range(rounds_y):
        for array, turn in zip(packed[2 + 3 * s : 5 + 3 * s], (None, 0, 1)):
            strips.append(lax.ppermute(array, plane, swap_pairs((nx, ny), (turn, s))))
    hinv, hside = call(functools.partial(inverse_sums, (nx, ny, nz)), [(16, 24, 128), (2, 24, 128)])
    zend = (ZTILES, 8, 128)
    ext, ends, *sends = call(
        functools.partial(extend, (nx, ny, nz)),
        [(7, 16, 24, 128), (7, 24, 128), zend, zend],
        *halves, *got, *strips,
    )
    ends_got = [lax.ppermute(sends[r], "gz", swap_pairs((nz,), (r,))) for r in (0, 1)]
    image, inverse, sums, around = call(
        functools.partial(apply_operator, nz),
        [field, field, (nx * ny, 1, 128), (7, 24, 128)],
        ext, *ends_got, residual, labels,
        scratch=[pltpu.VMEM((4, 3, 3, 10, 16, 128), f32)],
    )
    in_plane = jnp.sum(lax.all_to_all(sums, plane, 0, 0), axis=0, keepdims=True)
    total = lax.all_to_all(jnp.broadcast_to(in_plane, (nz, 1, 128)), "gz", 0, 0)
    return tuple(
        call(
            finish_step,
            [field, field, field, flat],
            ext, ends, around, total, image, inverse, residual, direction, hinv, hside,
            scratch=[
                pltpu.VMEM((4, 3, 16, 24, 128), f32), pltpu.VMEM((16, RAD + 1, 24, 128), f32),
                pltpu.VMEM(field, f32), pltpu.VMEM(field, f32), pltpu.VMEM(field, f32),
                pltpu.VMEM(flat, f32), pltpu.SemaphoreType.DMA((4,)),
            ],
            far_out=True,
        )
    )


def solution(mesh):
    wide, flat = P(None, "gx", "gy", "gz"), P("gx", "gy", "gz")
    return jax.shard_map(
        functools.partial(per_device, dict(mesh.shape)),
        mesh=mesh,
        in_specs=(wide, wide, wide, flat, flat),
        out_specs=(wide, wide, wide, flat),
        check_vma=False,
    )
```

```python
import functools
import math

import jax
import jax.numpy as jnp
from jax import lax
from jax.experimental import pallas as pl
from jax.experimental.pallas import tpu as pltpu
from jax.sharding import PartitionSpec as P

RAD = 3
HALO = RAD + 1
ZTILES = 11
stiff_floor = 0.001
penalty = 3.0
f32 = jnp.float32
neighbour_offsets = [
    (off_x, off_y, off_z)
    for off_x in (-1, 0, 1)
    for off_y in (-1, 0, 1)
    for off_z in (-1, 0, 1)
    if (off_x, off_y, off_z) != (0, 0, 0)
]
AXES = ("gx", "gy", "gz")


def cone(a, b, k):
    return max(0.0, RAD + 0.5 - math.sqrt(a * a + b * b + k * k))


def lanes_of(shape):
    return lax.broadcasted_iota(jnp.int32, shape, len(shape) - 1)


def rows_of(shape):
    return lax.broadcasted_iota(jnp.int32, shape, len(shape) - 2)


def roll(value, amount, axis):
    size = value.shape[axis]
    amount = amount % size
    return value if amount == 0 else pltpu.roll(value, amount, axis)


def call(body, outs, *args, scratch=(), cost=20000, far=(), far_out=False):
    args = [
        pltpu.with_memory_space_constraint(a, pltpu.HBM) if i in far else a for i, a in enumerate(args)
    ]
    return pl.pallas_call(
        body,
        out_shape=[jax.ShapeDtypeStruct(shape, f32) for shape in outs],
        in_specs=[
            pl.BlockSpec(memory_space=pl.ANY if i in far else pltpu.VMEM) for i in range(len(args))
        ],
        out_specs=[pl.BlockSpec(memory_space=pl.ANY if far_out else pltpu.VMEM)] * len(outs),
        scratch_shapes=list(scratch),
        compiler_params=pltpu.CompilerParams(vmem_limit_bytes=24 * 1024 * 1024),
        cost_estimate=pl.CostEstimate(flops=cost * 1000, bytes_accessed=cost, transcendentals=0),
    )(*args)


def is_even(axis):
    return lax.axis_index(axis) % 2 == 0


def pack_faces(rounds_y, sol_any, dire_any, den_any, lab_any, *refs):
    halves, packs = refs[:2], refs[2 : 2 + 3 * rounds_y]
    sol, dire, den, lab, sems = refs[2 + 3 * rounds_y :]
    copies = [
        pltpu.make_async_copy(source, target, sems.at[i])
        for i, (source, target) in enumerate(
            ((dire_any, dire), (sol_any, sol), (den_any, den), (lab_any, lab))
        )
    ]
    for copy in copies:
        copy.start()
    sub = rows_of((8, 128))
    even_x, even_y = is_even("gx"), is_even("gy")
    for copy in copies:
        copy.wait()

    def masked(x):
        label = lab[x]
        keep = jnp.where(label == 1, 0.0, 1.0).astype(f32)
        keep_last = jnp.where(label >= 1, 0.0, 1.0).astype(f32)
        fields = [dire[0, x] * keep, dire[1, x] * keep, dire[2, x] * keep_last]
        return fields + [sol[0, x], sol[1, x], sol[2, x], den[x]]

    for t in range(2):
        planes = {x: masked(x) for x in (2 * t, 2 * t + 1, 2 * t + 4, 2 * t + 5)}
        for f in range(7):
            for i in (2 * t, 2 * t + 1):
                low, high = planes[i][f], planes[i + 4][f]
                halves[0][f, i] = jnp.where(even_x, high, low)
                halves[1][f, i] = jnp.where(even_x, low, high)
            tiles = []
            for i in (2 * t, 2 * t + 4):
                p, q = planes[i][f], planes[i + 1][f]
                low = jnp.where(sub < 4, p[0:8], roll(q[0:8], 4, 0))
                high = jnp.where(sub < 4, roll(p[8:16], 4, 0), q[8:16])
                tiles.append((jnp.where(even_y, high, low), jnp.where(even_y, low, high)))
            for s in range(rounds_y):
                rows, corner0, corner1 = packs[3 * s : 3 * s + 3]
                low, high = tiles[0][s], tiles[1][s]
                rows[f, t] = low
                rows[f, t + 2] = high
                corner0[f, t] = jnp.where(even_x, high, low)
                corner1[f, t] = jnp.where(even_x, low, high)


def extend(counts, half0, half1, got0, got1, *refs):
    nx, ny, nz = counts
    sides, (ext, ends, send0, send1) = refs[:-4], refs[-4:]
    sub = rows_of((8, 128))
    lane = lanes_of((24, 128))
    lows = lanes_of((8, 128)) % 8 < 4
    ix, iy = lax.axis_index("gx"), lax.axis_index("gy")
    even_y, even_z = is_even("gy"), is_even("gz")
    x_ok = ((ix > 0).astype(f32), (ix < nx - 1).astype(f32))
    y_ok = ((iy > 0).astype(f32), (iy < ny - 1).astype(f32))

    def body(blocks, order):
        def strip(which, f, t):
            tiles = []
            for s in range(len(sides) // 3):
                rows, corner0, corner1 = sides[3 * s : 3 * s + 3]
                ref = rows if which is None else (corner0, corner1)[order[which]]
                tiles.append(ref[f, t])
            keep = 1.0 if which is None else x_ok[which]
            other = tiles[-1]
            low = jnp.where(even_y, other, tiles[0]) * (y_ok[0] * keep)
            high = jnp.where(even_y, tiles[0], other) * (y_ok[1] * keep)
            return low, high

        for f in range(7):
            packed = None
            for X in range(16):
                own = blocks[X // 4][f, X % 4]
                which = None
                if X < 4:
                    which, t = 0, X // 2
                elif X >= 12:
                    which, t = 1, (X - 12) // 2
                else:
                    t = (X - 4) // 2
                if which is not None:
                    own = own * x_ok[which]
                low, high = strip(which, f, t)
                if X % 2 == 0:
                    low = roll(low, 4, 0)
                else:
                    high = roll(high, 4, 0)
                plane = jnp.concatenate([own, jnp.where(sub < 4, high, low)], axis=0)
                ext[f, X] = plane
                turned = roll(plane, 8 * X + 4, 1)
                packed = turned if X == 0 else jnp.where(lane >= 8 * X, turned, packed)
            ends[f] = packed
        for j in range(ZTILES):
            tiles = []
            for t in (j, j + ZTILES):
                tiles.append(ends[t // 3, 8 * (t % 3) : 8 * (t % 3) + 8] if t < 21 else None)
            up, down = tiles[0], tiles[0]
            if tiles[1] is not None:
                up = jnp.where(lows, tiles[0], roll(tiles[1], 4, 1))
                down = jnp.where(lows, roll(tiles[1], -4, 1), tiles[0])
            send0[j] = jnp.where(even_z, up, down)
            send1[j] = jnp.where(even_z, down, up)

    @pl.when(ix % 2 == 0)
    def _():
        body((got1, half1, half0, got0), (1, 0))

    @pl.when(ix % 2 == 1)
    def _():
        body((got0, half0, half1, got1), (0, 1))


def inverse_sums(counts, main, side):
    shape = (24, 128)
    row, lane = rows_of(shape), lanes_of(shape)
    nx, ny, nz = counts
    base_x = lax.axis_index("gx") * 8 - HALO
    base_y = lax.axis_index("gy") * 16
    base_z = lax.axis_index("gz") * 128

    def folded(place, limit):
        def inside(p):
            return jnp.where((p >= 0) & (p < limit), 1.0, 0.0).astype(f32)

        return [inside(place)] + [inside(place - k) + inside(place + k) for k in range(1, RAD + 1)]

    along_y = folded(jnp.where(row < 16 + HALO, row, row - 24) + base_y, ny * 16)

    def partial(along_z):
        table = []
        for a in range(RAD + 1):
            total = jnp.zeros(shape, f32)
            for b in range(RAD + 1):
                line = None
                for k in range(RAD + 1):
                    w = cone(a, b, k)
                    if w > 0:
                        line = w * along_z[k] if line is None else line + w * along_z[k]
                if line is not None:
                    total = total + along_y[b] * line
            table.append(total)
        return table

    def finish(total, along_x, along_z):
        inner = along_x[0] * along_y[0] * along_z[0] > 0
        return jnp.where(inner, 1.0 / jnp.where(inner, total, 1.0), 0.0)

    along_z = folded(lane + base_z, nz * 128)
    table = partial(along_z)
    for X in range(16):
        along_x = folded(jnp.full(shape, X, jnp.int32) + base_x, nx * 8)
        total = sum(along_x[a] * table[a] for a in range(RAD + 1))
        main[X] = finish(total, along_x, along_z)
    place = lane % 8
    along_x = folded(lane // 8 + base_x, nx * 8)
    for s, shift in enumerate((-4, 124)):
        along_z = folded(place + (base_z + shift), nz * 128)
        table = partial(along_z)
        total = sum(along_x[a] * table[a] for a in range(RAD + 1))
        side[s] = finish(total, along_x, along_z)


def apply_operator(nz, ext, got0, got1, res, lab, image, inverse, sums, around, shifts):
    lane = lanes_of((24, 128))
    fields = (0, 1, 2, 6)
    iz = lax.axis_index("gz")
    even = is_even("gz")
    lows = lanes_of((8, 128)) % 8 < 4
    keep = jnp.where(lows, (iz > 0).astype(f32), (iz < nz - 1).astype(f32))
    for j in range(ZTILES):
        zero, one = got0[j], got1[j]
        below, above = jnp.where(even, one, zero), jnp.where(even, zero, one)
        for t in (j, j + ZTILES):
            if t < 21:
                if t != j:
                    below, above = roll(below, -4, 1), roll(above, 4, 1)
                around[t // 3, 8 * (t % 3) : 8 * (t % 3) + 8] = jnp.where(lows, below, above) * keep
    parts = [jnp.zeros((16, 128), f32) for _ in range(4)]
    for plane_at in range(10):
        X = plane_at + 3
        for g, f in enumerate(fields):
            value = ext[f, X]
            near = roll(around[f], 124 - 8 * X, 1)
            if g == 3:
                stiff = stiff_floor + (1.0 - stiff_floor) * value * value * value
                value = jnp.where(value > 0, stiff, 0.0)
                stiff = stiff_floor + (1.0 - stiff_floor) * near * near * near
                near = jnp.where(near > 0, stiff, 0.0)
            up = roll(jnp.where(lane == 0, near, value), -1, 1)
            down = roll(jnp.where(lane == 127, near, value), 1, 1)
            for z, plane in enumerate((down, value, up)):
                for y in range(3):
                    shifts[g, y, z, plane_at] = roll(plane, 1 - y, 0)[0:16]
        x = plane_at - 2
        if x < 0:
            continue
        n = x + 1
        mid = [shifts[g, 1, 1, n] for g in range(4)]
        classes = {1: [None] * 3, 2: [None] * 3, 3: [None] * 3}
        faces = [None] * 3
        edges = [None] * 3
        corners = None

        def add(old, new):
            return new if old is None else old + new

        for o in neighbour_offsets:
            near = [shifts[g, 1 + o[1], 1 + o[2], n + o[0]] for g in range(4)]
            norm = sum(abs(c) for c in o)
            weight = mid[3] + near[3]
            d = [mid[c] - near[c] for c in range(3)]
            acc = classes[norm]
            if norm == 1:
                c0 = [c for c in range(3) if o[c] != 0][0]
                faces[c0] = add(faces[c0], near[3])
                for c in range(3):
                    acc[c] = add(acc[c], weight * (d[c] + d[c] if c == c0 else d[c]))
            else:
                along = None
                for c in range(3):
                    if o[c] != 0:
                        term = d[c]
                        if along is None:
                            along, sign = term, o[c]
                        else:
                            along = along + term if o[c] == sign else along - term
                along = along * (1.0 / norm)
                for c in range(3):
                    if o[c] == 0:
                        pulled = d[c]
                    elif o[c] == sign:
                        pulled = d[c] + along
                    else:
                        pulled = d[c] - along
                    acc[c] = add(acc[c], weight * pulled)
                if norm == 2:
                    c0 = [c for c in range(3) if o[c] == 0][0]
                    edges[c0] = add(edges[c0], near[3])
                else:
                    corners = add(corners, near[3])
        s0 = mid[3]
        all_faces = faces[0] + faces[1] + faces[2]
        all_edges = edges[0] + edges[1] + edges[2]
        common = (all_faces + 6.0 * s0) + 0.75 * (all_edges + 12.0 * s0) + (4.0 / 9.0) * (corners + 8.0 * s0)
        label = lab[x]
        for c in range(3):
            diag = 0.5 * (common + (faces[c] + 2.0 * s0) - 0.25 * (edges[c] + 4.0 * s0))
            fixed = (label == 1) if c < 2 else (label >= 1)
            total = 0.5 * classes[1][c] + 0.25 * classes[2][c] + (1.0 / 6.0) * classes[3][c]
            total = jnp.where(fixed, 0.0, total)
            inv = 1.0 / jnp.where(fixed, 1.0, diag)
            r = res[c, x]
            zeta = r * inv
            scaled = total * inv
            image[c, x] = total
            inverse[c, x] = inv
            parts[0] = parts[0] + r * zeta
            parts[1] = parts[1] + mid[c] * total
            parts[2] = parts[2] + r * scaled
            parts[3] = parts[3] + total * scaled
    place = lanes_of((1, 128)) // 32
    row = None
    for k in range(4):
        part = parts[k][0:8] + parts[k][8:16]
        part = part + roll(part, 64, 1)
        part = jnp.sum(part + roll(part, 32, 1), axis=0, keepdims=True)
        row = part if k == 0 else jnp.where(place == k, part, row)
    sums[...] = jnp.broadcast_to(row[None], sums.shape)


def quadratic(d, o):
    norm = sum(abs(c) for c in o)
    square = d[0] * d[0] + d[1] * d[1] + d[2] * d[2]
    along, sign = None, 1
    for c in range(3):
        if o[c] != 0:
            if along is None:
                along, sign = d[c], o[c]
            else:
                along = along + d[c] if o[c] == sign else along - d[c]
    if norm == 1:
        return square + along * along
    return (1.0 / norm) * square + (1.0 / (norm * norm)) * (along * along)


pairs = [((1, 0, 0), 0, 0, 0, 0)]
pairs += [((a, 1, 0), 0, 0, 2, 2) for a in (-1, 0, 1)]
pairs += [((a, 0, 1), 0, 0, 1, 1) for a in (-1, 0, 1)]
pairs += [((a, 1, 1), 0, 0, 3, 3) for a in (-1, 0, 1)]
pairs += [((a, -1, 1), 2, 2, 1, 1) for a in (-1, 0, 1)]
energy_scale = -penalty * (1.0 - stiff_floor) * 0.5


def plus(old, new):
    return new if old is None else old + new


def finish_step(
    ext, ends, around, ours, theirs, image, inverse, res, dire, hinv, hside,
    new_sol_any, new_res_any, new_dir_any, sens_any, us, lines, new_sol, new_res, new_dir, sens, sems,
):
    lane = lanes_of((24, 128))
    lows = lane % 8 < 4
    copies = [
        pltpu.make_async_copy(source, target, sems.at[i])
        for i, (source, target) in enumerate(
            ((new_res, new_res_any), (new_dir, new_dir_any), (new_sol, new_sol_any), (sens, sens_any))
        )
    ]
    spread = jnp.broadcast_to(ours[...] + theirs[...], (8, 128))
    tot = jnp.sum(jnp.where(lanes_of((8, 128)) // 32 == rows_of((8, 128)), spread, 0.0), axis=1, keepdims=True)
    rz, pq, s2, s3 = (tot[k : k + 1] for k in range(4))
    alpha = rz / pq
    beta = (rz + alpha * (alpha * s3 - 2.0 * s2)) / rz

    for x in range(8):
        for c in range(3):
            r = res[c, x] - alpha * image[c, x]
            new_res[c, x] = r
            new_dir[c, x] = r * inverse[c, x] + beta * dire[c, x]
    copies[0].start()
    copies[1].start()

    halos, lefts, rights = [], [], []
    for c in range(3):
        halo_u = around[3 + c] + alpha * around[c]
        own_u = ends[3 + c] + alpha * ends[c]
        halos.append(halo_u)
        lefts.append(jnp.where(lows, halo_u, own_u))
        rights.append(jnp.where(lows, own_u, halo_u))
    sides, side_low = [], None
    den_left = jnp.where(lows, around[6], ends[6])
    den_right = jnp.where(lows, ends[6], around[6])
    for s, (u, den) in enumerate(((lefts, den_left), (rights, den_right))):
        up = [roll(v, -1, 1) for v in u]
        moved = [u, up, [roll(v, -1, 0) for v in u], [roll(v, -1, 0) for v in up]]
        far = {}
        acc = {}
        for o, field0, frame0, field1, frame1 in pairs:
            key = (field1, o[0])
            if key not in far:
                far[key] = [roll(v, -8 * o[0], 1) for v in moved[field1]]
            g = quadratic([moved[field0][c] - far[key][c] for c in range(3)], o)
            acc[frame0, 0] = plus(acc.get((frame0, 0)), g)
            acc[frame1, o[0]] = plus(acc.get((frame1, o[0])), g)
        frames = []
        for frame in range(4):
            value = None
            for a in (-1, 0, 1):
                if (frame, a) in acc:
                    value = plus(value, roll(acc[frame, a], 8 * a, 1))
            frames.append(value)
        up = frames[1] + roll(frames[3], 1, 0)
        if s == 0:
            side_low = up
        energy = frames[0] + roll(frames[2], 1, 0) + roll(up, 1, 1)
        sides.append(energy_scale * (den * den) * energy * hside[s])
    ends_scaled = jnp.where(lows, sides[0], sides[1])

    def iterate(X):
        for c in range(3):
            u = ext[3 + c, X] + alpha * ext[c, X]
            if 4 <= X < 12:
                new_sol[c, X - 4] = u[0:16]
            near = roll(halos[c], 124 - 8 * X, 1)
            up = roll(jnp.where(lane == 0, near, u), -1, 1)
            us[0, c, X] = u
            us[1, c, X] = up
            us[2, c, X] = roll(u, -1, 0)
            us[3, c, X] = roll(up, -1, 0)
        if X == 11:
            copies[2].start()

    acc = [[None] * 4 for _ in range(16)]

    def pair_up(X):
        for o, field0, frame0, field1, frame1 in pairs:
            to = X + o[0]
            if not 0 <= to < 16 or not (1 <= X < 15 or 1 <= to < 15):
                continue
            g = quadratic([us[field0, c, X] - us[field1, c, to] for c in range(3)], o)
            if 1 <= X < 15:
                acc[X][frame0] = plus(acc[X][frame0], g)
            if 1 <= to < 15:
                acc[to][frame1] = plus(acc[to][frame1], g)

    def filter_lines(X):
        frames = acc[X]
        up = frames[1] + roll(frames[3], 1, 0)
        below = roll(side_low, 127 - (8 * X + 3), 1)
        up = roll(jnp.where(lane == 127, below, up), 1, 1)
        den = ext[6, X]
        energy = frames[0] + roll(frames[2], 1, 0) + up
        s = energy_scale * (den * den) * energy * hinv[X]
        near = roll(ends_scaled, 124 - 8 * X, 1)
        fold = [s]
        for k in range(1, RAD + 1):
            above = roll(jnp.where(lane < k, near, s), -k, 1)
            under = roll(jnp.where(lane >= 128 - k, near, s), k, 1)
            fold.append(above + under)
        for k in range(RAD + 1):
            lines[X, k] = fold[k]

    def filter_rows(x):
        groups = {}
        for a in range(RAD + 1):
            for k in range(RAD + 1):
                if cone(a, 0, k) > 0:
                    both = lines[x + HALO + a, k]
                    if a > 0:
                        both = both + lines[x + HALO - a, k]
                    groups[a * a + k * k] = plus(groups.get(a * a + k * k), both)
        value = None
        for b in range(RAD + 1):
            row = None
            for d, group in groups.items():
                w = RAD + 0.5 - math.sqrt(d + b * b)
                if w > 0:
                    row = plus(row, w * group)
            value = row if b == 0 else value + roll(row, b, 0) + roll(row, -b, 0)
        sens[x] = value[0:16]

    for X in range(16 + 1):
        if X < 16:
            iterate(X)
        if X >= 1:
            pair_up(X - 1)
        if X >= 3:
            filter_lines(X - 2)
        if X - 2 - 2 * RAD - 1 >= 0:
            filter_rows(X - 2 - 2 * RAD - 1)
    copies[3].start()
    for copy in copies:
        copy.wait()


def partner(place, turn, count):
    other = (place ^ 1) if turn == 0 else ((place + 1) ^ 1) - 1
    return other if 0 <= other < count else None


def swap_pairs(counts, turns):
    pairs = []
    for flat in range(math.prod(counts)):
        rest, place = flat, []
        for count in reversed(counts):
            place.insert(0, rest % count)
            rest //= count
        to = [p if t is None else partner(p, t, c) for p, t, c in zip(place, turns, counts)]
        if None in to:
            continue
        index = 0
        for p, count in zip(to, counts):
            index = index * count + p
        pairs.append((flat, index))
    return pairs


def per_device(mesh_shape, solution, residual, direction, density, labels):
    nx, ny, nz = (mesh_shape[a] for a in AXES)
    half, full, corner = (7, 4, 16, 128), (7, 4, 8, 128), (7, 2, 8, 128)
    rounds_y = 1 if ny == 2 else 2
    field, flat = (3, 8, 16, 128), (8, 16, 128)
    steps = 2 if nx % 2 == 0 else 1
    same = [
        [i for i in range(nx * ny * nz) if i // (ny * nz) % steps == step] for step in range(steps)
    ]
    packed = call(
        functools.partial(pack_faces, rounds_y),
        [half, half] + [full, corner, corner] * rounds_y,
        solution, direction, density, labels,
        far=range(4),
        scratch=[
            pltpu.VMEM(field, f32), pltpu.VMEM(field, f32), pltpu.VMEM(flat, f32),
            pltpu.VMEM(flat, jnp.int32), pltpu.SemaphoreType.DMA((4,)),
        ],
    )
    halves = packed[:2]
    plane = ("gx", "gy")
    got = [lax.ppermute(halves[r], plane, swap_pairs((nx, ny), (r, None))) for r in (0, 1)]
    strips = []
    for s in range(rounds_y):
        for array, turn in zip(packed[2 + 3 * s : 5 + 3 * s], (None, 0, 1)):
            strips.append(lax.ppermute(array, plane, swap_pairs((nx, ny), (turn, s))))
    hinv, hside = call(functools.partial(inverse_sums, (nx, ny, nz)), [(16, 24, 128), (2, 24, 128)])
    zend = (ZTILES, 8, 128)
    ext, ends, *sends = call(
        functools.partial(extend, (nx, ny, nz)),
        [(7, 16, 24, 128), (7, 24, 128), zend, zend],
        *halves, *got, *strips,
    )
    ends_got = [lax.ppermute(sends[r], "gz", swap_pairs((nz,), (r,))) for r in (0, 1)]
    image, inverse, sums, around = call(
        functools.partial(apply_operator, nz),
        [field, field, (len(same[0]), 1, 128), (7, 24, 128)],
        ext, *ends_got, residual, labels,
        scratch=[pltpu.VMEM((4, 3, 3, 10, 16, 128), f32)],
    )
    ours = jnp.sum(lax.all_to_all(sums, AXES, 0, 0, axis_index_groups=same), axis=0)
    theirs = lax.ppermute(ours, "gx", swap_pairs((nx,), (0,))) if len(same) > 1 else jnp.zeros_like(ours)
    return tuple(
        call(
            finish_step,
            [field, field, field, flat],
            ext, ends, around, ours, theirs, image, inverse, residual, direction, hinv, hside,
            scratch=[
                pltpu.VMEM((4, 3, 16, 24, 128), f32), pltpu.VMEM((16, RAD + 1, 24, 128), f32),
                pltpu.VMEM(field, f32), pltpu.VMEM(field, f32), pltpu.VMEM(field, f32),
                pltpu.VMEM(flat, f32), pltpu.SemaphoreType.DMA((4,)),
            ],
            far_out=True,
        )
    )


def solution(mesh):
    wide, flat = P(None, "gx", "gy", "gz"), P("gx", "gy", "gz")
    return jax.shard_map(
        functools.partial(per_device, dict(mesh.shape)),
        mesh=mesh,
        in_specs=(wide, wide, wide, flat, flat),
        out_specs=(wide, wide, wide, flat),
        check_vma=False,
    )
```

```python
import functools
import math

import jax
import jax.numpy as jnp
from jax import lax
from jax.experimental import pallas as pl
from jax.experimental.pallas import tpu as pltpu
from jax.sharding import PartitionSpec as P

RAD = 3
HALO = RAD + 1
ZTILES = 11
stiff_floor = 0.001
penalty = 3.0
f32 = jnp.float32
neighbour_offsets = [
    (off_x, off_y, off_z)
    for off_x in (-1, 0, 1)
    for off_y in (-1, 0, 1)
    for off_z in (-1, 0, 1)
    if (off_x, off_y, off_z) != (0, 0, 0)
]
AXES = ("gx", "gy", "gz")


def cone(a, b, k):
    return max(0.0, RAD + 0.5 - math.sqrt(a * a + b * b + k * k))


def lanes_of(shape):
    return lax.broadcasted_iota(jnp.int32, shape, len(shape) - 1)


def rows_of(shape):
    return lax.broadcasted_iota(jnp.int32, shape, len(shape) - 2)


def roll(value, amount, axis):
    size = value.shape[axis]
    amount = amount % size
    return value if amount == 0 else pltpu.roll(value, amount, axis)


def call(body, outs, *args, scratch=(), cost=20000, far=(), far_out=False):
    args = [
        pltpu.with_memory_space_constraint(a, pltpu.HBM) if i in far else a for i, a in enumerate(args)
    ]
    return pl.pallas_call(
        body,
        out_shape=[jax.ShapeDtypeStruct(shape, f32) for shape in outs],
        in_specs=[
            pl.BlockSpec(memory_space=pl.ANY if i in far else pltpu.VMEM) for i in range(len(args))
        ],
        out_specs=[pl.BlockSpec(memory_space=pl.ANY if far_out else pltpu.VMEM)] * len(outs),
        scratch_shapes=list(scratch),
        compiler_params=pltpu.CompilerParams(vmem_limit_bytes=24 * 1024 * 1024),
        cost_estimate=pl.CostEstimate(flops=cost * 1000, bytes_accessed=cost, transcendentals=0),
    )(*args)


def is_even(axis):
    return lax.axis_index(axis) % 2 == 0


def pack_faces(rounds_y, sol_any, dire_any, den_any, lab_any, *refs):
    halves, packs = refs[:2], refs[2 : 2 + 3 * rounds_y]
    sol, dire, den, lab, sems = refs[2 + 3 * rounds_y :]
    copies = [
        pltpu.make_async_copy(source, target, sems.at[i])
        for i, (source, target) in enumerate(
            ((dire_any, dire), (sol_any, sol), (den_any, den), (lab_any, lab))
        )
    ]
    for copy in copies:
        copy.start()
    sub = rows_of((8, 128))
    even_x, even_y = is_even("gx"), is_even("gy")
    for copy in copies:
        copy.wait()

    def masked(x):
        label = lab[x]
        keep = jnp.where(label == 1, 0.0, 1.0).astype(f32)
        keep_last = jnp.where(label >= 1, 0.0, 1.0).astype(f32)
        fields = [dire[0, x] * keep, dire[1, x] * keep, dire[2, x] * keep_last]
        return fields + [sol[0, x], sol[1, x], sol[2, x], den[x]]

    for t in range(2):
        planes = {x: masked(x) for x in (2 * t, 2 * t + 1, 2 * t + 4, 2 * t + 5)}
        for f in range(7):
            for i in (2 * t, 2 * t + 1):
                low, high = planes[i][f], planes[i + 4][f]
                halves[0][f, i] = jnp.where(even_x, high, low)
                halves[1][f, i] = jnp.where(even_x, low, high)
            tiles = []
            for i in (2 * t, 2 * t + 4):
                p, q = planes[i][f], planes[i + 1][f]
                low = jnp.where(sub < 4, p[0:8], roll(q[0:8], 4, 0))
                high = jnp.where(sub < 4, roll(p[8:16], 4, 0), q[8:16])
                tiles.append((jnp.where(even_y, high, low), jnp.where(even_y, low, high)))
            for s in range(rounds_y):
                rows, corner0, corner1 = packs[3 * s : 3 * s + 3]
                low, high = tiles[0][s], tiles[1][s]
                rows[f, t] = low
                rows[f, t + 2] = high
                corner0[f, t] = jnp.where(even_x, high, low)
                corner1[f, t] = jnp.where(even_x, low, high)


def extend(counts, half0, half1, got0, got1, *refs):
    nx, ny, nz = counts
    sides, (ext, ends, send0, send1) = refs[:-4], refs[-4:]
    sub = rows_of((8, 128))
    lane = lanes_of((24, 128))
    lows = lanes_of((8, 128)) % 8 < 4
    ix, iy = lax.axis_index("gx"), lax.axis_index("gy")
    even_y, even_z = is_even("gy"), is_even("gz")
    x_ok = ((ix > 0).astype(f32), (ix < nx - 1).astype(f32))
    y_ok = ((iy > 0).astype(f32), (iy < ny - 1).astype(f32))

    def body(blocks, order):
        def strip(which, f, t):
            tiles = []
            for s in range(len(sides) // 3):
                rows, corner0, corner1 = sides[3 * s : 3 * s + 3]
                ref = rows if which is None else (corner0, corner1)[order[which]]
                tiles.append(ref[f, t])
            keep = 1.0 if which is None else x_ok[which]
            other = tiles[-1]
            low = jnp.where(even_y, other, tiles[0]) * (y_ok[0] * keep)
            high = jnp.where(even_y, tiles[0], other) * (y_ok[1] * keep)
            return low, high

        for f in range(7):
            packed = None
            for X in range(16):
                own = blocks[X // 4][f, X % 4]
                which = None
                if X < 4:
                    which, t = 0, X // 2
                elif X >= 12:
                    which, t = 1, (X - 12) // 2
                else:
                    t = (X - 4) // 2
                if which is not None:
                    own = own * x_ok[which]
                low, high = strip(which, f, t)
                if X % 2 == 0:
                    low = roll(low, 4, 0)
                else:
                    high = roll(high, 4, 0)
                plane = jnp.concatenate([own, jnp.where(sub < 4, high, low)], axis=0)
                ext[f, X] = plane
                turned = roll(plane, 8 * X + 4, 1)
                packed = turned if X == 0 else jnp.where(lane >= 8 * X, turned, packed)
            ends[f] = packed
        for j in range(ZTILES):
            tiles = []
            for t in (j, j + ZTILES):
                tiles.append(ends[t // 3, 8 * (t % 3) : 8 * (t % 3) + 8] if t < 21 else None)
            up, down = tiles[0], tiles[0]
            if tiles[1] is not None:
                up = jnp.where(lows, tiles[0], roll(tiles[1], 4, 1))
                down = jnp.where(lows, roll(tiles[1], -4, 1), tiles[0])
            send0[j] = jnp.where(even_z, up, down)
            send1[j] = jnp.where(even_z, down, up)

    @pl.when(ix % 2 == 0)
    def _():
        body((got1, half1, half0, got0), (1, 0))

    @pl.when(ix % 2 == 1)
    def _():
        body((got0, half0, half1, got1), (0, 1))


def inverse_sums(counts, main, side):
    shape = (24, 128)
    row, lane = rows_of(shape), lanes_of(shape)
    nx, ny, nz = counts
    base_x = lax.axis_index("gx") * 8 - HALO
    base_y = lax.axis_index("gy") * 16
    base_z = lax.axis_index("gz") * 128

    def folded(place, limit):
        def inside(p):
            return jnp.where((p >= 0) & (p < limit), 1.0, 0.0).astype(f32)

        return [inside(place)] + [inside(place - k) + inside(place + k) for k in range(1, RAD + 1)]

    along_y = folded(jnp.where(row < 16 + HALO, row, row - 24) + base_y, ny * 16)

    def partial(along_z):
        table = []
        for a in range(RAD + 1):
            total = jnp.zeros(shape, f32)
            for b in range(RAD + 1):
                line = None
                for k in range(RAD + 1):
                    w = cone(a, b, k)
                    if w > 0:
                        line = w * along_z[k] if line is None else line + w * along_z[k]
                if line is not None:
                    total = total + along_y[b] * line
            table.append(total)
        return table

    def finish(total, along_x, along_z):
        inner = along_x[0] * along_y[0] * along_z[0] > 0
        return jnp.where(inner, 1.0 / jnp.where(inner, total, 1.0), 0.0)

    along_z = folded(lane + base_z, nz * 128)
    table = partial(along_z)
    for X in range(16):
        along_x = folded(jnp.full(shape, X, jnp.int32) + base_x, nx * 8)
        total = sum(along_x[a] * table[a] for a in range(RAD + 1))
        main[X] = finish(total, along_x, along_z)
    place = lane % 8
    along_x = folded(lane // 8 + base_x, nx * 8)
    for s, shift in enumerate((-4, 124)):
        along_z = folded(place + (base_z + shift), nz * 128)
        table = partial(along_z)
        total = sum(along_x[a] * table[a] for a in range(RAD + 1))
        side[s] = finish(total, along_x, along_z)


def apply_operator(nz, ext, got0, got1, res, lab, image, inverse, sums, around, shifts):
    lane = lanes_of((24, 128))
    fields = (0, 1, 2, 6)
    iz = lax.axis_index("gz")
    even = is_even("gz")
    lows = lanes_of((8, 128)) % 8 < 4
    keep = jnp.where(lows, (iz > 0).astype(f32), (iz < nz - 1).astype(f32))
    for j in range(ZTILES):
        zero, one = got0[j], got1[j]
        below, above = jnp.where(even, one, zero), jnp.where(even, zero, one)
        for t in (j, j + ZTILES):
            if t < 21:
                if t != j:
                    below, above = roll(below, -4, 1), roll(above, 4, 1)
                around[t // 3, 8 * (t % 3) : 8 * (t % 3) + 8] = jnp.where(lows, below, above) * keep
    parts = [jnp.zeros((8, 128), f32) for _ in range(4)]
    for plane_at in range(10):
        X = plane_at + 3
        for g, f in enumerate(fields):
            value = ext[f, X]
            near = roll(around[f], 124 - 8 * X, 1)
            if g == 3:
                stiff = stiff_floor + (1.0 - stiff_floor) * value * value * value
                value = jnp.where(value > 0, stiff, 0.0)
                stiff = stiff_floor + (1.0 - stiff_floor) * near * near * near
                near = jnp.where(near > 0, stiff, 0.0)
            up = roll(jnp.where(lane == 0, near, value), -1, 1)
            down = roll(jnp.where(lane == 127, near, value), 1, 1)
            for z, plane in enumerate((down, value, up)):
                for y in range(3):
                    shifts[g, y, z, plane_at] = roll(plane, 1 - y, 0)[0:16]
        x = plane_at - 2
        if x < 0:
            continue
        n = x + 1
        for at in (slice(0, 8), slice(8, 16)):
            mid = [shifts[g, 1, 1, n, at] for g in range(4)]
            classes = {1: [None] * 3, 2: [None] * 3, 3: [None] * 3}
            faces = [None] * 3
            edges = [None] * 3
            corners = None

            def add(old, new):
                return new if old is None else old + new

            for o in neighbour_offsets:
                near = [shifts[g, 1 + o[1], 1 + o[2], n + o[0], at] for g in range(4)]
                norm = sum(abs(c) for c in o)
                weight = mid[3] + near[3]
                d = [mid[c] - near[c] for c in range(3)]
                acc = classes[norm]
                if norm == 1:
                    c0 = [c for c in range(3) if o[c] != 0][0]
                    faces[c0] = add(faces[c0], near[3])
                    for c in range(3):
                        acc[c] = add(acc[c], weight * (d[c] + d[c] if c == c0 else d[c]))
                else:
                    along = None
                    for c in range(3):
                        if o[c] != 0:
                            term = d[c]
                            if along is None:
                                along, sign = term, o[c]
                            else:
                                along = along + term if o[c] == sign else along - term
                    along = along * (1.0 / norm)
                    for c in range(3):
                        if o[c] == 0:
                            pulled = d[c]
                        elif o[c] == sign:
                            pulled = d[c] + along
                        else:
                            pulled = d[c] - along
                        acc[c] = add(acc[c], weight * pulled)
                    if norm == 2:
                        c0 = [c for c in range(3) if o[c] == 0][0]
                        edges[c0] = add(edges[c0], near[3])
                    else:
                        corners = add(corners, near[3])
            s0 = mid[3]
            all_faces = faces[0] + faces[1] + faces[2]
            all_edges = edges[0] + edges[1] + edges[2]
            common = (all_faces + 6.0 * s0) + 0.75 * (all_edges + 12.0 * s0) + (4.0 / 9.0) * (corners + 8.0 * s0)
            label = lab[x, at]
            for c in range(3):
                diag = 0.5 * (common + (faces[c] + 2.0 * s0) - 0.25 * (edges[c] + 4.0 * s0))
                fixed = (label == 1) if c < 2 else (label >= 1)
                total = 0.5 * classes[1][c] + 0.25 * classes[2][c] + (1.0 / 6.0) * classes[3][c]
                total = jnp.where(fixed, 0.0, total)
                inv = 1.0 / jnp.where(fixed, 1.0, diag)
                r = res[c, x, at]
                zeta = r * inv
                scaled = total * inv
                image[c, x, at] = total
                inverse[c, x, at] = inv
                parts[0] = parts[0] + r * zeta
                parts[1] = parts[1] + mid[c] * total
                parts[2] = parts[2] + r * scaled
                parts[3] = parts[3] + total * scaled
    place = lanes_of((1, 128)) // 32
    row = None
    for k in range(4):
        part = parts[k] + roll(parts[k], 64, 1)
        part = jnp.sum(part + roll(part, 32, 1), axis=0, keepdims=True)
        row = part if k == 0 else jnp.where(place == k, part, row)
    sums[...] = jnp.broadcast_to(row[None], sums.shape)


def quadratic(d, o):
    norm = sum(abs(c) for c in o)
    square = d[0] * d[0] + d[1] * d[1] + d[2] * d[2]
    along, sign = None, 1
    for c in range(3):
        if o[c] != 0:
            if along is None:
                along, sign = d[c], o[c]
            else:
                along = along + d[c] if o[c] == sign else along - d[c]
    if norm == 1:
        return square + along * along
    return (1.0 / norm) * square + (1.0 / (norm * norm)) * (along * along)


pairs = [((1, 0, 0), 0, 0, 0, 0)]
pairs += [((a, 1, 0), 0, 0, 2, 2) for a in (-1, 0, 1)]
pairs += [((a, 0, 1), 0, 0, 1, 1) for a in (-1, 0, 1)]
pairs += [((a, 1, 1), 0, 0, 3, 3) for a in (-1, 0, 1)]
pairs += [((a, -1, 1), 2, 2, 1, 1) for a in (-1, 0, 1)]
energy_scale = -penalty * (1.0 - stiff_floor) * 0.5


def plus(old, new):
    return new if old is None else old + new


def finish_step(
    ext, ends, around, total, image, inverse, res, dire, hinv, hside,
    new_sol_any, new_res_any, new_dir_any, sens_any, us, lines, new_sol, new_res, new_dir, sens, sems,
):
    lane = lanes_of((24, 128))
    lows = lane % 8 < 4
    copies = [
        pltpu.make_async_copy(source, target, sems.at[i])
        for i, (source, target) in enumerate(
            ((new_res, new_res_any), (new_dir, new_dir_any), (new_sol, new_sol_any), (sens, sens_any))
        )
    ]
    spread = jnp.broadcast_to(jnp.sum(total[...], axis=0), (8, 128))
    tot = jnp.sum(jnp.where(lanes_of((8, 128)) // 32 == rows_of((8, 128)), spread, 0.0), axis=1, keepdims=True)
    rz, pq, s2, s3 = (tot[k : k + 1] for k in range(4))
    alpha = rz / pq
    beta = (rz + alpha * (alpha * s3 - 2.0 * s2)) / rz

    for x in range(8):
        for c in range(3):
            r = res[c, x] - alpha * image[c, x]
            new_res[c, x] = r
            new_dir[c, x] = r * inverse[c, x] + beta * dire[c, x]
    copies[0].start()
    copies[1].start()

    halos, lefts, rights = [], [], []
    for c in range(3):
        halo_u = around[3 + c] + alpha * around[c]
        own_u = ends[3 + c] + alpha * ends[c]
        halos.append(halo_u)
        lefts.append(jnp.where(lows, halo_u, own_u))
        rights.append(jnp.where(lows, own_u, halo_u))
    sides, side_low = [], None
    den_left = jnp.where(lows, around[6], ends[6])
    den_right = jnp.where(lows, ends[6], around[6])
    for s, (u, den) in enumerate(((lefts, den_left), (rights, den_right))):
        up = [roll(v, -1, 1) for v in u]
        moved = [u, up, [roll(v, -1, 0) for v in u], [roll(v, -1, 0) for v in up]]
        far = {}
        acc = {}
        for o, field0, frame0, field1, frame1 in pairs:
            key = (field1, o[0])
            if key not in far:
                far[key] = [roll(v, -8 * o[0], 1) for v in moved[field1]]
            g = quadratic([moved[field0][c] - far[key][c] for c in range(3)], o)
            acc[frame0, 0] = plus(acc.get((frame0, 0)), g)
            acc[frame1, o[0]] = plus(acc.get((frame1, o[0])), g)
        frames = []
        for frame in range(4):
            value = None
            for a in (-1, 0, 1):
                if (frame, a) in acc:
                    value = plus(value, roll(acc[frame, a], 8 * a, 1))
            frames.append(value)
        up = frames[1] + roll(frames[3], 1, 0)
        if s == 0:
            side_low = up
        energy = frames[0] + roll(frames[2], 1, 0) + roll(up, 1, 1)
        sides.append(energy_scale * (den * den) * energy * hside[s])
    ends_scaled = jnp.where(lows, sides[0], sides[1])

    def iterate(X):
        for c in range(3):
            u = ext[3 + c, X] + alpha * ext[c, X]
            if 4 <= X < 12:
                new_sol[c, X - 4] = u[0:16]
            near = roll(halos[c], 124 - 8 * X, 1)
            up = roll(jnp.where(lane == 0, near, u), -1, 1)
            us[0, c, X] = u
            us[1, c, X] = up
            us[2, c, X] = roll(u, -1, 0)
            us[3, c, X] = roll(up, -1, 0)
        if X == 11:
            copies[2].start()

    acc = [[[None] * 3 for _ in range(4)] for _ in range(16)]

    def pair_up(X):
        for r in range(3):
            at = slice(8 * r, 8 * r + 8)
            for o, field0, frame0, field1, frame1 in pairs:
                to = X + o[0]
                if not 0 <= to < 16 or not (1 <= X < 15 or 1 <= to < 15):
                    continue
                g = quadratic([us[field0, c, X, at] - us[field1, c, to, at] for c in range(3)], o)
                if 1 <= X < 15:
                    acc[X][frame0][r] = plus(acc[X][frame0][r], g)
                if 1 <= to < 15:
                    acc[to][frame1][r] = plus(acc[to][frame1][r], g)

    def filter_lines(X):
        frames = [jnp.concatenate(tiles, axis=0) for tiles in acc[X]]
        up = frames[1] + roll(frames[3], 1, 0)
        below = roll(side_low, 127 - (8 * X + 3), 1)
        up = roll(jnp.where(lane == 127, below, up), 1, 1)
        den = ext[6, X]
        energy = frames[0] + roll(frames[2], 1, 0) + up
        s = energy_scale * (den * den) * energy * hinv[X]
        near = roll(ends_scaled, 124 - 8 * X, 1)
        fold = [s]
        for k in range(1, RAD + 1):
            above = roll(jnp.where(lane < k, near, s), -k, 1)
            under = roll(jnp.where(lane >= 128 - k, near, s), k, 1)
            fold.append(above + under)
        for k in range(RAD + 1):
            lines[X, k] = fold[k]

    def filter_rows(x):
        groups = {}
        for a in range(RAD + 1):
            for k in range(RAD + 1):
                if cone(a, 0, k) > 0:
                    both = lines[x + HALO + a, k]
                    if a > 0:
                        both = both + lines[x + HALO - a, k]
                    groups[a * a + k * k] = plus(groups.get(a * a + k * k), both)
        value = None
        for b in range(RAD + 1):
            row = None
            for d, group in groups.items():
                w = RAD + 0.5 - math.sqrt(d + b * b)
                if w > 0:
                    row = plus(row, w * group)
            value = row if b == 0 else value + roll(row, b, 0) + roll(row, -b, 0)
        sens[x] = value[0:16]

    for X in range(16 + 1):
        if X < 16:
            iterate(X)
        if X >= 1:
            pair_up(X - 1)
        if X >= 3:
            filter_lines(X - 2)
        if X - 2 - 2 * RAD - 1 >= 0:
            filter_rows(X - 2 - 2 * RAD - 1)
    copies[3].start()
    for copy in copies:
        copy.wait()


def partner(place, turn, count):
    other = (place ^ 1) if turn == 0 else ((place + 1) ^ 1) - 1
    return other if 0 <= other < count else None


def swap_pairs(counts, turns):
    pairs = []
    for flat in range(math.prod(counts)):
        rest, place = flat, []
        for count in reversed(counts):
            place.insert(0, rest % count)
            rest //= count
        to = [p if t is None else partner(p, t, c) for p, t, c in zip(place, turns, counts)]
        if None in to:
            continue
        index = 0
        for p, count in zip(to, counts):
            index = index * count + p
        pairs.append((flat, index))
    return pairs


def per_device(mesh_shape, solution, residual, direction, density, labels):
    nx, ny, nz = (mesh_shape[a] for a in AXES)
    half, full, corner = (7, 4, 16, 128), (7, 4, 8, 128), (7, 2, 8, 128)
    rounds_y = 1 if ny == 2 else 2
    field, flat = (3, 8, 16, 128), (8, 16, 128)
    packed = call(
        functools.partial(pack_faces, rounds_y),
        [half, half] + [full, corner, corner] * rounds_y,
        solution, direction, density, labels,
        far=range(4),
        scratch=[
            pltpu.VMEM(field, f32), pltpu.VMEM(field, f32), pltpu.VMEM(flat, f32),
            pltpu.VMEM(flat, jnp.int32), pltpu.SemaphoreType.DMA((4,)),
        ],
    )
    halves = packed[:2]
    plane = ("gx", "gy")
    got = [lax.ppermute(halves[r], plane, swap_pairs((nx, ny), (r, None))) for r in (0, 1)]
    strips = []
    for s in range(rounds_y):
        for array, turn in zip(packed[2 + 3 * s : 5 + 3 * s], (None, 0, 1)):
            strips.append(lax.ppermute(array, plane, swap_pairs((nx, ny), (turn, s))))
    hinv, hside = call(functools.partial(inverse_sums, (nx, ny, nz)), [(16, 24, 128), (2, 24, 128)])
    zend = (ZTILES, 8, 128)
    ext, ends, *sends = call(
        functools.partial(extend, (nx, ny, nz)),
        [(7, 16, 24, 128), (7, 24, 128), zend, zend],
        *halves, *got, *strips,
    )
    ends_got = [lax.ppermute(sends[r], "gz", swap_pairs((nz,), (r,))) for r in (0, 1)]
    image, inverse, sums, around = call(
        functools.partial(apply_operator, nz),
        [field, field, (nx * ny * nz, 1, 128), (7, 24, 128)],
        ext, *ends_got, residual, labels,
        scratch=[pltpu.VMEM((4, 3, 3, 10, 16, 128), f32)],
    )
    total = lax.all_to_all(sums, AXES, 0, 0)
    return tuple(
        call(
            finish_step,
            [field, field, field, flat],
            ext, ends, around, total, image, inverse, residual, direction, hinv, hside,
            scratch=[
                pltpu.VMEM((4, 3, 16, 24, 128), f32), pltpu.VMEM((16, RAD + 1, 24, 128), f32),
                pltpu.VMEM(field, f32), pltpu.VMEM(field, f32), pltpu.VMEM(field, f32),
                pltpu.VMEM(flat, f32), pltpu.SemaphoreType.DMA((4,)),
            ],
            far_out=True,
        )
    )


def solution(mesh):
    wide, flat = P(None, "gx", "gy", "gz"), P("gx", "gy", "gz")
    return jax.shard_map(
        functools.partial(per_device, dict(mesh.shape)),
        mesh=mesh,
        in_specs=(wide, wide, wide, flat, flat),
        out_specs=(wide, wide, wide, flat),
        check_vma=False,
    )
```

```python
import functools
import math

import jax
import jax.numpy as jnp
from jax import lax
from jax.experimental import pallas as pl
from jax.experimental.pallas import tpu as pltpu
from jax.sharding import PartitionSpec as P

RAD = 3
HALO = RAD + 1
ZTILES = 11
stiff_floor = 0.001
penalty = 3.0
f32 = jnp.float32
neighbour_offsets = [
    (off_x, off_y, off_z)
    for off_x in (-1, 0, 1)
    for off_y in (-1, 0, 1)
    for off_z in (-1, 0, 1)
    if (off_x, off_y, off_z) != (0, 0, 0)
]
AXES = ("gx", "gy", "gz")


def cone(a, b, k):
    return max(0.0, RAD + 0.5 - math.sqrt(a * a + b * b + k * k))


def lanes_of(shape):
    return lax.broadcasted_iota(jnp.int32, shape, len(shape) - 1)


def rows_of(shape):
    return lax.broadcasted_iota(jnp.int32, shape, len(shape) - 2)


def roll(value, amount, axis):
    size = value.shape[axis]
    amount = amount % size
    return value if amount == 0 else pltpu.roll(value, amount, axis)


def call(body, outs, *args, scratch=(), cost=20000, far=(), far_out=False):
    args = [
        pltpu.with_memory_space_constraint(a, pltpu.HBM) if i in far else a for i, a in enumerate(args)
    ]
    return pl.pallas_call(
        body,
        out_shape=[jax.ShapeDtypeStruct(shape, f32) for shape in outs],
        in_specs=[
            pl.BlockSpec(memory_space=pl.ANY if i in far else pltpu.VMEM) for i in range(len(args))
        ],
        out_specs=[pl.BlockSpec(memory_space=pl.ANY if far_out else pltpu.VMEM)] * len(outs),
        scratch_shapes=list(scratch),
        compiler_params=pltpu.CompilerParams(vmem_limit_bytes=24 * 1024 * 1024),
        cost_estimate=pl.CostEstimate(flops=cost * 1000, bytes_accessed=cost, transcendentals=0),
    )(*args)


def is_even(axis):
    return lax.axis_index(axis) % 2 == 0


def pack_faces(rounds_y, sol_any, dire_any, den_any, lab_any, *refs):
    halves, packs = refs[:2], refs[2 : 2 + 3 * rounds_y]
    sol, dire, den, lab, sems = refs[2 + 3 * rounds_y :]
    copies = [
        pltpu.make_async_copy(source, target, sems.at[i])
        for i, (source, target) in enumerate(
            ((dire_any, dire), (sol_any, sol), (den_any, den), (lab_any, lab))
        )
    ]
    for copy in copies:
        copy.start()
    sub = rows_of((8, 128))
    even_x, even_y = is_even("gx"), is_even("gy")
    for copy in copies:
        copy.wait()

    def masked(x):
        label = lab[x]
        keep = jnp.where(label == 1, 0.0, 1.0).astype(f32)
        keep_last = jnp.where(label >= 1, 0.0, 1.0).astype(f32)
        fields = [dire[0, x] * keep, dire[1, x] * keep, dire[2, x] * keep_last]
        return fields + [sol[0, x], sol[1, x], sol[2, x], den[x]]

    for t in range(2):
        planes = {x: masked(x) for x in (2 * t, 2 * t + 1, 2 * t + 4, 2 * t + 5)}
        for f in range(7):
            for i in (2 * t, 2 * t + 1):
                low, high = planes[i][f], planes[i + 4][f]
                halves[0][f, i] = jnp.where(even_x, high, low)
                halves[1][f, i] = jnp.where(even_x, low, high)
            tiles = []
            for i in (2 * t, 2 * t + 4):
                p, q = planes[i][f], planes[i + 1][f]
                low = jnp.where(sub < 4, p[0:8], roll(q[0:8], 4, 0))
                high = jnp.where(sub < 4, roll(p[8:16], 4, 0), q[8:16])
                tiles.append((jnp.where(even_y, high, low), jnp.where(even_y, low, high)))
            for s in range(rounds_y):
                rows, corner0, corner1 = packs[3 * s : 3 * s + 3]
                low, high = tiles[0][s], tiles[1][s]
                rows[f, t] = low
                rows[f, t + 2] = high
                corner0[f, t] = jnp.where(even_x, high, low)
                corner1[f, t] = jnp.where(even_x, low, high)


def extend(counts, half0, half1, got0, got1, *refs):
    nx, ny, nz = counts
    sides, (ext, ends, send0, send1) = refs[:-4], refs[-4:]
    sub = rows_of((8, 128))
    lane = lanes_of((24, 128))
    lows = lanes_of((8, 128)) % 8 < 4
    ix, iy = lax.axis_index("gx"), lax.axis_index("gy")
    even_y, even_z = is_even("gy"), is_even("gz")
    x_ok = ((ix > 0).astype(f32), (ix < nx - 1).astype(f32))
    y_ok = ((iy > 0).astype(f32), (iy < ny - 1).astype(f32))

    def body(blocks, order):
        def strip(which, f, t):
            tiles = []
            for s in range(len(sides) // 3):
                rows, corner0, corner1 = sides[3 * s : 3 * s + 3]
                ref = rows if which is None else (corner0, corner1)[order[which]]
                tiles.append(ref[f, t])
            keep = 1.0 if which is None else x_ok[which]
            other = tiles[-1]
            low = jnp.where(even_y, other, tiles[0]) * (y_ok[0] * keep)
            high = jnp.where(even_y, tiles[0], other) * (y_ok[1] * keep)
            return low, high

        for f in range(7):
            packed = None
            for X in range(16):
                own = blocks[X // 4][f, X % 4]
                which = None
                if X < 4:
                    which, t = 0, X // 2
                elif X >= 12:
                    which, t = 1, (X - 12) // 2
                else:
                    t = (X - 4) // 2
                if which is not None:
                    own = own * x_ok[which]
                low, high = strip(which, f, t)
                if X % 2 == 0:
                    low = roll(low, 4, 0)
                else:
                    high = roll(high, 4, 0)
                plane = jnp.concatenate([own, jnp.where(sub < 4, high, low)], axis=0)
                ext[f, X] = plane
                turned = roll(plane, 8 * X + 4, 1)
                packed = turned if X == 0 else jnp.where(lane >= 8 * X, turned, packed)
            ends[f] = packed
        for j in range(ZTILES):
            tiles = []
            for t in (j, j + ZTILES):
                tiles.append(ends[t // 3, 8 * (t % 3) : 8 * (t % 3) + 8] if t < 21 else None)
            up, down = tiles[0], tiles[0]
            if tiles[1] is not None:
                up = jnp.where(lows, tiles[0], roll(tiles[1], 4, 1))
                down = jnp.where(lows, roll(tiles[1], -4, 1), tiles[0])
            send0[j] = jnp.where(even_z, up, down)
            send1[j] = jnp.where(even_z, down, up)

    @pl.when(ix % 2 == 0)
    def _():
        body((got1, half1, half0, got0), (1, 0))

    @pl.when(ix % 2 == 1)
    def _():
        body((got0, half0, half1, got1), (0, 1))


def inverse_sums(counts, main, side):
    shape = (24, 128)
    row, lane = rows_of(shape), lanes_of(shape)
    nx, ny, nz = counts
    base_x = lax.axis_index("gx") * 8 - HALO
    base_y = lax.axis_index("gy") * 16
    base_z = lax.axis_index("gz") * 128

    def folded(place, limit):
        def inside(p):
            return jnp.where((p >= 0) & (p < limit), 1.0, 0.0).astype(f32)

        return [inside(place)] + [inside(place - k) + inside(place + k) for k in range(1, RAD + 1)]

    along_y = folded(jnp.where(row < 16 + HALO, row, row - 24) + base_y, ny * 16)

    def partial(along_z):
        table = []
        for a in range(RAD + 1):
            total = jnp.zeros(shape, f32)
            for b in range(RAD + 1):
                line = None
                for k in range(RAD + 1):
                    w = cone(a, b, k)
                    if w > 0:
                        line = w * along_z[k] if line is None else line + w * along_z[k]
                if line is not None:
                    total = total + along_y[b] * line
            table.append(total)
        return table

    def finish(total, along_x, along_z):
        inner = along_x[0] * along_y[0] * along_z[0] > 0
        return jnp.where(inner, 1.0 / jnp.where(inner, total, 1.0), 0.0)

    along_z = folded(lane + base_z, nz * 128)
    table = partial(along_z)
    for X in range(16):
        along_x = folded(jnp.full(shape, X, jnp.int32) + base_x, nx * 8)
        total = sum(along_x[a] * table[a] for a in range(RAD + 1))
        main[X] = finish(total, along_x, along_z)
    place = lane % 8
    along_x = folded(lane // 8 + base_x, nx * 8)
    for s, shift in enumerate((-4, 124)):
        along_z = folded(place + (base_z + shift), nz * 128)
        table = partial(along_z)
        total = sum(along_x[a] * table[a] for a in range(RAD + 1))
        side[s] = finish(total, along_x, along_z)


def apply_operator(nz, ext, got0, got1, res, lab, image, inverse, sums, around, shifts):
    lane = lanes_of((24, 128))
    fields = (0, 1, 2, 6)
    iz = lax.axis_index("gz")
    even = is_even("gz")
    lows = lanes_of((8, 128)) % 8 < 4
    keep = jnp.where(lows, (iz > 0).astype(f32), (iz < nz - 1).astype(f32))
    for j in range(ZTILES):
        zero, one = got0[j], got1[j]
        below, above = jnp.where(even, one, zero), jnp.where(even, zero, one)
        for t in (j, j + ZTILES):
            if t < 21:
                if t != j:
                    below, above = roll(below, -4, 1), roll(above, 4, 1)
                around[t // 3, 8 * (t % 3) : 8 * (t % 3) + 8] = jnp.where(lows, below, above) * keep
    parts = [jnp.zeros((16, 128), f32) for _ in range(4)]
    for plane_at in range(10):
        X = plane_at + 3
        for g, f in enumerate(fields):
            value = ext[f, X]
            near = roll(around[f], 124 - 8 * X, 1)
            if g == 3:
                stiff = stiff_floor + (1.0 - stiff_floor) * value * value * value
                value = jnp.where(value > 0, stiff, 0.0)
                stiff = stiff_floor + (1.0 - stiff_floor) * near * near * near
                near = jnp.where(near > 0, stiff, 0.0)
            up = roll(jnp.where(lane == 0, near, value), -1, 1)
            down = roll(jnp.where(lane == 127, near, value), 1, 1)
            for z, plane in enumerate((down, value, up)):
                for y in range(3):
                    shifts[g, y, z, plane_at] = roll(plane, 1 - y, 0)[0:16]
        x = plane_at - 2
        if x < 0:
            continue
        n = x + 1
        mid = [shifts[g, 1, 1, n] for g in range(4)]
        classes = {1: [None] * 3, 2: [None] * 3, 3: [None] * 3}
        faces = [None] * 3
        edges = [None] * 3
        corners = None

        def add(old, new):
            return new if old is None else old + new

        for o in neighbour_offsets:
            near = [shifts[g, 1 + o[1], 1 + o[2], n + o[0]] for g in range(4)]
            norm = sum(abs(c) for c in o)
            weight = mid[3] + near[3]
            d = [mid[c] - near[c] for c in range(3)]
            acc = classes[norm]
            if norm == 1:
                c0 = [c for c in range(3) if o[c] != 0][0]
                faces[c0] = add(faces[c0], near[3])
                for c in range(3):
                    acc[c] = add(acc[c], weight * (d[c] + d[c] if c == c0 else d[c]))
            else:
                along = None
                for c in range(3):
                    if o[c] != 0:
                        term = d[c]
                        if along is None:
                            along, sign = term, o[c]
                        else:
                            along = along + term if o[c] == sign else along - term
                along = along * (1.0 / norm)
                for c in range(3):
                    if o[c] == 0:
                        pulled = d[c]
                    elif o[c] == sign:
                        pulled = d[c] + along
                    else:
                        pulled = d[c] - along
                    acc[c] = add(acc[c], weight * pulled)
                if norm == 2:
                    c0 = [c for c in range(3) if o[c] == 0][0]
                    edges[c0] = add(edges[c0], near[3])
                else:
                    corners = add(corners, near[3])
        s0 = mid[3]
        all_faces = faces[0] + faces[1] + faces[2]
        all_edges = edges[0] + edges[1] + edges[2]
        common = (all_faces + 6.0 * s0) + 0.75 * (all_edges + 12.0 * s0) + (4.0 / 9.0) * (corners + 8.0 * s0)
        label = lab[x]
        for c in range(3):
            diag = 0.5 * (common + (faces[c] + 2.0 * s0) - 0.25 * (edges[c] + 4.0 * s0))
            fixed = (label == 1) if c < 2 else (label >= 1)
            total = 0.5 * classes[1][c] + 0.25 * classes[2][c] + (1.0 / 6.0) * classes[3][c]
            total = jnp.where(fixed, 0.0, total)
            inv = 1.0 / jnp.where(fixed, 1.0, diag)
            r = res[c, x]
            zeta = r * inv
            scaled = total * inv
            image[c, x] = total
            inverse[c, x] = inv
            parts[0] = parts[0] + r * zeta
            parts[1] = parts[1] + mid[c] * total
            parts[2] = parts[2] + r * scaled
            parts[3] = parts[3] + total * scaled
    place = lanes_of((1, 128)) // 32
    row = None
    for k in range(4):
        part = parts[k][0:8] + parts[k][8:16]
        part = part + roll(part, 64, 1)
        part = jnp.sum(part + roll(part, 32, 1), axis=0, keepdims=True)
        row = part if k == 0 else jnp.where(place == k, part, row)
    sums[...] = jnp.broadcast_to(row[None], sums.shape)


def quadratic(d, o):
    norm = sum(abs(c) for c in o)
    square = d[0] * d[0] + d[1] * d[1] + d[2] * d[2]
    along, sign = None, 1
    for c in range(3):
        if o[c] != 0:
            if along is None:
                along, sign = d[c], o[c]
            else:
                along = along + d[c] if o[c] == sign else along - d[c]
    if norm == 1:
        return square + along * along
    return (1.0 / norm) * square + (1.0 / (norm * norm)) * (along * along)


pairs = [((1, 0, 0), 0, 0, 0, 0)]
pairs += [((a, 1, 0), 0, 0, 2, 2) for a in (-1, 0, 1)]
pairs += [((a, 0, 1), 0, 0, 1, 1) for a in (-1, 0, 1)]
pairs += [((a, 1, 1), 0, 0, 3, 3) for a in (-1, 0, 1)]
pairs += [((a, -1, 1), 2, 2, 1, 1) for a in (-1, 0, 1)]
energy_scale = -penalty * (1.0 - stiff_floor) * 0.5


def plus(old, new):
    return new if old is None else old + new


def finish_step(
    ext, ends, around, total, image, inverse, res, dire, hinv, hside,
    new_sol_any, new_res_any, new_dir_any, sens_any, us, lines, new_sol, new_res, new_dir, sens, sems,
):
    lane = lanes_of((24, 128))
    lows = lane % 8 < 4
    copies = [
        pltpu.make_async_copy(source, target, sems.at[i])
        for i, (source, target) in enumerate(
            ((new_res, new_res_any), (new_dir, new_dir_any), (new_sol, new_sol_any), (sens, sens_any))
        )
    ]
    spread = jnp.broadcast_to(jnp.sum(total[...], axis=0), (8, 128))
    tot = jnp.sum(jnp.where(lanes_of((8, 128)) // 32 == rows_of((8, 128)), spread, 0.0), axis=1, keepdims=True)
    rz, pq, s2, s3 = (tot[k : k + 1] for k in range(4))
    alpha = rz / pq
    beta = (rz + alpha * (alpha * s3 - 2.0 * s2)) / rz

    for x in range(8):
        for c in range(3):
            r = res[c, x] - alpha * image[c, x]
            new_res[c, x] = r
            new_dir[c, x] = r * inverse[c, x] + beta * dire[c, x]
    copies[0].start()
    copies[1].start()

    halos, lefts, rights = [], [], []
    for c in range(3):
        halo_u = around[3 + c] + alpha * around[c]
        own_u = ends[3 + c] + alpha * ends[c]
        halos.append(halo_u)
        lefts.append(jnp.where(lows, halo_u, own_u))
        rights.append(jnp.where(lows, own_u, halo_u))
    sides, side_low = [], None
    den_left = jnp.where(lows, around[6], ends[6])
    den_right = jnp.where(lows, ends[6], around[6])
    for s, (u, den) in enumerate(((lefts, den_left), (rights, den_right))):
        up = [roll(v, -1, 1) for v in u]
        moved = [u, up, [roll(v, -1, 0) for v in u], [roll(v, -1, 0) for v in up]]
        far = {}
        acc = {}
        for o, field0, frame0, field1, frame1 in pairs:
            key = (field1, o[0])
            if key not in far:
                far[key] = [roll(v, -8 * o[0], 1) for v in moved[field1]]
            g = quadratic([moved[field0][c] - far[key][c] for c in range(3)], o)
            acc[frame0, 0] = plus(acc.get((frame0, 0)), g)
            acc[frame1, o[0]] = plus(acc.get((frame1, o[0])), g)
        frames = []
        for frame in range(4):
            value = None
            for a in (-1, 0, 1):
                if (frame, a) in acc:
                    value = plus(value, roll(acc[frame, a], 8 * a, 1))
            frames.append(value)
        up = frames[1] + roll(frames[3], 1, 0)
        if s == 0:
            side_low = up
        energy = frames[0] + roll(frames[2], 1, 0) + roll(up, 1, 1)
        sides.append(energy_scale * (den * den) * energy * hside[s])
    ends_scaled = jnp.where(lows, sides[0], sides[1])

    def iterate(X):
        for c in range(3):
            u = ext[3 + c, X] + alpha * ext[c, X]
            if 4 <= X < 12:
                new_sol[c, X - 4] = u[0:16]
            near = roll(halos[c], 124 - 8 * X, 1)
            up = roll(jnp.where(lane == 0, near, u), -1, 1)
            us[0, c, X] = u
            us[1, c, X] = up
            us[2, c, X] = roll(u, -1, 0)
            us[3, c, X] = roll(up, -1, 0)
        if X == 11:
            copies[2].start()

    acc = [[[None] * 3 for _ in range(4)] for _ in range(16)]

    def pair_up(X):
        for r in range(3):
            at = slice(8 * r, 8 * r + 8)
            for o, field0, frame0, field1, frame1 in pairs:
                to = X + o[0]
                if not 0 <= to < 16 or not (1 <= X < 15 or 1 <= to < 15):
                    continue
                g = quadratic([us[field0, c, X, at] - us[field1, c, to, at] for c in range(3)], o)
                if 1 <= X < 15:
                    acc[X][frame0][r] = plus(acc[X][frame0][r], g)
                if 1 <= to < 15:
                    acc[to][frame1][r] = plus(acc[to][frame1][r], g)

    def filter_lines(X):
        frames = [jnp.concatenate(tiles, axis=0) for tiles in acc[X]]
        up = frames[1] + roll(frames[3], 1, 0)
        below = roll(side_low, 127 - (8 * X + 3), 1)
        up = roll(jnp.where(lane == 127, below, up), 1, 1)
        den = ext[6, X]
        energy = frames[0] + roll(frames[2], 1, 0) + up
        s = energy_scale * (den * den) * energy * hinv[X]
        near = roll(ends_scaled, 124 - 8 * X, 1)
        fold = [s]
        for k in range(1, RAD + 1):
            above = roll(jnp.where(lane < k, near, s), -k, 1)
            under = roll(jnp.where(lane >= 128 - k, near, s), k, 1)
            fold.append(above + under)
        for k in range(RAD + 1):
            lines[X, k] = fold[k]

    def filter_rows(x):
        groups = {}
        for a in range(RAD + 1):
            for k in range(RAD + 1):
                if cone(a, 0, k) > 0:
                    both = lines[x + HALO + a, k]
                    if a > 0:
                        both = both + lines[x + HALO - a, k]
                    groups[a * a + k * k] = plus(groups.get(a * a + k * k), both)
        value = None
        for b in range(RAD + 1):
            row = None
            for d, group in groups.items():
                w = RAD + 0.5 - math.sqrt(d + b * b)
                if w > 0:
                    row = plus(row, w * group)
            value = row if b == 0 else value + roll(row, b, 0) + roll(row, -b, 0)
        sens[x] = value[0:16]

    for X in range(16 + 1):
        if X < 16:
            iterate(X)
        if X >= 1:
            pair_up(X - 1)
        if X >= 3:
            filter_lines(X - 2)
        if X - 2 - 2 * RAD - 1 >= 0:
            filter_rows(X - 2 - 2 * RAD - 1)
    copies[3].start()
    for copy in copies:
        copy.wait()


def partner(place, turn, count):
    other = (place ^ 1) if turn == 0 else ((place + 1) ^ 1) - 1
    return other if 0 <= other < count else None


def swap_pairs(counts, turns):
    pairs = []
    for flat in range(math.prod(counts)):
        rest, place = flat, []
        for count in reversed(counts):
            place.insert(0, rest % count)
            rest //= count
        to = [p if t is None else partner(p, t, c) for p, t, c in zip(place, turns, counts)]
        if None in to:
            continue
        index = 0
        for p, count in zip(to, counts):
            index = index * count + p
        pairs.append((flat, index))
    return pairs


def per_device(mesh_shape, solution, residual, direction, density, labels):
    nx, ny, nz = (mesh_shape[a] for a in AXES)
    half, full, corner = (7, 4, 16, 128), (7, 4, 8, 128), (7, 2, 8, 128)
    rounds_y = 1 if ny == 2 else 2
    field, flat = (3, 8, 16, 128), (8, 16, 128)
    packed = call(
        functools.partial(pack_faces, rounds_y),
        [half, half] + [full, corner, corner] * rounds_y,
        solution, direction, density, labels,
        far=range(4),
        scratch=[
            pltpu.VMEM(field, f32), pltpu.VMEM(field, f32), pltpu.VMEM(flat, f32),
            pltpu.VMEM(flat, jnp.int32), pltpu.SemaphoreType.DMA((4,)),
        ],
    )
    halves = packed[:2]
    plane = ("gx", "gy")
    got = [lax.ppermute(halves[r], plane, swap_pairs((nx, ny), (r, None))) for r in (0, 1)]
    strips = []
    for s in range(rounds_y):
        for array, turn in zip(packed[2 + 3 * s : 5 + 3 * s], (None, 0, 1)):
            strips.append(lax.ppermute(array, plane, swap_pairs((nx, ny), (turn, s))))
    hinv, hside = call(functools.partial(inverse_sums, (nx, ny, nz)), [(16, 24, 128), (2, 24, 128)])
    zend = (ZTILES, 8, 128)
    ext, ends, *sends = call(
        functools.partial(extend, (nx, ny, nz)),
        [(7, 16, 24, 128), (7, 24, 128), zend, zend],
        *halves, *got, *strips,
    )
    ends_got = [lax.ppermute(sends[r], "gz", swap_pairs((nz,), (r,))) for r in (0, 1)]
    image, inverse, sums, around = call(
        functools.partial(apply_operator, nz),
        [field, field, (nx * ny * nz, 1, 128), (7, 24, 128)],
        ext, *ends_got, residual, labels,
        scratch=[pltpu.VMEM((4, 3, 3, 10, 16, 128), f32)],
    )
    total = lax.all_to_all(sums, AXES, 0, 0)
    return tuple(
        call(
            finish_step,
            [field, field, field, flat],
            ext, ends, around, total, image, inverse, residual, direction, hinv, hside,
            scratch=[
                pltpu.VMEM((4, 3, 16, 24, 128), f32), pltpu.VMEM((16, RAD + 1, 24, 128), f32),
                pltpu.VMEM(field, f32), pltpu.VMEM(field, f32), pltpu.VMEM(field, f32),
                pltpu.VMEM(flat, f32), pltpu.SemaphoreType.DMA((4,)),
            ],
            far_out=True,
        )
    )


def solution(mesh):
    wide, flat = P(None, "gx", "gy", "gz"), P("gx", "gy", "gz")
    return jax.shard_map(
        functools.partial(per_device, dict(mesh.shape)),
        mesh=mesh,
        in_specs=(wide, wide, wide, flat, flat),
        out_specs=(wide, wide, wide, flat),
        check_vma=False,
    )
```

```python
import functools
import math

import jax
import jax.numpy as jnp
from jax import lax
from jax.experimental import pallas as pl
from jax.experimental.pallas import tpu as pltpu
from jax.sharding import PartitionSpec as P

RAD = 3
HALO = RAD + 1
ZTILES = 11
stiff_floor = 0.001
penalty = 3.0
f32 = jnp.float32
neighbour_offsets = [
    (off_x, off_y, off_z)
    for off_x in (-1, 0, 1)
    for off_y in (-1, 0, 1)
    for off_z in (-1, 0, 1)
    if (off_x, off_y, off_z) != (0, 0, 0)
]
AXES = ("gx", "gy", "gz")


def cone(a, b, k):
    return max(0.0, RAD + 0.5 - math.sqrt(a * a + b * b + k * k))


def lanes_of(shape):
    return lax.broadcasted_iota(jnp.int32, shape, len(shape) - 1)


def rows_of(shape):
    return lax.broadcasted_iota(jnp.int32, shape, len(shape) - 2)


def roll(value, amount, axis):
    size = value.shape[axis]
    amount = amount % size
    return value if amount == 0 else pltpu.roll(value, amount, axis)


def call(body, outs, *args, scratch=(), cost=20000, far=(), far_out=False):
    args = [
        pltpu.with_memory_space_constraint(a, pltpu.HBM) if i in far else a for i, a in enumerate(args)
    ]
    return pl.pallas_call(
        body,
        out_shape=[jax.ShapeDtypeStruct(shape, f32) for shape in outs],
        in_specs=[
            pl.BlockSpec(memory_space=pl.ANY if i in far else pltpu.VMEM) for i in range(len(args))
        ],
        out_specs=[pl.BlockSpec(memory_space=pl.ANY if far_out else pltpu.VMEM)] * len(outs),
        scratch_shapes=list(scratch),
        compiler_params=pltpu.CompilerParams(vmem_limit_bytes=24 * 1024 * 1024),
        cost_estimate=pl.CostEstimate(flops=cost * 1000, bytes_accessed=cost, transcendentals=0),
    )(*args)


def is_even(axis):
    return lax.axis_index(axis) % 2 == 0


def pack_faces(rounds_y, sol_any, dire_any, den_any, lab_any, *refs):
    halves, packs = refs[:2], refs[2 : 2 + 3 * rounds_y]
    sol, dire, den, lab, sems = refs[2 + 3 * rounds_y :]
    copies = [
        pltpu.make_async_copy(source, target, sems.at[i])
        for i, (source, target) in enumerate(
            ((dire_any, dire), (sol_any, sol), (den_any, den), (lab_any, lab))
        )
    ]
    for copy in copies:
        copy.start()
    sub = rows_of((8, 128))
    even_x, even_y = is_even("gx"), is_even("gy")
    for copy in copies:
        copy.wait()

    def masked(x):
        label = lab[x]
        keep = jnp.where(label == 1, 0.0, 1.0).astype(f32)
        keep_last = jnp.where(label >= 1, 0.0, 1.0).astype(f32)
        fields = [dire[0, x] * keep, dire[1, x] * keep, dire[2, x] * keep_last]
        return fields + [sol[0, x], sol[1, x], sol[2, x], den[x]]

    for t in range(2):
        planes = {x: masked(x) for x in (2 * t, 2 * t + 1, 2 * t + 4, 2 * t + 5)}
        for f in range(7):
            for i in (2 * t, 2 * t + 1):
                low, high = planes[i][f], planes[i + 4][f]
                halves[0][f, i] = jnp.where(even_x, high, low)
                halves[1][f, i] = jnp.where(even_x, low, high)
            tiles = []
            for i in (2 * t, 2 * t + 4):
                p, q = planes[i][f], planes[i + 1][f]
                low = jnp.where(sub < 4, p[0:8], roll(q[0:8], 4, 0))
                high = jnp.where(sub < 4, roll(p[8:16], 4, 0), q[8:16])
                tiles.append((jnp.where(even_y, high, low), jnp.where(even_y, low, high)))
            for s in range(rounds_y):
                rows, corner0, corner1 = packs[3 * s : 3 * s + 3]
                low, high = tiles[0][s], tiles[1][s]
                rows[f, t] = low
                rows[f, t + 2] = high
                corner0[f, t] = jnp.where(even_x, high, low)
                corner1[f, t] = jnp.where(even_x, low, high)


def extend(counts, half0, half1, got0, got1, *refs):
    nx, ny, nz = counts
    sides, (ext, ends, send1, send0) = refs[:-4], refs[-4:]
    sub = rows_of((8, 128))
    lane = lanes_of((24, 128))
    lows = lanes_of((8, 128)) % 8 < 4
    ix, iy = lax.axis_index("gx"), lax.axis_index("gy")
    even_y, even_z = is_even("gy"), is_even("gz")
    x_ok = ((ix > 0).astype(f32), (ix < nx - 1).astype(f32))
    y_ok = ((iy > 0).astype(f32), (iy < ny - 1).astype(f32))

    def body(blocks, order):
        def strip(which, f, t):
            tiles = []
            for s in range(len(sides) // 3):
                rows, corner0, corner1 = sides[3 * s : 3 * s + 3]
                ref = rows if which is None else (corner0, corner1)[order[which]]
                tiles.append(ref[f, t])
            keep = 1.0 if which is None else x_ok[which]
            other = tiles[-1]
            low = jnp.where(even_y, other, tiles[0]) * (y_ok[0] * keep)
            high = jnp.where(even_y, tiles[0], other) * (y_ok[1] * keep)
            return low, high

        for f in range(7):
            packed = None
            for X in range(16):
                own = blocks[X // 4][f, X % 4]
                which = None
                if X < 4:
                    which, t = 0, X // 2
                elif X >= 12:
                    which, t = 1, (X - 12) // 2
                else:
                    t = (X - 4) // 2
                if which is not None:
                    own = own * x_ok[which]
                low, high = strip(which, f, t)
                if X % 2 == 0:
                    low = roll(low, 4, 0)
                else:
                    high = roll(high, 4, 0)
                plane = jnp.concatenate([own, jnp.where(sub < 4, high, low)], axis=0)
                ext[f, X] = plane
                turned = roll(plane, 8 * X + 4, 1)
                packed = turned if X == 0 else jnp.where(lane >= 8 * X, turned, packed)
            ends[f] = packed
        for j in range(ZTILES):
            tiles = []
            for t in (j, j + ZTILES):
                tiles.append(ends[t // 3, 8 * (t % 3) : 8 * (t % 3) + 8] if t < 21 else None)
            up, down = tiles[0], tiles[0]
            if tiles[1] is not None:
                up = jnp.where(lows, tiles[0], roll(tiles[1], 4, 1))
                down = jnp.where(lows, roll(tiles[1], -4, 1), tiles[0])
            send0[j] = jnp.where(even_z, up, down)
            send1[j] = jnp.where(even_z, down, up)

    @pl.when(ix % 2 == 0)
    def _():
        body((got1, half1, half0, got0), (1, 0))

    @pl.when(ix % 2 == 1)
    def _():
        body((got0, half0, half1, got1), (0, 1))


def inverse_sums(counts, main, side):
    shape = (24, 128)
    row, lane = rows_of(shape), lanes_of(shape)
    nx, ny, nz = counts
    base_x = lax.axis_index("gx") * 8 - HALO
    base_y = lax.axis_index("gy") * 16
    base_z = lax.axis_index("gz") * 128

    def folded(place, limit):
        def inside(p):
            return jnp.where((p >= 0) & (p < limit), 1.0, 0.0).astype(f32)

        return [inside(place)] + [inside(place - k) + inside(place + k) for k in range(1, RAD + 1)]

    along_y = folded(jnp.where(row < 16 + HALO, row, row - 24) + base_y, ny * 16)

    def partial(along_z):
        table = []
        for a in range(RAD + 1):
            total = jnp.zeros(shape, f32)
            for b in range(RAD + 1):
                line = None
                for k in range(RAD + 1):
                    w = cone(a, b, k)
                    if w > 0:
                        line = w * along_z[k] if line is None else line + w * along_z[k]
                if line is not None:
                    total = total + along_y[b] * line
            table.append(total)
        return table

    def finish(total, along_x, along_z):
        inner = along_x[0] * along_y[0] * along_z[0] > 0
        return jnp.where(inner, 1.0 / jnp.where(inner, total, 1.0), 0.0)

    along_z = folded(lane + base_z, nz * 128)
    table = partial(along_z)
    for X in range(16):
        along_x = folded(jnp.full(shape, X, jnp.int32) + base_x, nx * 8)
        total = sum(along_x[a] * table[a] for a in range(RAD + 1))
        main[X] = finish(total, along_x, along_z)
    place = lane % 8
    along_x = folded(lane // 8 + base_x, nx * 8)
    for s, shift in enumerate((-4, 124)):
        along_z = folded(place + (base_z + shift), nz * 128)
        table = partial(along_z)
        total = sum(along_x[a] * table[a] for a in range(RAD + 1))
        side[s] = finish(total, along_x, along_z)


def apply_operator(nz, ext, got1, got0, res, lab, image, inverse, sums, around, shifts):
    lane = lanes_of((24, 128))
    fields = (0, 1, 2, 6)
    iz = lax.axis_index("gz")
    even = is_even("gz")
    lows = lanes_of((8, 128)) % 8 < 4
    keep = jnp.where(lows, (iz > 0).astype(f32), (iz < nz - 1).astype(f32))
    for j in range(ZTILES):
        zero, one = got0[j], got1[j]
        below, above = jnp.where(even, one, zero), jnp.where(even, zero, one)
        for t in (j, j + ZTILES):
            if t < 21:
                if t != j:
                    below, above = roll(below, -4, 1), roll(above, 4, 1)
                around[t // 3, 8 * (t % 3) : 8 * (t % 3) + 8] = jnp.where(lows, below, above) * keep
    parts = [jnp.zeros((16, 128), f32) for _ in range(4)]
    for plane_at in range(10):
        X = plane_at + 3
        for g, f in enumerate(fields):
            value = ext[f, X]
            near = roll(around[f], 124 - 8 * X, 1)
            if g == 3:
                stiff = stiff_floor + (1.0 - stiff_floor) * value * value * value
                value = jnp.where(value > 0, stiff, 0.0)
                stiff = stiff_floor + (1.0 - stiff_floor) * near * near * near
                near = jnp.where(near > 0, stiff, 0.0)
            up = roll(jnp.where(lane == 0, near, value), -1, 1)
            down = roll(jnp.where(lane == 127, near, value), 1, 1)
            for z, plane in enumerate((down, value, up)):
                for y in range(3):
                    shifts[g, y, z, plane_at] = roll(plane, 1 - y, 0)[0:16]
        x = plane_at - 2
        if x < 0:
            continue
        n = x + 1
        mid = [shifts[g, 1, 1, n] for g in range(4)]
        classes = {1: [None] * 3, 2: [None] * 3, 3: [None] * 3}
        faces = [None] * 3
        edges = [None] * 3
        corners = None

        def add(old, new):
            return new if old is None else old + new

        for o in neighbour_offsets:
            near = [shifts[g, 1 + o[1], 1 + o[2], n + o[0]] for g in range(4)]
            norm = sum(abs(c) for c in o)
            weight = mid[3] + near[3]
            d = [mid[c] - near[c] for c in range(3)]
            acc = classes[norm]
            if norm == 1:
                c0 = [c for c in range(3) if o[c] != 0][0]
                faces[c0] = add(faces[c0], near[3])
                for c in range(3):
                    acc[c] = add(acc[c], weight * (d[c] + d[c] if c == c0 else d[c]))
            else:
                along = None
                for c in range(3):
                    if o[c] != 0:
                        term = d[c]
                        if along is None:
                            along, sign = term, o[c]
                        else:
                            along = along + term if o[c] == sign else along - term
                along = along * (1.0 / norm)
                for c in range(3):
                    if o[c] == 0:
                        pulled = d[c]
                    elif o[c] == sign:
                        pulled = d[c] + along
                    else:
                        pulled = d[c] - along
                    acc[c] = add(acc[c], weight * pulled)
                if norm == 2:
                    c0 = [c for c in range(3) if o[c] == 0][0]
                    edges[c0] = add(edges[c0], near[3])
                else:
                    corners = add(corners, near[3])
        s0 = mid[3]
        all_faces = faces[0] + faces[1] + faces[2]
        all_edges = edges[0] + edges[1] + edges[2]
        common = (all_faces + 6.0 * s0) + 0.75 * (all_edges + 12.0 * s0) + (4.0 / 9.0) * (corners + 8.0 * s0)
        label = lab[x]
        for c in range(3):
            diag = 0.5 * (common + (faces[c] + 2.0 * s0) - 0.25 * (edges[c] + 4.0 * s0))
            fixed = (label == 1) if c < 2 else (label >= 1)
            total = 0.5 * classes[1][c] + 0.25 * classes[2][c] + (1.0 / 6.0) * classes[3][c]
            total = jnp.where(fixed, 0.0, total)
            inv = 1.0 / jnp.where(fixed, 1.0, diag)
            r = res[c, x]
            zeta = r * inv
            scaled = total * inv
            image[c, x] = total
            inverse[c, x] = inv
            parts[0] = parts[0] + r * zeta
            parts[1] = parts[1] + mid[c] * total
            parts[2] = parts[2] + r * scaled
            parts[3] = parts[3] + total * scaled
    place = lanes_of((1, 128)) // 32
    row = None
    for k in range(4):
        part = parts[k][0:8] + parts[k][8:16]
        part = part + roll(part, 64, 1)
        part = jnp.sum(part + roll(part, 32, 1), axis=0, keepdims=True)
        row = part if k == 0 else jnp.where(place == k, part, row)
    sums[...] = jnp.broadcast_to(row[None], sums.shape)


def quadratic(d, o):
    norm = sum(abs(c) for c in o)
    square = d[0] * d[0] + d[1] * d[1] + d[2] * d[2]
    along, sign = None, 1
    for c in range(3):
        if o[c] != 0:
            if along is None:
                along, sign = d[c], o[c]
            else:
                along = along + d[c] if o[c] == sign else along - d[c]
    if norm == 1:
        return square + along * along
    return (1.0 / norm) * square + (1.0 / (norm * norm)) * (along * along)


pairs = [((1, 0, 0), 0, 0, 0, 0)]
pairs += [((a, 1, 0), 0, 0, 2, 2) for a in (-1, 0, 1)]
pairs += [((a, 0, 1), 0, 0, 1, 1) for a in (-1, 0, 1)]
pairs += [((a, 1, 1), 0, 0, 3, 3) for a in (-1, 0, 1)]
pairs += [((a, -1, 1), 2, 2, 1, 1) for a in (-1, 0, 1)]
energy_scale = -penalty * (1.0 - stiff_floor) * 0.5


def plus(old, new):
    return new if old is None else old + new


def finish_step(
    ext, ends, around, total, image, inverse, res, dire, hinv, hside,
    new_sol_any, new_res_any, new_dir_any, sens_any, us, lines, new_sol, new_res, new_dir, sens, sems,
):
    lane = lanes_of((24, 128))
    lows = lane % 8 < 4
    copies = [
        pltpu.make_async_copy(source, target, sems.at[i])
        for i, (source, target) in enumerate(
            ((new_res, new_res_any), (new_dir, new_dir_any), (new_sol, new_sol_any), (sens, sens_any))
        )
    ]
    spread = jnp.broadcast_to(jnp.sum(total[...], axis=0), (8, 128))
    tot = jnp.sum(jnp.where(lanes_of((8, 128)) // 32 == rows_of((8, 128)), spread, 0.0), axis=1, keepdims=True)
    rz, pq, s2, s3 = (tot[k : k + 1] for k in range(4))
    alpha = rz / pq
    beta = (rz + alpha * (alpha * s3 - 2.0 * s2)) / rz

    for x in range(8):
        for c in range(3):
            r = res[c, x] - alpha * image[c, x]
            new_res[c, x] = r
            new_dir[c, x] = r * inverse[c, x] + beta * dire[c, x]
    copies[0].start()
    copies[1].start()

    halos, lefts, rights = [], [], []
    for c in range(3):
        halo_u = around[3 + c] + alpha * around[c]
        own_u = ends[3 + c] + alpha * ends[c]
        halos.append(halo_u)
        lefts.append(jnp.where(lows, halo_u, own_u))
        rights.append(jnp.where(lows, own_u, halo_u))
    sides, side_low = [], None
    den_left = jnp.where(lows, around[6], ends[6])
    den_right = jnp.where(lows, ends[6], around[6])
    for s, (u, den) in enumerate(((lefts, den_left), (rights, den_right))):
        up = [roll(v, -1, 1) for v in u]
        moved = [u, up, [roll(v, -1, 0) for v in u], [roll(v, -1, 0) for v in up]]
        far = {}
        acc = {}
        for o, field0, frame0, field1, frame1 in pairs:
            key = (field1, o[0])
            if key not in far:
                far[key] = [roll(v, -8 * o[0], 1) for v in moved[field1]]
            g = quadratic([moved[field0][c] - far[key][c] for c in range(3)], o)
            acc[frame0, 0] = plus(acc.get((frame0, 0)), g)
            acc[frame1, o[0]] = plus(acc.get((frame1, o[0])), g)
        frames = []
        for frame in range(4):
            value = None
            for a in (-1, 0, 1):
                if (frame, a) in acc:
                    value = plus(value, roll(acc[frame, a], 8 * a, 1))
            frames.append(value)
        up = frames[1] + roll(frames[3], 1, 0)
        if s == 0:
            side_low = up
        energy = frames[0] + roll(frames[2], 1, 0) + roll(up, 1, 1)
        sides.append(energy_scale * (den * den) * energy * hside[s])
    ends_scaled = jnp.where(lows, sides[0], sides[1])

    def iterate(X):
        for c in range(3):
            u = ext[3 + c, X] + alpha * ext[c, X]
            if 4 <= X < 12:
                new_sol[c, X - 4] = u[0:16]
            near = roll(halos[c], 124 - 8 * X, 1)
            up = roll(jnp.where(lane == 0, near, u), -1, 1)
            us[0, c, X] = u
            us[1, c, X] = up
            us[2, c, X] = roll(u, -1, 0)
            us[3, c, X] = roll(up, -1, 0)
        if X == 11:
            copies[2].start()

    acc = [[[None] * 3 for _ in range(4)] for _ in range(16)]

    def pair_up(X):
        for r in range(3):
            at = slice(8 * r, 8 * r + 8)
            for o, field0, frame0, field1, frame1 in pairs:
                to = X + o[0]
                if not 0 <= to < 16 or not (1 <= X < 15 or 1 <= to < 15):
                    continue
                g = quadratic([us[field0, c, X, at] - us[field1, c, to, at] for c in range(3)], o)
                if 1 <= X < 15:
                    acc[X][frame0][r] = plus(acc[X][frame0][r], g)
                if 1 <= to < 15:
                    acc[to][frame1][r] = plus(acc[to][frame1][r], g)

    def filter_lines(X):
        frames = [jnp.concatenate(tiles, axis=0) for tiles in acc[X]]
        up = frames[1] + roll(frames[3], 1, 0)
        below = roll(side_low, 127 - (8 * X + 3), 1)
        up = roll(jnp.where(lane == 127, below, up), 1, 1)
        den = ext[6, X]
        energy = frames[0] + roll(frames[2], 1, 0) + up
        s = energy_scale * (den * den) * energy * hinv[X]
        near = roll(ends_scaled, 124 - 8 * X, 1)
        fold = [s]
        for k in range(1, RAD + 1):
            above = roll(jnp.where(lane < k, near, s), -k, 1)
            under = roll(jnp.where(lane >= 128 - k, near, s), k, 1)
            fold.append(above + under)
        for k in range(RAD + 1):
            lines[X, k] = fold[k]

    def filter_rows(x):
        groups = {}
        for a in range(RAD + 1):
            for k in range(RAD + 1):
                if cone(a, 0, k) > 0:
                    both = lines[x + HALO + a, k]
                    if a > 0:
                        both = both + lines[x + HALO - a, k]
                    groups[a * a + k * k] = plus(groups.get(a * a + k * k), both)
        value = None
        for b in range(RAD + 1):
            row = None
            for d, group in groups.items():
                w = RAD + 0.5 - math.sqrt(d + b * b)
                if w > 0:
                    row = plus(row, w * group)
            value = row if b == 0 else value + roll(row, b, 0) + roll(row, -b, 0)
        sens[x] = value[0:16]

    for X in range(16 + 1):
        if X < 16:
            iterate(X)
        if X >= 1:
            pair_up(X - 1)
        if X >= 3:
            filter_lines(X - 2)
        if X - 2 - 2 * RAD - 1 >= 0:
            filter_rows(X - 2 - 2 * RAD - 1)
    copies[3].start()
    for copy in copies:
        copy.wait()


def partner(place, turn, count):
    other = (place ^ 1) if turn == 0 else ((place + 1) ^ 1) - 1
    return other if 0 <= other < count else None


def swap_pairs(counts, turns):
    pairs = []
    for flat in range(math.prod(counts)):
        rest, place = flat, []
        for count in reversed(counts):
            place.insert(0, rest % count)
            rest //= count
        to = [p if t is None else partner(p, t, c) for p, t, c in zip(place, turns, counts)]
        if None in to:
            continue
        index = 0
        for p, count in zip(to, counts):
            index = index * count + p
        pairs.append((flat, index))
    return pairs


def per_device(mesh_shape, solution, residual, direction, density, labels):
    nx, ny, nz = (mesh_shape[a] for a in AXES)
    half, full, corner = (7, 4, 16, 128), (7, 4, 8, 128), (7, 2, 8, 128)
    rounds_y = 1 if ny == 2 else 2
    field, flat = (3, 8, 16, 128), (8, 16, 128)
    packed = call(
        functools.partial(pack_faces, rounds_y),
        [half, half] + [full, corner, corner] * rounds_y,
        solution, direction, density, labels,
        far=range(4),
        scratch=[
            pltpu.VMEM(field, f32), pltpu.VMEM(field, f32), pltpu.VMEM(flat, f32),
            pltpu.VMEM(flat, jnp.int32), pltpu.SemaphoreType.DMA((4,)),
        ],
    )
    halves = packed[:2]
    plane = ("gx", "gy")
    got = [lax.ppermute(halves[r], plane, swap_pairs((nx, ny), (r, None))) for r in (0, 1)]
    strips = []
    for s in range(rounds_y):
        for array, turn in zip(packed[2 + 3 * s : 5 + 3 * s], (None, 0, 1)):
            strips.append(lax.ppermute(array, plane, swap_pairs((nx, ny), (turn, s))))
    hinv, hside = call(functools.partial(inverse_sums, (nx, ny, nz)), [(16, 24, 128), (2, 24, 128)])
    zend = (ZTILES, 8, 128)
    ext, ends, *sends = call(
        functools.partial(extend, (nx, ny, nz)),
        [(7, 16, 24, 128), (7, 24, 128), zend, zend],
        *halves, *got, *strips,
    )
    later = lax.ppermute(sends[0], "gz", swap_pairs((nz,), (1,)))
    first = lax.ppermute(sends[1], "gz", swap_pairs((nz,), (0,)))
    ends_got = [later, first]
    image, inverse, sums, around = call(
        functools.partial(apply_operator, nz),
        [field, field, (nx * ny * nz, 1, 128), (7, 24, 128)],
        ext, *ends_got, residual, labels,
        scratch=[pltpu.VMEM((4, 3, 3, 10, 16, 128), f32)],
    )
    total = lax.all_to_all(sums, AXES, 0, 0)
    return tuple(
        call(
            finish_step,
            [field, field, field, flat],
            ext, ends, around, total, image, inverse, residual, direction, hinv, hside,
            scratch=[
                pltpu.VMEM((4, 3, 16, 24, 128), f32), pltpu.VMEM((16, RAD + 1, 24, 128), f32),
                pltpu.VMEM(field, f32), pltpu.VMEM(field, f32), pltpu.VMEM(field, f32),
                pltpu.VMEM(flat, f32), pltpu.SemaphoreType.DMA((4,)),
            ],
            far_out=True,
        )
    )


def solution(mesh):
    wide, flat = P(None, "gx", "gy", "gz"), P("gx", "gy", "gz")
    return jax.shard_map(
        functools.partial(per_device, dict(mesh.shape)),
        mesh=mesh,
        in_specs=(wide, wide, wide, flat, flat),
        out_specs=(wide, wide, wide, flat),
        check_vma=False,
    )
```

```python
import functools
import math

import jax
import jax.numpy as jnp
from jax import lax
from jax.experimental import pallas as pl
from jax.experimental.pallas import tpu as pltpu
from jax.sharding import PartitionSpec as P

RAD = 3
HALO = RAD + 1
ZTILES = 11
stiff_floor = 0.001
penalty = 3.0
f32 = jnp.float32
neighbour_offsets = [
    (off_x, off_y, off_z)
    for off_x in (-1, 0, 1)
    for off_y in (-1, 0, 1)
    for off_z in (-1, 0, 1)
    if (off_x, off_y, off_z) != (0, 0, 0)
]
AXES = ("gx", "gy", "gz")


def cone(a, b, k):
    return max(0.0, RAD + 0.5 - math.sqrt(a * a + b * b + k * k))


def lanes_of(shape):
    return lax.broadcasted_iota(jnp.int32, shape, len(shape) - 1)


def rows_of(shape):
    return lax.broadcasted_iota(jnp.int32, shape, len(shape) - 2)


def roll(value, amount, axis):
    size = value.shape[axis]
    amount = amount % size
    return value if amount == 0 else pltpu.roll(value, amount, axis)


def call(body, outs, *args, scratch=(), cost=20000, far=(), far_out=False):
    args = [
        pltpu.with_memory_space_constraint(a, pltpu.HBM) if i in far else a for i, a in enumerate(args)
    ]
    return pl.pallas_call(
        body,
        out_shape=[jax.ShapeDtypeStruct(shape, f32) for shape in outs],
        in_specs=[
            pl.BlockSpec(memory_space=pl.ANY if i in far else pltpu.VMEM) for i in range(len(args))
        ],
        out_specs=[pl.BlockSpec(memory_space=pl.ANY if far_out else pltpu.VMEM)] * len(outs),
        scratch_shapes=list(scratch),
        compiler_params=pltpu.CompilerParams(vmem_limit_bytes=24 * 1024 * 1024),
        cost_estimate=pl.CostEstimate(flops=cost * 1000, bytes_accessed=cost, transcendentals=0),
    )(*args)


def is_even(axis):
    return lax.axis_index(axis) % 2 == 0


def pack_faces(rounds_y, sol_any, dire_any, den_any, lab_any, *refs):
    halves, packs = refs[:2], refs[2 : 2 + 3 * rounds_y]
    sol, dire, den, lab, sems = refs[2 + 3 * rounds_y :]
    copies = [
        pltpu.make_async_copy(source, target, sems.at[i])
        for i, (source, target) in enumerate(
            ((dire_any, dire), (sol_any, sol), (den_any, den), (lab_any, lab))
        )
    ]
    for copy in copies:
        copy.start()
    sub = rows_of((8, 128))
    even_x, even_y = is_even("gx"), is_even("gy")
    for copy in copies:
        copy.wait()

    def masked(x):
        label = lab[x]
        keep = jnp.where(label == 1, 0.0, 1.0).astype(f32)
        keep_last = jnp.where(label >= 1, 0.0, 1.0).astype(f32)
        fields = [dire[0, x] * keep, dire[1, x] * keep, dire[2, x] * keep_last]
        return fields + [sol[0, x], sol[1, x], sol[2, x], den[x]]

    for t in range(2):
        planes = {x: masked(x) for x in (2 * t, 2 * t + 1, 2 * t + 4, 2 * t + 5)}
        for f in range(7):
            for i in (2 * t, 2 * t + 1):
                low, high = planes[i][f], planes[i + 4][f]
                halves[0][f, i] = jnp.where(even_x, high, low)
                halves[1][f, i] = jnp.where(even_x, low, high)
            tiles = []
            for i in (2 * t, 2 * t + 4):
                p, q = planes[i][f], planes[i + 1][f]
                low = jnp.where(sub < 4, p[0:8], roll(q[0:8], 4, 0))
                high = jnp.where(sub < 4, roll(p[8:16], 4, 0), q[8:16])
                tiles.append((jnp.where(even_y, high, low), jnp.where(even_y, low, high)))
            for s in range(rounds_y):
                rows, corner0, corner1 = packs[3 * s : 3 * s + 3]
                low, high = tiles[0][s], tiles[1][s]
                rows[f, t] = low
                rows[f, t + 2] = high
                corner0[f, t] = jnp.where(even_x, high, low)
                corner1[f, t] = jnp.where(even_x, low, high)


def extend(counts, half0, half1, got1, got0, *refs):
    nx, ny, nz = counts
    sides, (ext, ends, send1, send0) = refs[:-4], refs[-4:]
    sub = rows_of((8, 128))
    lane = lanes_of((24, 128))
    lows = lanes_of((8, 128)) % 8 < 4
    ix, iy = lax.axis_index("gx"), lax.axis_index("gy")
    even_y, even_z = is_even("gy"), is_even("gz")
    x_ok = ((ix > 0).astype(f32), (ix < nx - 1).astype(f32))
    y_ok = ((iy > 0).astype(f32), (iy < ny - 1).astype(f32))

    def body(blocks, order):
        def strip(which, f, t):
            tiles = []
            for s in range(len(sides) // 3):
                rows, corner1, corner0 = sides[3 * s : 3 * s + 3]
                ref = rows if which is None else (corner0, corner1)[order[which]]
                tiles.append(ref[f, t])
            keep = 1.0 if which is None else x_ok[which]
            other = tiles[-1]
            low = jnp.where(even_y, other, tiles[0]) * (y_ok[0] * keep)
            high = jnp.where(even_y, tiles[0], other) * (y_ok[1] * keep)
            return low, high

        for f in range(7):
            packed = None
            for X in range(16):
                own = blocks[X // 4][f, X % 4]
                which = None
                if X < 4:
                    which, t = 0, X // 2
                elif X >= 12:
                    which, t = 1, (X - 12) // 2
                else:
                    t = (X - 4) // 2
                if which is not None:
                    own = own * x_ok[which]
                low, high = strip(which, f, t)
                if X % 2 == 0:
                    low = roll(low, 4, 0)
                else:
                    high = roll(high, 4, 0)
                plane = jnp.concatenate([own, jnp.where(sub < 4, high, low)], axis=0)
                ext[f, X] = plane
                turned = roll(plane, 8 * X + 4, 1)
                packed = turned if X == 0 else jnp.where(lane >= 8 * X, turned, packed)
            ends[f] = packed
        for j in range(ZTILES):
            tiles = []
            for t in (j, j + ZTILES):
                tiles.append(ends[t // 3, 8 * (t % 3) : 8 * (t % 3) + 8] if t < 21 else None)
            up, down = tiles[0], tiles[0]
            if tiles[1] is not None:
                up = jnp.where(lows, tiles[0], roll(tiles[1], 4, 1))
                down = jnp.where(lows, roll(tiles[1], -4, 1), tiles[0])
            send0[j] = jnp.where(even_z, up, down)
            send1[j] = jnp.where(even_z, down, up)

    @pl.when(ix % 2 == 0)
    def _():
        body((got1, half1, half0, got0), (1, 0))

    @pl.when(ix % 2 == 1)
    def _():
        body((got0, half0, half1, got1), (0, 1))


def inverse_sums(counts, main, side):
    shape = (24, 128)
    row, lane = rows_of(shape), lanes_of(shape)
    nx, ny, nz = counts
    base_x = lax.axis_index("gx") * 8 - HALO
    base_y = lax.axis_index("gy") * 16
    base_z = lax.axis_index("gz") * 128

    def folded(place, limit):
        def inside(p):
            return jnp.where((p >= 0) & (p < limit), 1.0, 0.0).astype(f32)

        return [inside(place)] + [inside(place - k) + inside(place + k) for k in range(1, RAD + 1)]

    along_y = folded(jnp.where(row < 16 + HALO, row, row - 24) + base_y, ny * 16)

    def partial(along_z):
        table = []
        for a in range(RAD + 1):
            total = jnp.zeros(shape, f32)
            for b in range(RAD + 1):
                line = None
                for k in range(RAD + 1):
                    w = cone(a, b, k)
                    if w > 0:
                        line = w * along_z[k] if line is None else line + w * along_z[k]
                if line is not None:
                    total = total + along_y[b] * line
            table.append(total)
        return table

    def finish(total, along_x, along_z):
        inner = along_x[0] * along_y[0] * along_z[0] > 0
        return jnp.where(inner, 1.0 / jnp.where(inner, total, 1.0), 0.0)

    along_z = folded(lane + base_z, nz * 128)
    table = partial(along_z)
    for X in range(16):
        along_x = folded(jnp.full(shape, X, jnp.int32) + base_x, nx * 8)
        total = sum(along_x[a] * table[a] for a in range(RAD + 1))
        main[X] = finish(total, along_x, along_z)
    place = lane % 8
    along_x = folded(lane // 8 + base_x, nx * 8)
    for s, shift in enumerate((-4, 124)):
        along_z = folded(place + (base_z + shift), nz * 128)
        table = partial(along_z)
        total = sum(along_x[a] * table[a] for a in range(RAD + 1))
        side[s] = finish(total, along_x, along_z)


def apply_operator(nz, ext, got1, got0, res, lab, image, inverse, sums, around, shifts):
    lane = lanes_of((24, 128))
    fields = (0, 1, 2, 6)
    iz = lax.axis_index("gz")
    even = is_even("gz")
    lows = lanes_of((8, 128)) % 8 < 4
    keep = jnp.where(lows, (iz > 0).astype(f32), (iz < nz - 1).astype(f32))
    for j in range(ZTILES):
        zero, one = got0[j], got1[j]
        below, above = jnp.where(even, one, zero), jnp.where(even, zero, one)
        for t in (j, j + ZTILES):
            if t < 21:
                if t != j:
                    below, above = roll(below, -4, 1), roll(above, 4, 1)
                around[t // 3, 8 * (t % 3) : 8 * (t % 3) + 8] = jnp.where(lows, below, above) * keep
    parts = [jnp.zeros((16, 128), f32) for _ in range(4)]
    for plane_at in range(10):
        X = plane_at + 3
        for g, f in enumerate(fields):
            value = ext[f, X]
            near = roll(around[f], 124 - 8 * X, 1)
            if g == 3:
                stiff = stiff_floor + (1.0 - stiff_floor) * value * value * value
                value = jnp.where(value > 0, stiff, 0.0)
                stiff = stiff_floor + (1.0 - stiff_floor) * near * near * near
                near = jnp.where(near > 0, stiff, 0.0)
            up = roll(jnp.where(lane == 0, near, value), -1, 1)
            down = roll(jnp.where(lane == 127, near, value), 1, 1)
            for z, plane in enumerate((down, value, up)):
                for y in range(3):
                    shifts[g, y, z, plane_at] = roll(plane, 1 - y, 0)[0:16]
        x = plane_at - 2
        if x < 0:
            continue
        n = x + 1
        mid = [shifts[g, 1, 1, n] for g in range(4)]
        classes = {1: [None] * 3, 2: [None] * 3, 3: [None] * 3}
        faces = [None] * 3
        edges = [None] * 3
        corners = None

        def add(old, new):
            return new if old is None else old + new

        for o in neighbour_offsets:
            near = [shifts[g, 1 + o[1], 1 + o[2], n + o[0]] for g in range(4)]
            norm = sum(abs(c) for c in o)
            weight = mid[3] + near[3]
            d = [mid[c] - near[c] for c in range(3)]
            acc = classes[norm]
            if norm == 1:
                c0 = [c for c in range(3) if o[c] != 0][0]
                faces[c0] = add(faces[c0], near[3])
                for c in range(3):
                    acc[c] = add(acc[c], weight * (d[c] + d[c] if c == c0 else d[c]))
            else:
                along = None
                for c in range(3):
                    if o[c] != 0:
                        term = d[c]
                        if along is None:
                            along, sign = term, o[c]
                        else:
                            along = along + term if o[c] == sign else along - term
                along = along * (1.0 / norm)
                for c in range(3):
                    if o[c] == 0:
                        pulled = d[c]
                    elif o[c] == sign:
                        pulled = d[c] + along
                    else:
                        pulled = d[c] - along
                    acc[c] = add(acc[c], weight * pulled)
                if norm == 2:
                    c0 = [c for c in range(3) if o[c] == 0][0]
                    edges[c0] = add(edges[c0], near[3])
                else:
                    corners = add(corners, near[3])
        s0 = mid[3]
        all_faces = faces[0] + faces[1] + faces[2]
        all_edges = edges[0] + edges[1] + edges[2]
        common = (all_faces + 6.0 * s0) + 0.75 * (all_edges + 12.0 * s0) + (4.0 / 9.0) * (corners + 8.0 * s0)
        label = lab[x]
        for c in range(3):
            diag = 0.5 * (common + (faces[c] + 2.0 * s0) - 0.25 * (edges[c] + 4.0 * s0))
            fixed = (label == 1) if c < 2 else (label >= 1)
            total = 0.5 * classes[1][c] + 0.25 * classes[2][c] + (1.0 / 6.0) * classes[3][c]
            total = jnp.where(fixed, 0.0, total)
            inv = 1.0 / jnp.where(fixed, 1.0, diag)
            r = res[c, x]
            zeta = r * inv
            scaled = total * inv
            image[c, x] = total
            inverse[c, x] = inv
            parts[0] = parts[0] + r * zeta
            parts[1] = parts[1] + mid[c] * total
            parts[2] = parts[2] + r * scaled
            parts[3] = parts[3] + total * scaled
    place = lanes_of((1, 128)) // 32
    row = None
    for k in range(4):
        part = parts[k][0:8] + parts[k][8:16]
        part = part + roll(part, 64, 1)
        part = jnp.sum(part + roll(part, 32, 1), axis=0, keepdims=True)
        row = part if k == 0 else jnp.where(place == k, part, row)
    sums[...] = jnp.broadcast_to(row[None], sums.shape)


def quadratic(d, o):
    norm = sum(abs(c) for c in o)
    square = d[0] * d[0] + d[1] * d[1] + d[2] * d[2]
    along, sign = None, 1
    for c in range(3):
        if o[c] != 0:
            if along is None:
                along, sign = d[c], o[c]
            else:
                along = along + d[c] if o[c] == sign else along - d[c]
    if norm == 1:
        return square + along * along
    return (1.0 / norm) * square + (1.0 / (norm * norm)) * (along * along)


pairs = [((1, 0, 0), 0, 0, 0, 0)]
pairs += [((a, 1, 0), 0, 0, 2, 2) for a in (-1, 0, 1)]
pairs += [((a, 0, 1), 0, 0, 1, 1) for a in (-1, 0, 1)]
pairs += [((a, 1, 1), 0, 0, 3, 3) for a in (-1, 0, 1)]
pairs += [((a, -1, 1), 2, 2, 1, 1) for a in (-1, 0, 1)]
energy_scale = -penalty * (1.0 - stiff_floor) * 0.5


def plus(old, new):
    return new if old is None else old + new


def finish_step(
    ext, ends, around, total, image, inverse, res, dire, hinv, hside,
    new_sol_any, new_res_any, new_dir_any, sens_any, us, lines, new_sol, new_res, new_dir, sens, sems,
):
    lane = lanes_of((24, 128))
    lows = lane % 8 < 4
    copies = [
        pltpu.make_async_copy(source, target, sems.at[i])
        for i, (source, target) in enumerate(
            ((new_res, new_res_any), (new_dir, new_dir_any), (new_sol, new_sol_any), (sens, sens_any))
        )
    ]
    spread = jnp.broadcast_to(jnp.sum(total[...], axis=0), (8, 128))
    tot = jnp.sum(jnp.where(lanes_of((8, 128)) // 32 == rows_of((8, 128)), spread, 0.0), axis=1, keepdims=True)
    rz, pq, s2, s3 = (tot[k : k + 1] for k in range(4))
    alpha = rz / pq
    beta = (rz + alpha * (alpha * s3 - 2.0 * s2)) / rz

    for x in range(8):
        for c in range(3):
            r = res[c, x] - alpha * image[c, x]
            new_res[c, x] = r
            new_dir[c, x] = r * inverse[c, x] + beta * dire[c, x]
    copies[0].start()
    copies[1].start()

    halos, lefts, rights = [], [], []
    for c in range(3):
        halo_u = around[3 + c] + alpha * around[c]
        own_u = ends[3 + c] + alpha * ends[c]
        halos.append(halo_u)
        lefts.append(jnp.where(lows, halo_u, own_u))
        rights.append(jnp.where(lows, own_u, halo_u))
    sides, side_low = [], None
    den_left = jnp.where(lows, around[6], ends[6])
    den_right = jnp.where(lows, ends[6], around[6])
    for s, (u, den) in enumerate(((lefts, den_left), (rights, den_right))):
        up = [roll(v, -1, 1) for v in u]
        moved = [u, up, [roll(v, -1, 0) for v in u], [roll(v, -1, 0) for v in up]]
        far = {}
        acc = {}
        for o, field0, frame0, field1, frame1 in pairs:
            key = (field1, o[0])
            if key not in far:
                far[key] = [roll(v, -8 * o[0], 1) for v in moved[field1]]
            g = quadratic([moved[field0][c] - far[key][c] for c in range(3)], o)
            acc[frame0, 0] = plus(acc.get((frame0, 0)), g)
            acc[frame1, o[0]] = plus(acc.get((frame1, o[0])), g)
        frames = []
        for frame in range(4):
            value = None
            for a in (-1, 0, 1):
                if (frame, a) in acc:
                    value = plus(value, roll(acc[frame, a], 8 * a, 1))
            frames.append(value)
        up = frames[1] + roll(frames[3], 1, 0)
        if s == 0:
            side_low = up
        energy = frames[0] + roll(frames[2], 1, 0) + roll(up, 1, 1)
        sides.append(energy_scale * (den * den) * energy * hside[s])
    ends_scaled = jnp.where(lows, sides[0], sides[1])

    def iterate(X):
        for c in range(3):
            u = ext[3 + c, X] + alpha * ext[c, X]
            if 4 <= X < 12:
                new_sol[c, X - 4] = u[0:16]
            near = roll(halos[c], 124 - 8 * X, 1)
            up = roll(jnp.where(lane == 0, near, u), -1, 1)
            us[0, c, X] = u
            us[1, c, X] = up
            us[2, c, X] = roll(u, -1, 0)
            us[3, c, X] = roll(up, -1, 0)
        if X == 11:
            copies[2].start()

    acc = [[[None] * 3 for _ in range(4)] for _ in range(16)]

    def pair_up(X):
        for r in range(3):
            at = slice(8 * r, 8 * r + 8)
            for o, field0, frame0, field1, frame1 in pairs:
                to = X + o[0]
                if not 0 <= to < 16 or not (1 <= X < 15 or 1 <= to < 15):
                    continue
                g = quadratic([us[field0, c, X, at] - us[field1, c, to, at] for c in range(3)], o)
                if 1 <= X < 15:
                    acc[X][frame0][r] = plus(acc[X][frame0][r], g)
                if 1 <= to < 15:
                    acc[to][frame1][r] = plus(acc[to][frame1][r], g)

    def filter_lines(X):
        frames = [jnp.concatenate(tiles, axis=0) for tiles in acc[X]]
        up = frames[1] + roll(frames[3], 1, 0)
        below = roll(side_low, 127 - (8 * X + 3), 1)
        up = roll(jnp.where(lane == 127, below, up), 1, 1)
        den = ext[6, X]
        energy = frames[0] + roll(frames[2], 1, 0) + up
        s = energy_scale * (den * den) * energy * hinv[X]
        near = roll(ends_scaled, 124 - 8 * X, 1)
        fold = [s]
        for k in range(1, RAD + 1):
            above = roll(jnp.where(lane < k, near, s), -k, 1)
            under = roll(jnp.where(lane >= 128 - k, near, s), k, 1)
            fold.append(above + under)
        for k in range(RAD + 1):
            lines[X, k] = fold[k]

    def filter_rows(x):
        groups = {}
        for a in range(RAD + 1):
            for k in range(RAD + 1):
                if cone(a, 0, k) > 0:
                    both = lines[x + HALO + a, k]
                    if a > 0:
                        both = both + lines[x + HALO - a, k]
                    groups[a * a + k * k] = plus(groups.get(a * a + k * k), both)
        value = None
        for b in range(RAD + 1):
            row = None
            for d, group in groups.items():
                w = RAD + 0.5 - math.sqrt(d + b * b)
                if w > 0:
                    row = plus(row, w * group)
            value = row if b == 0 else value + roll(row, b, 0) + roll(row, -b, 0)
        sens[x] = value[0:16]

    for X in range(16 + 1):
        if X < 16:
            iterate(X)
        if X >= 1:
            pair_up(X - 1)
        if X >= 3:
            filter_lines(X - 2)
        if X - 2 - 2 * RAD - 1 >= 0:
            filter_rows(X - 2 - 2 * RAD - 1)
    copies[3].start()
    for copy in copies:
        copy.wait()


def partner(place, turn, count):
    other = (place ^ 1) if turn == 0 else ((place + 1) ^ 1) - 1
    return other if 0 <= other < count else None


def swap_pairs(counts, turns):
    pairs = []
    for flat in range(math.prod(counts)):
        rest, place = flat, []
        for count in reversed(counts):
            place.insert(0, rest % count)
            rest //= count
        to = [p if t is None else partner(p, t, c) for p, t, c in zip(place, turns, counts)]
        if None in to:
            continue
        index = 0
        for p, count in zip(to, counts):
            index = index * count + p
        pairs.append((flat, index))
    return pairs


def per_device(mesh_shape, solution, residual, direction, density, labels):
    nx, ny, nz = (mesh_shape[a] for a in AXES)
    half, full, corner = (7, 4, 16, 128), (7, 4, 8, 128), (7, 2, 8, 128)
    rounds_y = 1 if ny == 2 else 2
    field, flat = (3, 8, 16, 128), (8, 16, 128)
    packed = call(
        functools.partial(pack_faces, rounds_y),
        [half, half] + [full, corner, corner] * rounds_y,
        solution, direction, density, labels,
        far=range(4),
        scratch=[
            pltpu.VMEM(field, f32), pltpu.VMEM(field, f32), pltpu.VMEM(flat, f32),
            pltpu.VMEM(flat, jnp.int32), pltpu.SemaphoreType.DMA((4,)),
        ],
    )
    halves = packed[:2]
    plane = ("gx", "gy")
    got = [lax.ppermute(halves[r], plane, swap_pairs((nx, ny), (r, None))) for r in (1, 0)]
    strips = []
    for s in range(rounds_y):
        rows, corner0, corner1 = packed[2 + 3 * s : 5 + 3 * s]
        for array, turn in ((rows, None), (corner1, 1), (corner0, 0)):
            strips.append(lax.ppermute(array, plane, swap_pairs((nx, ny), (turn, s))))
    hinv, hside = call(functools.partial(inverse_sums, (nx, ny, nz)), [(16, 24, 128), (2, 24, 128)])
    zend = (ZTILES, 8, 128)
    ext, ends, *sends = call(
        functools.partial(extend, (nx, ny, nz)),
        [(7, 16, 24, 128), (7, 24, 128), zend, zend],
        *halves, *got, *strips,
    )
    later = lax.ppermute(sends[0], "gz", swap_pairs((nz,), (1,)))
    first = lax.ppermute(sends[1], "gz", swap_pairs((nz,), (0,)))
    ends_got = [later, first]
    image, inverse, sums, around = call(
        functools.partial(apply_operator, nz),
        [field, field, (nx * ny * nz, 1, 128), (7, 24, 128)],
        ext, *ends_got, residual, labels,
        scratch=[pltpu.VMEM((4, 3, 3, 10, 16, 128), f32)],
    )
    total = lax.all_to_all(sums, AXES, 0, 0)
    return tuple(
        call(
            finish_step,
            [field, field, field, flat],
            ext, ends, around, total, image, inverse, residual, direction, hinv, hside,
            scratch=[
                pltpu.VMEM((4, 3, 16, 24, 128), f32), pltpu.VMEM((16, RAD + 1, 24, 128), f32),
                pltpu.VMEM(field, f32), pltpu.VMEM(field, f32), pltpu.VMEM(field, f32),
                pltpu.VMEM(flat, f32), pltpu.SemaphoreType.DMA((4,)),
            ],
            far_out=True,
        )
    )


def solution(mesh):
    wide, flat = P(None, "gx", "gy", "gz"), P("gx", "gy", "gz")
    return jax.shard_map(
        functools.partial(per_device, dict(mesh.shape)),
        mesh=mesh,
        in_specs=(wide, wide, wide, flat, flat),
        out_specs=(wide, wide, wide, flat),
        check_vma=False,
    )
```

```python
import functools
import math

import jax
import jax.numpy as jnp
from jax import lax
from jax.experimental import pallas as pl
from jax.experimental.pallas import tpu as pltpu
from jax.sharding import PartitionSpec as P

RAD = 3
HALO = RAD + 1
ZTILES = 11
stiff_floor = 0.001
penalty = 3.0
f32 = jnp.float32
neighbour_offsets = [
    (off_x, off_y, off_z)
    for off_x in (-1, 0, 1)
    for off_y in (-1, 0, 1)
    for off_z in (-1, 0, 1)
    if (off_x, off_y, off_z) != (0, 0, 0)
]
AXES = ("gx", "gy", "gz")


def cone(a, b, k):
    return max(0.0, RAD + 0.5 - math.sqrt(a * a + b * b + k * k))


def lanes_of(shape):
    return lax.broadcasted_iota(jnp.int32, shape, len(shape) - 1)


def rows_of(shape):
    return lax.broadcasted_iota(jnp.int32, shape, len(shape) - 2)


def roll(value, amount, axis):
    size = value.shape[axis]
    amount = amount % size
    return value if amount == 0 else pltpu.roll(value, amount, axis)


def call(body, outs, *args, scratch=(), cost=20000, far=(), far_out=False, near_out=()):
    args = [
        pltpu.with_memory_space_constraint(a, pltpu.HBM) if i in far else a for i, a in enumerate(args)
    ]
    return pl.pallas_call(
        body,
        out_shape=[
            pltpu.VMEM(shape, f32) if i in near_out else jax.ShapeDtypeStruct(shape, f32)
            for i, shape in enumerate(outs)
        ],
        in_specs=[
            pl.BlockSpec(memory_space=pl.ANY if i in far else pltpu.VMEM) for i in range(len(args))
        ],
        out_specs=[pl.BlockSpec(memory_space=pl.ANY if far_out else pltpu.VMEM)] * len(outs),
        scratch_shapes=list(scratch),
        compiler_params=pltpu.CompilerParams(vmem_limit_bytes=24 * 1024 * 1024),
        cost_estimate=pl.CostEstimate(flops=cost * 1000, bytes_accessed=cost, transcendentals=0),
    )(*args)


def is_even(axis):
    return lax.axis_index(axis) % 2 == 0


def pack_faces(rounds_y, sol_any, dire_any, den_any, lab_any, *refs):
    halves, packs = refs[:2], refs[2 : 2 + 3 * rounds_y]
    sol, dire, den, lab, sems = refs[2 + 3 * rounds_y :]
    copies = [
        pltpu.make_async_copy(source, target, sems.at[i])
        for i, (source, target) in enumerate(
            ((dire_any, dire), (sol_any, sol), (den_any, den), (lab_any, lab))
        )
    ]
    for copy in copies:
        copy.start()
    sub = rows_of((8, 128))
    even_x, even_y = is_even("gx"), is_even("gy")
    for copy in copies:
        copy.wait()

    def masked(x):
        label = lab[x]
        keep = jnp.where(label == 1, 0.0, 1.0).astype(f32)
        keep_last = jnp.where(label >= 1, 0.0, 1.0).astype(f32)
        fields = [dire[0, x] * keep, dire[1, x] * keep, dire[2, x] * keep_last]
        return fields + [sol[0, x], sol[1, x], sol[2, x], den[x]]

    for t in range(2):
        planes = {x: masked(x) for x in (2 * t, 2 * t + 1, 2 * t + 4, 2 * t + 5)}
        for f in range(7):
            for i in (2 * t, 2 * t + 1):
                low, high = planes[i][f], planes[i + 4][f]
                halves[0][f, i] = jnp.where(even_x, high, low)
                halves[1][f, i] = jnp.where(even_x, low, high)
            tiles = []
            for i in (2 * t, 2 * t + 4):
                p, q = planes[i][f], planes[i + 1][f]
                low = jnp.where(sub < 4, p[0:8], roll(q[0:8], 4, 0))
                high = jnp.where(sub < 4, roll(p[8:16], 4, 0), q[8:16])
                tiles.append((jnp.where(even_y, high, low), jnp.where(even_y, low, high)))
            for s in range(rounds_y):
                rows, corner0, corner1 = packs[3 * s : 3 * s + 3]
                low, high = tiles[0][s], tiles[1][s]
                rows[f, t] = low
                rows[f, t + 2] = high
                corner0[f, t] = jnp.where(even_x, high, low)
                corner1[f, t] = jnp.where(even_x, low, high)


def extend(counts, half0, half1, got0, got1, *refs):
    nx, ny, nz = counts
    sides, (ext, ends, send1, send0) = refs[:-4], refs[-4:]
    sub = rows_of((8, 128))
    lane = lanes_of((24, 128))
    lows = lanes_of((8, 128)) % 8 < 4
    ix, iy = lax.axis_index("gx"), lax.axis_index("gy")
    even_y, even_z = is_even("gy"), is_even("gz")
    x_ok = ((ix > 0).astype(f32), (ix < nx - 1).astype(f32))
    y_ok = ((iy > 0).astype(f32), (iy < ny - 1).astype(f32))

    def body(blocks, order):
        def strip(which, f, t):
            tiles = []
            for s in range(len(sides) // 3):
                rows, corner0, corner1 = sides[3 * s : 3 * s + 3]
                ref = rows if which is None else (corner0, corner1)[order[which]]
                tiles.append(ref[f, t])
            keep = 1.0 if which is None else x_ok[which]
            other = tiles[-1]
            low = jnp.where(even_y, other, tiles[0]) * (y_ok[0] * keep)
            high = jnp.where(even_y, tiles[0], other) * (y_ok[1] * keep)
            return low, high

        for f in range(7):
            packed = None
            for X in range(16):
                own = blocks[X // 4][f, X % 4]
                which = None
                if X < 4:
                    which, t = 0, X // 2
                elif X >= 12:
                    which, t = 1, (X - 12) // 2
                else:
                    t = (X - 4) // 2
                if which is not None:
                    own = own * x_ok[which]
                low, high = strip(which, f, t)
                if X % 2 == 0:
                    low = roll(low, 4, 0)
                else:
                    high = roll(high, 4, 0)
                plane = jnp.concatenate([own, jnp.where(sub < 4, high, low)], axis=0)
                ext[f, X] = plane
                turned = roll(plane, 8 * X + 4, 1)
                packed = turned if X == 0 else jnp.where(lane >= 8 * X, turned, packed)
            ends[f] = packed
        for j in range(ZTILES):
            tiles = []
            for t in (j, j + ZTILES):
                tiles.append(ends[t // 3, 8 * (t % 3) : 8 * (t % 3) + 8] if t < 21 else None)
            up, down = tiles[0], tiles[0]
            if tiles[1] is not None:
                up = jnp.where(lows, tiles[0], roll(tiles[1], 4, 1))
                down = jnp.where(lows, roll(tiles[1], -4, 1), tiles[0])
            send0[j] = jnp.where(even_z, up, down)
            send1[j] = jnp.where(even_z, down, up)

    @pl.when(ix % 2 == 0)
    def _():
        body((got1, half1, half0, got0), (1, 0))

    @pl.when(ix % 2 == 1)
    def _():
        body((got0, half0, half1, got1), (0, 1))


def inverse_sums(counts, main, side):
    shape = (24, 128)
    row, lane = rows_of(shape), lanes_of(shape)
    nx, ny, nz = counts
    base_x = lax.axis_index("gx") * 8 - HALO
    base_y = lax.axis_index("gy") * 16
    base_z = lax.axis_index("gz") * 128

    def folded(place, limit):
        def inside(p):
            return jnp.where((p >= 0) & (p < limit), 1.0, 0.0).astype(f32)

        return [inside(place)] + [inside(place - k) + inside(place + k) for k in range(1, RAD + 1)]

    along_y = folded(jnp.where(row < 16 + HALO, row, row - 24) + base_y, ny * 16)

    def partial(along_z):
        table = []
        for a in range(RAD + 1):
            total = jnp.zeros(shape, f32)
            for b in range(RAD + 1):
                line = None
                for k in range(RAD + 1):
                    w = cone(a, b, k)
                    if w > 0:
                        line = w * along_z[k] if line is None else line + w * along_z[k]
                if line is not None:
                    total = total + along_y[b] * line
            table.append(total)
        return table

    def finish(total, along_x, along_z):
        inner = along_x[0] * along_y[0] * along_z[0] > 0
        return jnp.where(inner, 1.0 / jnp.where(inner, total, 1.0), 0.0)

    along_z = folded(lane + base_z, nz * 128)
    table = partial(along_z)
    for X in range(16):
        along_x = folded(jnp.full(shape, X, jnp.int32) + base_x, nx * 8)
        total = sum(along_x[a] * table[a] for a in range(RAD + 1))
        main[X] = finish(total, along_x, along_z)
    place = lane % 8
    along_x = folded(lane // 8 + base_x, nx * 8)
    for s, shift in enumerate((-4, 124)):
        along_z = folded(place + (base_z + shift), nz * 128)
        table = partial(along_z)
        total = sum(along_x[a] * table[a] for a in range(RAD + 1))
        side[s] = finish(total, along_x, along_z)


def apply_operator(nz, ext, got1, got0, res, lab, image, inverse, sums, around, shifts):
    lane = lanes_of((24, 128))
    fields = (0, 1, 2, 6)
    iz = lax.axis_index("gz")
    even = is_even("gz")
    lows = lanes_of((8, 128)) % 8 < 4
    keep = jnp.where(lows, (iz > 0).astype(f32), (iz < nz - 1).astype(f32))
    for j in range(ZTILES):
        zero, one = got0[j], got1[j]
        below, above = jnp.where(even, one, zero), jnp.where(even, zero, one)
        for t in (j, j + ZTILES):
            if t < 21:
                if t != j:
                    below, above = roll(below, -4, 1), roll(above, 4, 1)
                around[t // 3, 8 * (t % 3) : 8 * (t % 3) + 8] = jnp.where(lows, below, above) * keep
    parts = [jnp.zeros((16, 128), f32) for _ in range(4)]
    for plane_at in range(10):
        X = plane_at + 3
        for g, f in enumerate(fields):
            value = ext[f, X]
            near = roll(around[f], 124 - 8 * X, 1)
            if g == 3:
                stiff = stiff_floor + (1.0 - stiff_floor) * value * value * value
                value = jnp.where(value > 0, stiff, 0.0)
                stiff = stiff_floor + (1.0 - stiff_floor) * near * near * near
                near = jnp.where(near > 0, stiff, 0.0)
            up = roll(jnp.where(lane == 0, near, value), -1, 1)
            down = roll(jnp.where(lane == 127, near, value), 1, 1)
            for z, plane in enumerate((down, value, up)):
                for y in range(3):
                    shifts[g, y, z, plane_at] = roll(plane, 1 - y, 0)[0:16]
        x = plane_at - 2
        if x < 0:
            continue
        n = x + 1
        mid = [shifts[g, 1, 1, n] for g in range(4)]
        classes = {1: [None] * 3, 2: [None] * 3, 3: [None] * 3}
        faces = [None] * 3
        edges = [None] * 3
        corners = None

        def add(old, new):
            return new if old is None else old + new

        for o in neighbour_offsets:
            near = [shifts[g, 1 + o[1], 1 + o[2], n + o[0]] for g in range(4)]
            norm = sum(abs(c) for c in o)
            weight = mid[3] + near[3]
            d = [mid[c] - near[c] for c in range(3)]
            acc = classes[norm]
            if norm == 1:
                c0 = [c for c in range(3) if o[c] != 0][0]
                faces[c0] = add(faces[c0], near[3])
                for c in range(3):
                    acc[c] = add(acc[c], weight * (d[c] + d[c] if c == c0 else d[c]))
            else:
                along = None
                for c in range(3):
                    if o[c] != 0:
                        term = d[c]
                        if along is None:
                            along, sign = term, o[c]
                        else:
                            along = along + term if o[c] == sign else along - term
                along = along * (1.0 / norm)
                for c in range(3):
                    if o[c] == 0:
                        pulled = d[c]
                    elif o[c] == sign:
                        pulled = d[c] + along
                    else:
                        pulled = d[c] - along
                    acc[c] = add(acc[c], weight * pulled)
                if norm == 2:
                    c0 = [c for c in range(3) if o[c] == 0][0]
                    edges[c0] = add(edges[c0], near[3])
                else:
                    corners = add(corners, near[3])
        s0 = mid[3]
        all_faces = faces[0] + faces[1] + faces[2]
        all_edges = edges[0] + edges[1] + edges[2]
        common = (all_faces + 6.0 * s0) + 0.75 * (all_edges + 12.0 * s0) + (4.0 / 9.0) * (corners + 8.0 * s0)
        label = lab[x]
        for c in range(3):
            diag = 0.5 * (common + (faces[c] + 2.0 * s0) - 0.25 * (edges[c] + 4.0 * s0))
            fixed = (label == 1) if c < 2 else (label >= 1)
            total = 0.5 * classes[1][c] + 0.25 * classes[2][c] + (1.0 / 6.0) * classes[3][c]
            total = jnp.where(fixed, 0.0, total)
            inv = 1.0 / jnp.where(fixed, 1.0, diag)
            r = res[c, x]
            zeta = r * inv
            scaled = total * inv
            image[c, x] = total
            inverse[c, x] = inv
            parts[0] = parts[0] + r * zeta
            parts[1] = parts[1] + mid[c] * total
            parts[2] = parts[2] + r * scaled
            parts[3] = parts[3] + total * scaled
    place = lanes_of((1, 128)) // 32
    row = None
    for k in range(4):
        part = parts[k][0:8] + parts[k][8:16]
        part = part + roll(part, 64, 1)
        part = jnp.sum(part + roll(part, 32, 1), axis=0, keepdims=True)
        row = part if k == 0 else jnp.where(place == k, part, row)
    sums[...] = jnp.broadcast_to(row[None], sums.shape)


def quadratic(d, o):
    norm = sum(abs(c) for c in o)
    square = d[0] * d[0] + d[1] * d[1] + d[2] * d[2]
    along, sign = None, 1
    for c in range(3):
        if o[c] != 0:
            if along is None:
                along, sign = d[c], o[c]
            else:
                along = along + d[c] if o[c] == sign else along - d[c]
    if norm == 1:
        return square + along * along
    return (1.0 / norm) * square + (1.0 / (norm * norm)) * (along * along)


pairs = [((1, 0, 0), 0, 0, 0, 0)]
pairs += [((a, 1, 0), 0, 0, 2, 2) for a in (-1, 0, 1)]
pairs += [((a, 0, 1), 0, 0, 1, 1) for a in (-1, 0, 1)]
pairs += [((a, 1, 1), 0, 0, 3, 3) for a in (-1, 0, 1)]
pairs += [((a, -1, 1), 2, 2, 1, 1) for a in (-1, 0, 1)]
energy_scale = -penalty * (1.0 - stiff_floor) * 0.5


def plus(old, new):
    return new if old is None else old + new


def finish_step(
    ext, ends, around, total, image, inverse, res, dire, hinv, hside,
    new_sol_any, new_res_any, new_dir_any, sens_any, us, lines, new_sol, new_res, new_dir, sens, sems,
):
    lane = lanes_of((24, 128))
    lows = lane % 8 < 4
    copies = [
        pltpu.make_async_copy(source, target, sems.at[i])
        for i, (source, target) in enumerate(
            ((new_res, new_res_any), (new_dir, new_dir_any), (new_sol, new_sol_any), (sens, sens_any))
        )
    ]
    spread = jnp.broadcast_to(jnp.sum(total[...], axis=0), (8, 128))
    tot = jnp.sum(jnp.where(lanes_of((8, 128)) // 32 == rows_of((8, 128)), spread, 0.0), axis=1, keepdims=True)
    rz, pq, s2, s3 = (tot[k : k + 1] for k in range(4))
    alpha = rz / pq
    beta = (rz + alpha * (alpha * s3 - 2.0 * s2)) / rz

    for x in range(8):
        for c in range(3):
            r = res[c, x] - alpha * image[c, x]
            new_res[c, x] = r
            new_dir[c, x] = r * inverse[c, x] + beta * dire[c, x]
    copies[0].start()
    copies[1].start()

    halos, lefts, rights = [], [], []
    for c in range(3):
        halo_u = around[3 + c] + alpha * around[c]
        own_u = ends[3 + c] + alpha * ends[c]
        halos.append(halo_u)
        lefts.append(jnp.where(lows, halo_u, own_u))
        rights.append(jnp.where(lows, own_u, halo_u))
    sides, side_low = [], None
    den_left = jnp.where(lows, around[6], ends[6])
    den_right = jnp.where(lows, ends[6], around[6])
    for s, (u, den) in enumerate(((lefts, den_left), (rights, den_right))):
        up = [roll(v, -1, 1) for v in u]
        moved = [u, up, [roll(v, -1, 0) for v in u], [roll(v, -1, 0) for v in up]]
        far = {}
        acc = {}
        for o, field0, frame0, field1, frame1 in pairs:
            key = (field1, o[0])
            if key not in far:
                far[key] = [roll(v, -8 * o[0], 1) for v in moved[field1]]
            g = quadratic([moved[field0][c] - far[key][c] for c in range(3)], o)
            acc[frame0, 0] = plus(acc.get((frame0, 0)), g)
            acc[frame1, o[0]] = plus(acc.get((frame1, o[0])), g)
        frames = []
        for frame in range(4):
            value = None
            for a in (-1, 0, 1):
                if (frame, a) in acc:
                    value = plus(value, roll(acc[frame, a], 8 * a, 1))
            frames.append(value)
        up = frames[1] + roll(frames[3], 1, 0)
        if s == 0:
            side_low = up
        energy = frames[0] + roll(frames[2], 1, 0) + roll(up, 1, 1)
        sides.append(energy_scale * (den * den) * energy * hside[s])
    ends_scaled = jnp.where(lows, sides[0], sides[1])

    def iterate(X):
        for c in range(3):
            u = ext[3 + c, X] + alpha * ext[c, X]
            if 4 <= X < 12:
                new_sol[c, X - 4] = u[0:16]
            near = roll(halos[c], 124 - 8 * X, 1)
            up = roll(jnp.where(lane == 0, near, u), -1, 1)
            us[0, c, X] = u
            us[1, c, X] = up
            us[2, c, X] = roll(u, -1, 0)
            us[3, c, X] = roll(up, -1, 0)
        if X == 11:
            copies[2].start()

    acc = [[[None] * 3 for _ in range(4)] for _ in range(16)]

    def pair_up(X):
        for r in range(3):
            at = slice(8 * r, 8 * r + 8)
            for o, field0, frame0, field1, frame1 in pairs:
                to = X + o[0]
                if not 0 <= to < 16 or not (1 <= X < 15 or 1 <= to < 15):
                    continue
                g = quadratic([us[field0, c, X, at] - us[field1, c, to, at] for c in range(3)], o)
                if 1 <= X < 15:
                    acc[X][frame0][r] = plus(acc[X][frame0][r], g)
                if 1 <= to < 15:
                    acc[to][frame1][r] = plus(acc[to][frame1][r], g)

    def filter_lines(X):
        frames = [jnp.concatenate(tiles, axis=0) for tiles in acc[X]]
        up = frames[1] + roll(frames[3], 1, 0)
        below = roll(side_low, 127 - (8 * X + 3), 1)
        up = roll(jnp.where(lane == 127, below, up), 1, 1)
        den = ext[6, X]
        energy = frames[0] + roll(frames[2], 1, 0) + up
        s = energy_scale * (den * den) * energy * hinv[X]
        near = roll(ends_scaled, 124 - 8 * X, 1)
        fold = [s]
        for k in range(1, RAD + 1):
            above = roll(jnp.where(lane < k, near, s), -k, 1)
            under = roll(jnp.where(lane >= 128 - k, near, s), k, 1)
            fold.append(above + under)
        for k in range(RAD + 1):
            lines[X, k] = fold[k]

    def filter_rows(x):
        groups = {}
        for a in range(RAD + 1):
            for k in range(RAD + 1):
                if cone(a, 0, k) > 0:
                    both = lines[x + HALO + a, k]
                    if a > 0:
                        both = both + lines[x + HALO - a, k]
                    groups[a * a + k * k] = plus(groups.get(a * a + k * k), both)
        value = None
        for b in range(RAD + 1):
            row = None
            for d, group in groups.items():
                w = RAD + 0.5 - math.sqrt(d + b * b)
                if w > 0:
                    row = plus(row, w * group)
            value = row if b == 0 else value + roll(row, b, 0) + roll(row, -b, 0)
        sens[x] = value[0:16]

    for X in range(16 + 1):
        if X < 16:
            iterate(X)
        if X >= 1:
            pair_up(X - 1)
        if X >= 3:
            filter_lines(X - 2)
        if X - 2 - 2 * RAD - 1 >= 0:
            filter_rows(X - 2 - 2 * RAD - 1)
    copies[3].start()
    for copy in copies:
        copy.wait()


def partner(place, turn, count):
    other = (place ^ 1) if turn == 0 else ((place + 1) ^ 1) - 1
    return other if 0 <= other < count else None


def swap_pairs(counts, turns):
    pairs = []
    for flat in range(math.prod(counts)):
        rest, place = flat, []
        for count in reversed(counts):
            place.insert(0, rest % count)
            rest //= count
        to = [p if t is None else partner(p, t, c) for p, t, c in zip(place, turns, counts)]
        if None in to:
            continue
        index = 0
        for p, count in zip(to, counts):
            index = index * count + p
        pairs.append((flat, index))
    return pairs


def per_device(mesh_shape, solution, residual, direction, density, labels):
    nx, ny, nz = (mesh_shape[a] for a in AXES)
    half, full, corner = (7, 4, 16, 128), (7, 4, 8, 128), (7, 2, 8, 128)
    rounds_y = 1 if ny == 2 else 2
    field, flat = (3, 8, 16, 128), (8, 16, 128)
    packed = call(
        functools.partial(pack_faces, rounds_y),
        [half, half] + [full, corner, corner] * rounds_y,
        solution, direction, density, labels,
        far=range(4),
        scratch=[
            pltpu.VMEM(field, f32), pltpu.VMEM(field, f32), pltpu.VMEM(flat, f32),
            pltpu.VMEM(flat, jnp.int32), pltpu.SemaphoreType.DMA((4,)),
        ],
    )
    halves = packed[:2]
    plane = ("gx", "gy")
    got = [lax.ppermute(halves[r], plane, swap_pairs((nx, ny), (r, None))) for r in (0, 1)]
    strips = []
    for s in range(rounds_y):
        for array, turn in zip(packed[2 + 3 * s : 5 + 3 * s], (None, 0, 1)):
            strips.append(lax.ppermute(array, plane, swap_pairs((nx, ny), (turn, s))))
    hinv, hside = call(functools.partial(inverse_sums, (nx, ny, nz)), [(16, 24, 128), (2, 24, 128)])
    zend = (ZTILES, 8, 128)
    ext, ends, *sends = call(
        functools.partial(extend, (nx, ny, nz)),
        [(7, 16, 24, 128), (7, 24, 128), zend, zend],
        *halves, *got, *strips,
    )
    later = lax.ppermute(sends[0], "gz", swap_pairs((nz,), (1,)))
    first = lax.ppermute(sends[1], "gz", swap_pairs((nz,), (0,)))
    ends_got = [later, first]
    image, inverse, sums, around = call(
        functools.partial(apply_operator, nz),
        [field, field, (nx * ny * nz, 1, 128), (7, 24, 128)],
        ext, *ends_got, residual, labels,
        scratch=[pltpu.VMEM((4, 3, 3, 10, 16, 128), f32)],
        near_out=(2,),
    )
    total = lax.all_to_all(sums, AXES, 0, 0)
    return tuple(
        call(
            finish_step,
            [field, field, field, flat],
            ext, ends, around, total, image, inverse, residual, direction, hinv, hside,
            scratch=[
                pltpu.VMEM((4, 3, 16, 24, 128), f32), pltpu.VMEM((16, RAD + 1, 24, 128), f32),
                pltpu.VMEM(field, f32), pltpu.VMEM(field, f32), pltpu.VMEM(field, f32),
                pltpu.VMEM(flat, f32), pltpu.SemaphoreType.DMA((4,)),
            ],
            far_out=True,
        )
    )


def solution(mesh):
    wide, flat = P(None, "gx", "gy", "gz"), P("gx", "gy", "gz")
    return jax.shard_map(
        functools.partial(per_device, dict(mesh.shape)),
        mesh=mesh,
        in_specs=(wide, wide, wide, flat, flat),
        out_specs=(wide, wide, wide, flat),
        check_vma=False,
    )
```
